32 devices in a mesh: dp: 8 (over y, x, core), mp: 4 (over z).
Axes of the slice: x: 2, y: 2, z: 4, core: 2. Of those that a mesh axis runs over, the one named last changes fastest.
Arguments:
- node_state: bfloat16 [5568, 128], P('dp', 'mp'), may hold values from -6 to 6
- edge_feat: bfloat16 [16, 155904], P(None, 'dp'), may hold values from -6 to 6
- sender: int32 [155904], P('dp'), may hold values from 0 to 28, as said below
- receiver: int32 [155904], P('dp'), may hold values from 0 to 28, as said below
- edge_mask: int32 [155904], P('dp'), may hold values from 0 to 1, as said below
- node_mask: int32 [5568], P('dp'), may hold values from 0 to 1, as said below
- out_grad: float32 [5568, 128], P('dp', 'mp'), may hold values from -6 to 6
- edge_in: float32 [16, 128], P(None, 'dp'), may hold values from -1.5 to 1.5
- edge_out: float32 [128, 16384], P('dp', 'mp'), may hold values from -0.0078125 to 0.0078125
- gru_weight: float32 [2, 3, 128, 128], P(None, None, 'dp', 'mp'), may hold values from -0.5 to 0.5
- edge_in_m1: float32 [16, 128], P(None, 'dp'), may hold values from -96 to 96
- edge_in_m2: float32 [16, 128], P(None, 'dp'), may hold values from 222.72 to 890.88
- edge_out_m1: float32 [128, 16384], P('dp', 'mp'), may hold values from -448 to 448
- edge_out_m2: float32 [128, 16384], P('dp', 'mp'), may hold values from 5612.544 to 22450.176
- gru_m1: float32 [2, 3, 128, 128], P(None, None, 'dp', 'mp'), may hold values from -56 to 56
- gru_m2: float32 [2, 3, 128, 128], P(None, None, 'dp', 'mp'), may hold values from 94.656 to 378.624
Outputs:
- out_state: float32 [5568, 128], P('dp', 'mp')
- grad_state: float32 [5568, 128], P('dp', 'mp')
- grad_edges: float32 [16, 155904], P(None, 'dp')
- edge_in_m1_new: float32 [16, 128], P(None, 'dp')
- edge_in_m2_new: float32 [16, 128], P(None, 'dp')
- edge_in_new: float32 [16, 128], P(None, 'dp')
- edge_in_low: bfloat16 [16, 128], P(None, 'dp')
- edge_out_m1_new: float32 [128, 16384], P('dp', 'mp')
- edge_out_m2_new: float32 [128, 16384], P('dp', 'mp')
- edge_out_new: float32 [128, 16384], P('dp', 'mp')
- edge_out_low: bfloat16 [128, 16384], P('dp', 'mp')
- gru_m1_new: float32 [2, 3, 128, 128], P(None, None, 'dp', 'mp')
- gru_m2_new: float32 [2, 3, 128, 128], P(None, None, 'dp', 'mp')
- gru_new: float32 [2, 3, 128, 128], P(None, None, 'dp', 'mp')
- gru_low: bfloat16 [2, 3, 128, 128], P(None, None, 'dp', 'mp')
The draws below stay inside these ranges and needn't reach their ends.
Inputs may be any that keep to these rules, and one draw needn't show every extreme that they name: In every molecule the 812 edges are all ordered pairs of distinct atoms, each once, in an order drawn from the seed; sender and receiver differ. `receiver`: in every molecule the 812 edges are all ordered pairs of distinct atoms, each once. `edge_mask`: 0 wherever the sender or the receiver is a padded atom. `node_mask`: in each molecule a run of ones followed by zeros, with at least 10 ones.
All inputs are finite; a program needn't handle non-finite values.
Results may differ from the reference program's by a relative error of at most 0.018.
Values may be sent and summed in bfloat16 or wider, within the bound.
A program may use at most 128 MiB of HBM per device.

```python
import math
import jax
import jax.numpy as jnp
from jax import lax

HID = 128
EFEAT = 16
MOL_ATOMS = 29
MOL_EDGES = 812
STEP = 5
MOLECULES = 192
ATOMS = 5568
EDGES = 155904


def molecule_layout(key):
    count_key, order_key, edge_key = jax.random.split(key, 3)
    counts = jax.random.randint(count_key, (MOLECULES,), MOL_ATOMS // 3 + 1, MOL_ATOMS + 1)

    def shuffled(subkey):
        return jax.random.permutation(subkey, MOL_EDGES)
    edge_order = jax.vmap(shuffled)(jax.random.split(order_key, MOLECULES)).astype(jnp.int32)
    first_atom = edge_order // (MOL_ATOMS - 1)
    remainder = edge_order % (MOL_ATOMS - 1)
    second_atom = remainder + (remainder >= first_atom).astype(jnp.int32)
    kept_edge = jax.random.randint(edge_key, (MOLECULES, MOL_EDGES), 0, 5) > 0
    live = (first_atom < counts[:, None]) & (second_atom < counts[:, None]) & kept_edge
    return (first_atom, second_atom, live, counts)


def draw_sender(key, part):
    first_atom, second_atom, live, counts = molecule_layout(key)
    return second_atom.reshape(-1).astype(jnp.int32)


def draw_receiver(key, part):
    first_atom, second_atom, live, counts = molecule_layout(key)
    return first_atom.reshape(-1).astype(jnp.int32)


def draw_edge_mask(key, part):
    first_atom, second_atom, live, counts = molecule_layout(key)
    return live.reshape(-1).astype(jnp.int32)


def draw_node_mask(key, part):
    first_atom, second_atom, live, counts = molecule_layout(key)
    atom_iota = jnp.arange(MOL_ATOMS, dtype=jnp.int32)
    return (atom_iota[None, :] < counts[:, None]).reshape(-1).astype(jnp.int32)


def block_scale(rng, extent, cuts, least, high):
    def one(position, shards_of):
        draws = jax.random.uniform(jax.random.fold_in(jax.random.fold_in(rng, 6), position), (shards_of,), jnp.float32, least / len(cuts), high / len(cuts))
        return jnp.repeat(jnp.exp(draws), extent[position] // shards_of).reshape((-1,) + (1,) * (len(extent) - position - 1))

    loudness = one(*cuts[0])
    for cut in cuts[1:]:
        loudness = loudness * one(*cut)
    return loudness


def gaussian(stream_key, dims, width, most, shards=(), held_as=jnp.bfloat16):
    drawn = jax.random.normal(stream_key, dims, jnp.float32) * width
    if len(shards) > 0:
        drawn = block_scale(stream_key, dims, shards, -0.22, 0.18) * drawn
    return jnp.clip(drawn, min=-most, max=most).astype(held_as)


def setup_inputs(seed: int = 0) -> dict:
    arg_keys = jax.random.split(jax.random.key(seed), 17)
    return {
        "node_state": gaussian(arg_keys[0], (ATOMS, HID), 1.0, 6.0, ((0, 8), (1, 4))),
        "edge_feat": gaussian(arg_keys[1], (EFEAT, EDGES), 1.0, 6.0, ((1, 8),)),
        "sender": draw_sender(jax.random.fold_in(arg_keys[16], 71), 0),
        "receiver": draw_receiver(jax.random.fold_in(arg_keys[16], 71), 0),
        "edge_mask": draw_edge_mask(jax.random.fold_in(arg_keys[16], 71), 0),
        "node_mask": draw_node_mask(jax.random.fold_in(arg_keys[16], 71), 0),
        "out_grad": gaussian(arg_keys[6], (ATOMS, HID), 1.0, 6.0, ((0, 8), (1, 4)), jnp.float32),
        "edge_in": gaussian(arg_keys[7], (EFEAT, HID), EFEAT ** -0.5, 1.5, ((1, 8),), jnp.float32),
        "edge_out": gaussian(arg_keys[8], (HID, HID * HID), (HID * HID * (MOL_ATOMS - 1)) ** -0.5, 0.0078125, ((0, 8), (1, 4)), jnp.float32),
        "gru_weight": gaussian(arg_keys[9], (2, 3, HID, HID), HID ** -0.5, 0.5, ((2, 8), (3, 4)), jnp.float32),
        "edge_in_m1": gaussian(arg_keys[10], (EFEAT, HID), (0.2 * (EDGES / (MOL_ATOMS - 1)) ** 0.5), 96.0, ((1, 8),), jnp.float32),
        "edge_in_m2": jnp.clip(jnp.exp(math.log(890.88) - 1.3862944 * jax.random.uniform(arg_keys[11], (EFEAT, HID), jnp.float32) ** block_scale(arg_keys[11], (EFEAT, HID), ((1, 8),), -0.2, 0.2)), 222.72, 890.88),
        "edge_out_m1": gaussian(arg_keys[12], (HID, HID * HID), (0.19 * EDGES ** 0.5), 448.0, ((0, 8), (1, 4)), jnp.float32),
        "edge_out_m2": jnp.clip(jnp.exp(math.log(22450.176) - 1.3862944 * jax.random.uniform(arg_keys[13], (HID, HID * HID), jnp.float32) ** block_scale(arg_keys[13], (HID, HID * HID), ((0, 8), (1, 4)), -0.2, 0.2)), 5612.544, 22450.176),
        "gru_m1": gaussian(arg_keys[14], (2, 3, HID, HID), (0.13 * ATOMS ** 0.5), 56.0, ((2, 8), (3, 4)), jnp.float32),
        "gru_m2": jnp.clip(jnp.exp(math.log(378.624) - 1.3862944 * jax.random.uniform(arg_keys[15], (2, 3, HID, HID), jnp.float32) ** block_scale(arg_keys[15], (2, 3, HID, HID), ((2, 8), (3, 4)), -0.2, 0.2)), 94.656, 378.624),
    }


@jax.custom_vjp
def low(v):
    return lax.optimization_barrier(v.astype(jnp.bfloat16)).astype(jnp.float32)

@jax.custom_vjp
def low_back(v):
    return v

def low_keep(v):
    return (low(v), None)

def low_pass(kept, grad):
    return (grad,)

def back_keep(v):
    return (v, None)

def back_low(kept, grad):
    return (low(grad),)
low.defvjp(low_keep, low_pass)
low_back.defvjp(back_keep, back_low)
highest = lax.Precision.HIGHEST
beta_one = 0.5
beta_two = 0.5
learn_rate = 0.05
decay_rate = 0.01
epsilon = 1e-08

def adam_update(weight, gradient, first_moment, second_moment):
    first_new = beta_one * first_moment + (1.0 - beta_one) * gradient
    second_new = beta_two * second_moment + (1.0 - beta_two) * gradient * gradient
    mean_hat = first_new / (1.0 - beta_one ** STEP)
    square_hat = second_new / (1.0 - beta_two ** STEP)
    weight_new = weight - learn_rate * (mean_hat / (jnp.sqrt(square_hat) + epsilon) + decay_rate * weight)
    return (first_new, second_new, weight_new, weight_new.astype(jnp.bfloat16))

def atom_table(indices):
    atom_iota = jnp.arange(MOL_ATOMS, dtype=jnp.int32)
    return (indices[:, None] == atom_iota[None, :]).astype(jnp.float32)

def reference(node_state, edge_feat, sender, receiver, edge_mask, node_mask, out_grad, edge_in, edge_out, gru_weight, edge_in_m1, edge_in_m2, edge_out_m1, edge_out_m2, gru_m1, gru_m2):
    states = node_state.astype(jnp.float32)
    features = edge_feat.astype(jnp.float32)
    senders = sender.reshape(MOLECULES, MOL_EDGES)
    receivers = receiver.reshape(MOLECULES, MOL_EDGES)
    edge_live = edge_mask.reshape(MOLECULES, MOL_EDGES).astype(jnp.float32)
    atom_live = node_mask.astype(jnp.float32)[:, None]

    def layer(states, features, weight_in, weight_out, weight_gru):
        w_in = low(weight_in)
        w_out = low(weight_out)
        w_gru = low(weight_gru)
        per_features = features.reshape(EFEAT, MOLECULES, MOL_EDGES).transpose(1, 0, 2)
        per_states = states.reshape(MOLECULES, MOL_ATOMS, HID)

        def molecule_messages(pieces):
            features_m, senders_m, receivers_m, live_m, states_m = pieces
            preact = low_back(jnp.dot(features_m.T, w_in, precision=highest))
            hidden = low(jax.nn.silu(preact))
            matrices = low(low_back(jnp.dot(hidden, w_out, precision=highest))).reshape(MOL_EDGES, HID, HID)
            gathered = jnp.dot(atom_table(senders_m), states_m, precision=highest)
            message = jnp.einsum('erk,ek->er', matrices, gathered, precision=highest) * live_m[:, None]
            return jnp.dot(atom_table(receivers_m).T, message, precision=highest)
        summed = lax.map(jax.checkpoint(molecule_messages), (per_features, senders, receivers, edge_live, per_states))
        summed = low(low_back(summed.reshape(ATOMS, HID)))
        gate_in = low_back(jnp.einsum('ai,gij->gaj', summed, w_gru[0], precision=highest))
        gate_state = low_back(jnp.einsum('ai,gij->gaj', states, w_gru[1], precision=highest))
        reset_gate = jax.nn.sigmoid(gate_in[0] + gate_state[0])
        update = jax.nn.sigmoid(gate_in[1] + gate_state[1])
        candidate = jnp.tanh(gate_in[2] + reset_gate * gate_state[2])
        return atom_live * ((1.0 - update) * candidate + update * states)
    out_state, pullback = jax.vjp(layer, states, features, edge_in, edge_out, gru_weight)
    grad_state, grad_edges, grad_in, grad_out, grad_gru = pullback(out_grad)
    in_first, in_second, in_new, in_low = adam_update(edge_in, grad_in, edge_in_m1, edge_in_m2)
    out_first, out_second, out_new, out_low = adam_update(edge_out, grad_out, edge_out_m1, edge_out_m2)
    gru_first, gru_second, gru_new, gru_low = adam_update(gru_weight, grad_gru, gru_m1, gru_m2)
    return (out_state, grad_state, grad_edges, in_first, in_second, in_new, in_low, out_first, out_second, out_new, out_low, gru_first, gru_second, gru_new, gru_low)
```

```python
import functools

import jax
import jax.numpy as jnp
from jax import lax
from jax.experimental import pallas as pl
from jax.experimental.pallas import tpu as pltpu
from jax.sharding import PartitionSpec as P

HID = 128
EFEAT = 16
MA = 29
ME = 812
PADA = 32
STEP = 5
DXC = 4
MESH = pl.DeviceIdType.MESH
VMEM_LIMIT = 60 << 20
bf = jnp.bfloat16
f32 = jnp.float32
NT = (((1,), (1,)), ((), ()))
TN = (((0,), (0,)), ((), ()))
NN = (((1,), (0,)), ((), ()))

def dot(a,b,dn): return lax.dot_general(a,b,dn,preferred_element_type=f32)

def lane_take(x, src, dst):
    sh=(dst-src)%128
    y=pltpu.roll(x,sh,1) if sh else x
    return y

def compute_kernel(nm, ndp, nmp, hl, wr, il,
        feat_ref, key_ref, xs_ref, wall_ref,
        grads_ref, outs_ref, ge_ref,
        featp, kron, emat, hid, slope, bmat, cmat, dpre, gin, gacc, gfull, wgs, geacc):
    gr=wr; wi=wr+32
    bases=[(ME*i//128)*128 for i in range(nm)]
    lanes128=lax.broadcasted_iota(jnp.int32,(1,128),1)
    w_in=jnp.zeros((EFEAT,HID),f32)
    for d in range(ndp):
        w_in=w_in+wall_ref[d,0,wi:wi+16,:].astype(f32)
    w_in=w_in.astype(bf)
    delta=(lax.broadcasted_iota(jnp.int32,(PADA,256),0)==lax.broadcasted_iota(jnp.int32,(PADA,256),1)%32)
    @pl.loop(0,16)
    def _(c):
        e=jnp.where(lax.broadcasted_iota(jnp.int32,(HID,256),0)==c*8+lax.broadcasted_iota(jnp.int32,(HID,256),1)//32,1.0,0.0).astype(bf)
        emat[c]=e
        wexp=dot(w_in,e,NN)
        for f in range(EFEAT):
            kron[c,f*32:(f+1)*32,:]=jnp.where(delta,wexp[f:f+1,:],0.0).astype(bf)
    wio=lax.broadcasted_iota(jnp.int32,(PADA,1024),0)
    for m in range(nm):
        b=bases[m]
        sk=key_ref[0:1,b:b+1024]; rk=key_ref[1:2,b:b+1024]
        st=(wio+32*m)==sk
        rt=jnp.where(wio==rk,1.0,0.0).astype(bf)
        ff=feat_ref[:,b:b+1024].astype(f32)
        for q in range(4):
            z=jnp.concatenate([jnp.where(st,ff[f:f+1,:],0.0).astype(bf) for f in range(4*q,4*q+4)],axis=0)
            featp[m*32:(m+1)*32,q*128:(q+1)*128]=dot(rt,z,NT).astype(bf)
    fp=featp[...]
    @pl.loop(0,16)
    def _(c):
        p=dot(fp,kron[c],NN)
        s=0.5+0.5*jnp.tanh(0.5*p)
        h=p*s
        hid[c]=h.astype(bf)
        slope[c]=(s+h-h*s).astype(bf)
    lane=lanes128
    xf=jnp.zeros((nm*32,HID),f32); cf=jnp.zeros((nm*32,HID),f32)
    for j in range(nmp):
        sl=xs_ref[j].astype(f32)
        here=(lane>=32*j)&(lane<32*j+32)
        xf=jnp.where(here,lane_take(sl,0,32*j),xf)
        cf=jnp.where(here,lane_take(sl,32,32*j),cf)
    x=xf.astype(bf)
    @pl.loop(0,ndp)
    def _(d):
        for q in range(hl//2):
            w=jnp.concatenate([wall_ref[d,j,(2*q+t)*32:(2*q+t+1)*32,:] for t in range(2) for j in range(nmp)],axis=0)
            o=dot(x,w,NT).astype(bf)
            bmat[d*hl+2*q]=o[:,:128]
            bmat[d*hl+2*q+1]=o[:,128:]
    sums=[]
    for m in range(nm):
        hm=jnp.concatenate([hid[c,m*32:(m+1)*32,:] for c in range(16)],axis=1)
        sums.append(dot(hm,bmat[:,m*32:(m+1)*32,:].reshape(4096,128),NN))
    summed=jnp.concatenate(sums,axis=0).astype(bf)
    for s in range(2):
        for j in range(nmp):
            for d in range(ndp):
                wgs[s,j,d*il:(d+1)*il,:]=wall_ref[d,j,gr+16*s:gr+16*s+16,:].astype(f32)[:il]
    wg=[[wgs[s,j].astype(bf) for j in range(nmp)] for s in range(2)]
    def gates(a,s):
        outs=[dot(a,wg[s][j],NN) for j in range(nmp)]
        res=[]
        for g in range(3):
            t=None
            for j in range(nmp):
                y=lane_take(outs[j],32*g,32*j)
                here=(lane>=32*j)&(lane<32*j+32)
                t=y if t is None else jnp.where(here,y,t)
            res.append(t)
        return res
    gi=gates(summed,0); gs=gates(x,1)
    def sig(v): return 0.5+0.5*jnp.tanh(0.5*v)
    reset=sig(gi[0]+gs[0]); update=sig(gi[1]+gs[1]); cand=jnp.tanh(gi[2]+reset*gs[2])
    ostate=(1.0-update)*cand+update*xf
    dc=cf*(1.0-update)*(1.0-cand*cand)
    du=cf*(xf-cand)*update*(1.0-update)
    dr=dc*gs[2]*reset*(1.0-reset)
    def pack(gl,j):
        t=jnp.zeros((nm*32,HID),f32)
        for g in range(3):
            here=(lane>=32*g)&(lane<32*g+32)
            t=jnp.where(here,lane_take(gl[g],32*j,32*g),t)
        return t.astype(bf)
    al=[];bl=[]
    for j in range(nmp):
        a=pack([dr,du,dc],j); b=pack([dr,du,dc*reset],j)
        al.append(a);bl.append(b)
        for s,(l,r) in enumerate(((summed,a),(x,b))):
            gg=dot(l,r,TN)
            for d in range(ndp):
                part=gg[d*il:(d+1)*il]
                if il<16:
                    part=jnp.concatenate([part,jnp.zeros((16-il,128),f32)],axis=0)
                grads_ref[d,j,gr+16*s:gr+16*s+16,:]=part.astype(bf)
    dsum=dot(jnp.concatenate(al,axis=1),jnp.concatenate(wg[0],axis=1),NT)
    gfull[:,128:256]=cf*update
    gfull[:,0:128]=dot(jnp.concatenate(bl,axis=1),jnp.concatenate(wg[1],axis=1),NT)
    ds=dsum.astype(bf)
    zero=jnp.zeros((32,128),bf)
    for p in range(nm//2):
        blk=jnp.concatenate([jnp.concatenate([ds[p*64:p*64+32],zero],axis=1),jnp.concatenate([zero,ds[p*64+32:p*64+64]],axis=1)],axis=0)
        @pl.loop(0,16)
        def _(c):
            o=dot(hid[c,p*64:(p+1)*64,:],blk,TN).astype(bf)
            cmat[pl.ds(c*8,8),p*64:p*64+32,:]=o[:,:128].reshape(8,32,128)
            cmat[pl.ds(c*8,8),p*64+32:p*64+64,:]=o[:,128:].reshape(8,32,128)
    @pl.loop(0,ndp)
    def _(d):
        for q in range(hl):
            o=dot(cmat[d*hl+q],x,TN).astype(bf)
            for j in range(nmp):
                grads_ref[d,j,q*32:(q+1)*32,:]=o[32*j:32*j+32]
    gacc[...]=jnp.zeros(gacc.shape,f32)
    @pl.loop(0,ndp)
    def _(d):
        for q4 in range(hl//min(DXC,hl)):
            qs=range(q4*min(DXC,hl),(q4+1)*min(DXC,hl))
            cc=jnp.concatenate([cmat[d*hl+q] for q in qs],axis=1)
            w=jnp.concatenate([wall_ref[d,j,q*32:(q+1)*32,:] for q in qs for j in range(nmp)],axis=0)
            gacc[...]+=dot(cc,w,NN)
    gfin=gacc[...]+gfull[:,0:128]+gfull[:,128:256]
    for j in range(nmp):
        a=lane_take(ostate,32*j,0); b=lane_take(gfin,32*j,32)
        outs_ref[j]=jnp.where(lane<32,a,b).astype(bf)
    for m in range(nm):
        dm=ds[m*32:(m+1)*32]
        for c in range(16):
            o=dot(dm,bmat[c*8:(c+1)*8,m*32:(m+1)*32,:].reshape(256,128),NT)
            dpre[c,m*32:(m+1)*32,:]=(o*slope[c,m*32:(m+1)*32,:].astype(f32)).astype(bf)
    gfull[...]=jnp.zeros(gfull.shape,f32)
    gin[...]=jnp.zeros(gin.shape,f32)
    @pl.loop(0,16)
    def _(c):
        dp_=dpre[c]
        gfull[...]+=dot(dp_,kron[c],NT)
        full=dot(fp,dp_,TN)
        full=jnp.where(delta[None],full.reshape(16,32,256),0.0).sum(axis=1)
        gin[...]+=dot(full.astype(bf),emat[c],NT)
    gin_bf=gin[...].astype(bf)
    for d in range(ndp):
        for j in range(nmp):
            grads_ref[d,j,wi:wi+16,:]=gin_bf
    gb=gfull[...].astype(bf)
    geacc[...]=jnp.zeros(geacc.shape,f32)
    for m in range(nm):
        b=bases[m]
        sk=key_ref[0:1,b:b+1024]; rk=key_ref[1:2,b:b+1024]
        for n in range(4):
            lo=b+n*256
            w2=wio[:,:256]
            st=(w2+32*m)==key_ref[0:1,lo:lo+256]
            rt=jnp.where(w2==key_ref[1:2,lo:lo+256],1.0,0.0).astype(bf)
            u=dot(gb[m*32:(m+1)*32],rt,TN).reshape(16,32,256)
            geacc[:,lo:lo+256]+=jnp.where(st[None],u,0.0).sum(axis=1)
    ge_ref[...]=geacc[...].astype(bf)

def compute(feat,key,xs,wall,nm,ndp,nmp,hl,wr,il):
    rb=wall.shape[2]; win=feat.shape[1]
    return pl.pallas_call(functools.partial(compute_kernel,nm,ndp,nmp,hl,wr,il),
        out_shape=(jax.ShapeDtypeStruct((ndp,nmp,rb,128),bf),jax.ShapeDtypeStruct((nmp,nm*32,128),bf),jax.ShapeDtypeStruct((16,win),bf)),
        in_specs=[pl.BlockSpec(memory_space=pltpu.VMEM)]*4,
        out_specs=(pl.BlockSpec(memory_space=pltpu.VMEM),)*3,
        scratch_shapes=[pltpu.VMEM((nm*32,512),bf),pltpu.VMEM((16,512,256),bf),pltpu.VMEM((16,128,256),bf),
            pltpu.VMEM((16,nm*32,256),bf),pltpu.VMEM((16,nm*32,256),bf),
            pltpu.VMEM((128,nm*32,128),bf),pltpu.VMEM((128,nm*32,128),bf),pltpu.VMEM((16,nm*32,256),bf),
            pltpu.VMEM((16,128),f32),pltpu.VMEM((nm*32,128),f32),pltpu.VMEM((nm*32,512),f32),pltpu.VMEM((2,nmp,128,128),f32),pltpu.VMEM((16,win),f32)],
        compiler_params=pltpu.CompilerParams(vmem_limit_bytes=60<<20))(feat,key,xs,wall)

def places(ndp, nmp):
    d = lax.axis_index("dp")
    m = lax.axis_index("mp")
    half = ndp // 2
    u = d // 2
    c = d % 2
    zp = [(d, (m + i) % nmp) for i in range(1, nmp)]
    pp = [(2 * ((u + t) % half) + c, m) for t in range(1, half)]
    cp = (2 * u + (1 - c), m)
    return d, m, u, c, half, zp, pp, cp


def greet(plist):
    bar = pltpu.get_barrier_semaphore()
    for p in plist:
        pl.semaphore_signal(bar, inc=1, device_id=p, device_id_type=MESH)
    pl.semaphore_wait(bar, len(plist))


def rcopy(src, dst, ssem, rsem, dev):
    return pltpu.make_async_remote_copy(
        src_ref=src, dst_ref=dst, send_sem=ssem, recv_sem=rsem, device_id=dev, device_id_type=MESH
    )


def gather_kernel(ndp, nmp, blk_ref, xs_ref, wall_ref, xo_ref, zsem, psem, csem, rsem, xssem, xrsem, lsem):
    d, m, u, c, half, zp, pp, cp = places(ndp, nmp)
    greet(zp + pp + [cp])
    local = [
        pltpu.make_async_copy(blk_ref, wall_ref.at[d, m], lsem.at[0]),
        pltpu.make_async_copy(xs_ref.at[m], xo_ref.at[m], lsem.at[1]),
    ]
    sends = []
    for i, p in enumerate(zp):
        sends.append(rcopy(xs_ref.at[p[1]], xo_ref.at[m], xssem.at[i], xrsem.at[m], p))
        sends.append(rcopy(blk_ref, wall_ref.at[d, m], zsem.at[i], rsem.at[d, m], p))
    for x in sends + local:
        x.start()

    def push(n, row, col, plane):
        src = wall_ref.at[row, col]
        out = []
        if plane:
            for t, p in enumerate(pp):
                out.append(rcopy(src, src, psem.at[n, t], rsem.at[row, col], p))
        out.append(rcopy(src, src, csem.at[n if plane else nmp + n], rsem.at[row, col], cp))
        for x in out:
            x.start()
        sends.extend(out)

    def arrived(row, col):
        here = wall_ref.at[row, col]
        rcopy(here, here, zsem.at[0], rsem.at[row, col], cp).wait_recv()

    local[0].wait()
    push(0, d, m, True)
    for i in range(1, nmp):
        col = (m - i + nmp) % nmp
        arrived(d, col)
        push(i, d, col, True)
    n = 0
    for i in range(nmp):
        col = (m - i + nmp) % nmp
        for t in range(1, half):
            row = 2 * ((u - t + half) % half) + c
            arrived(row, col)
            push(n, row, col, False)
            n += 1
    for i in range(nmp):
        for t in range(half):
            arrived(2 * ((u - t + half) % half) + (1 - c), (m - i + nmp) % nmp)
    for i in range(1, nmp):
        col = (m - i + nmp) % nmp
        here = xo_ref.at[col]
        rcopy(here, here, xssem.at[0], xrsem.at[col], cp).wait_recv()
    local[1].wait()
    for x in sends:
        x.wait_send()


def gather(blk, xs, ndp, nmp):
    rb = blk.shape[0]
    half = ndp // 2
    dma = pltpu.SemaphoreType.DMA
    return pl.pallas_call(
        functools.partial(gather_kernel, ndp, nmp),
        out_shape=(
            jax.ShapeDtypeStruct((ndp, nmp, rb, 128), bf),
            jax.ShapeDtypeStruct(xs.shape, bf),
        ),
        in_specs=[pl.BlockSpec(memory_space=pltpu.VMEM)] * 2,
        out_specs=(pl.BlockSpec(memory_space=pltpu.VMEM),) * 2,
        scratch_shapes=[
            dma((nmp - 1,)),
            dma((nmp, half - 1)),
            dma((nmp + nmp * (half - 1),)),
            dma((ndp, nmp)),
            dma((nmp - 1,)),
            dma((nmp,)),
            dma((2,)),
        ],
        compiler_params=pltpu.CompilerParams(
            collective_id=0, has_side_effects=True, vmem_limit_bytes=VMEM_LIMIT
        ),
    )(blk, xs)


def scatter_kernel(
    ndp, nmp,
    g_ref, ge_ref, os_ref,
    fin_ref, geo_ref, oso_ref,
    rc, sb, rp, zs, rz,
    cs, cr, ps, pr, zsem, zr, os_s, os_r, ge_s, ge_r, lsem,
):
    d, m, u, c, half, zp, pp, cp = places(ndp, nmp)
    greet(zp + pp + [cp])
    local = [
        pltpu.make_async_copy(ge_ref, geo_ref.at[m], lsem.at[0]),
        pltpu.make_async_copy(os_ref.at[m], oso_ref.at[m], lsem.at[1]),
    ]
    sends = []
    order = list(range(1, half)) + [0]
    cols = [(m + i) % nmp for i in range(1, nmp)] + [m]
    for t in order:
        row = 2 * ((u + t) % half) + (1 - c)
        sends.append(rcopy(g_ref.at[row], rc.at[t], cs.at[t], cr.at[t], cp))
    for i, p in enumerate(zp):
        sends.append(rcopy(os_ref.at[p[1]], oso_ref.at[m], os_s.at[i], os_r.at[m], p))
        sends.append(rcopy(ge_ref, geo_ref.at[m], ge_s.at[i], ge_r.at[m], p))
    for x in sends + local:
        x.start()
    for t in order:
        rcopy(rc.at[t], rc.at[t], cs.at[t], cr.at[t], cp).wait_recv()
        if t == 0:
            continue
        row = 2 * ((u + t) % half) + c
        for i, col in enumerate(cols):
            sb[t - 1, i] = (g_ref[row, col].astype(f32) + rc[t, col].astype(f32)).astype(bf)
            x = rcopy(sb.at[t - 1, i], rp.at[t - 1, col], ps.at[t - 1, i], pr.at[t - 1, col], pp[t - 1])
            x.start()
            sends.append(x)
    for i, col in enumerate(cols):
        q = g_ref[d, col].astype(f32) + rc[0, col].astype(f32)
        for t in range(1, half):
            here = rp.at[t - 1, col]
            rcopy(here, here, ps.at[0, 0], pr.at[t - 1, col], cp).wait_recv()
            q = q + rp[t - 1, col].astype(f32)
        if i < nmp - 1:
            zs[i] = q.astype(bf)
            x = rcopy(zs.at[i], rz.at[m], zsem.at[i], zr.at[m], zp[i])
            x.start()
            sends.append(x)
        else:
            fin_ref[...] = q
    for i in range(1, nmp):
        col = (m - i + nmp) % nmp
        here = rz.at[col]
        rcopy(here, here, zsem.at[0], zr.at[col], cp).wait_recv()
        fin_ref[...] += rz[col].astype(f32)
    for i in range(1, nmp):
        col = (m - i + nmp) % nmp
        rcopy(geo_ref.at[col], geo_ref.at[col], ge_s.at[0], ge_r.at[col], cp).wait_recv()
        rcopy(oso_ref.at[col], oso_ref.at[col], os_s.at[0], os_r.at[col], cp).wait_recv()
    for x in local:
        x.wait()
    for x in sends:
        x.wait_send()


def scatter(grads, ge, os, ndp, nmp):
    rb = grads.shape[2]
    half = ndp // 2
    dma = pltpu.SemaphoreType.DMA
    return pl.pallas_call(
        functools.partial(scatter_kernel, ndp, nmp),
        out_shape=(
            jax.ShapeDtypeStruct((rb, 128), f32),
            jax.ShapeDtypeStruct((nmp,) + ge.shape, bf),
            jax.ShapeDtypeStruct(os.shape, bf),
        ),
        in_specs=[pl.BlockSpec(memory_space=pltpu.VMEM)] * 3,
        out_specs=(pl.BlockSpec(memory_space=pltpu.VMEM),) * 3,
        scratch_shapes=[
            pltpu.VMEM((half, nmp, rb, 128), bf),
            pltpu.VMEM((half - 1, nmp, rb, 128), bf),
            pltpu.VMEM((half - 1, nmp, rb, 128), bf),
            pltpu.VMEM((nmp - 1, rb, 128), bf),
            pltpu.VMEM((nmp, rb, 128), bf),
            dma((half,)), dma((half,)),
            dma((half - 1, nmp)), dma((half - 1, nmp)),
            dma((nmp - 1,)), dma((nmp,)),
            dma((nmp - 1,)), dma((nmp,)),
            dma((nmp - 1,)), dma((nmp,)),
            dma((2,)),
        ],
        compiler_params=pltpu.CompilerParams(
            collective_id=1, has_side_effects=True, vmem_limit_bytes=VMEM_LIMIT
        ),
    )(grads, ge, os)


beta_one = 0.5
beta_two = 0.5
learn_rate = 0.05
decay_rate = 0.01
epsilon = 1e-08


def adam_update(weight, gradient, first_moment, second_moment):
    first_new = beta_one * first_moment + (1.0 - beta_one) * gradient
    second_new = beta_two * second_moment + (1.0 - beta_two) * gradient * gradient
    mean_hat = first_new / (1.0 - beta_one**STEP)
    square_hat = second_new / (1.0 - beta_two**STEP)
    weight_new = weight - learn_rate * (
        mean_hat / (jnp.sqrt(square_hat) + epsilon) + decay_rate * weight
    )
    return (first_new, second_new, weight_new, weight_new.astype(bf))


def body(
    ndp, nmp,
    node_state, edge_feat, sender, receiver, edge_mask, node_mask, out_grad,
    edge_in, edge_out, gru_weight,
    edge_in_m1, edge_in_m2, edge_out_m1, edge_out_m2, gru_m1, gru_m2,
):
    d = lax.axis_index("dp")
    m = lax.axis_index("mp")
    atoms = node_state.shape[0]
    edges = sender.shape[0]
    mols = atoms // MA
    nm = mols // nmp
    uw = node_state.shape[1]
    hl = edge_out.shape[0]
    il = gru_weight.shape[2]
    wr = hl * edge_out.shape[1] // HID
    w_rows = edge_out.astype(bf).reshape(wr, HID)
    g_rows = gru_weight.transpose(0, 2, 1, 3).reshape(2, il, 3 * uw).astype(bf)
    g_rows = jnp.pad(g_rows, ((0, 0), (0, 16 - il), (0, HID - 3 * uw))).reshape(32, HID)
    i_rows = lax.dynamic_update_slice(
        jnp.zeros((EFEAT, HID), bf), edge_in.astype(bf), (0, d * edge_in.shape[1])
    )
    blk = jnp.concatenate([w_rows, g_rows, i_rows], axis=0)
    cot = (out_grad * node_mask.astype(f32)[:, None]).astype(bf)
    xs = jnp.concatenate([node_state, cot], axis=1).reshape(mols, MA, 2 * uw)
    xs = jnp.pad(xs, ((0, 0), (0, PADA - MA), (0, HID - 2 * uw))).reshape(nmp, nm * PADA, HID)
    per = nm * ME
    starts = [per * j // 128 * 128 for j in range(nmp)]
    shift = max(per * j - s for j, s in enumerate(starts))
    win = max(ME * i // 128 * 128 for i in range(nm)) + 1024
    assert all(ME * i + shift + ME <= ME * i // 128 * 128 + 1024 for i in range(nm))
    start = (per * m) // 128 * 128
    total = max(starts[-1] + win, edges)
    mol_id = lax.broadcasted_iota(jnp.int32, (1, edges), 1) // ME
    s_key = jnp.where(edge_mask[None] == 1, sender[None] + PADA * mol_id, -1)
    keys = jnp.concatenate([s_key, receiver[None]], axis=0)
    keys = jnp.pad(keys, ((0, 0), (0, total - edges)), constant_values=-1)
    keys = lax.dynamic_slice(keys, (0, start), (2, win))
    keys = keys - jnp.array([[1], [0]], jnp.int32) * (PADA * nm * m)
    feat = lax.dynamic_slice(jnp.pad(edge_feat, ((0, 0), (0, total - edges))), (0, start), (EFEAT, win))

    wall, xo = gather(blk, xs, ndp, nmp)
    grads, outs, ge = compute(feat, keys, xo, wall, nm, ndp, nmp, hl, wr, il)
    fin, geo, oso = scatter(grads, ge, outs, ndp, nmp)

    oso = oso.reshape(mols, PADA, HID)[:, :MA].reshape(atoms, HID).astype(f32)
    out_state = oso[:, :uw] * node_mask.astype(f32)[:, None]
    grad_state = oso[:, uw : 2 * uw]
    grad_edges = jnp.concatenate(
        [geo[j][:, per * j - starts[j] : per * (j + 1) - starts[j]] for j in range(nmp)], axis=1
    ).astype(f32)
    g_out = fin[:wr].reshape(edge_out.shape)
    g_gru = fin[wr : wr + 32].reshape(2, 16, HID)[:, :il, : 3 * uw].reshape(2, il, 3, uw).transpose(0, 2, 1, 3)
    g_in = lax.dynamic_slice(fin[wr + 32 :], (0, d * edge_in.shape[1]), edge_in.shape)
    return (
        (out_state, grad_state, grad_edges)
        + adam_update(edge_in, g_in, edge_in_m1, edge_in_m2)
        + adam_update(edge_out, g_out, edge_out_m1, edge_out_m2)
        + adam_update(gru_weight, g_gru, gru_m1, gru_m2)
    )


def solution(mesh):
    ndp, nmp = mesh.shape["dp"], mesh.shape["mp"]
    rows, lanes, gru = P("dp", "mp"), P(None, "dp"), P(None, None, "dp", "mp")
    edge = P("dp")
    return jax.shard_map(
        functools.partial(body, ndp, nmp),
        mesh=mesh,
        in_specs=(
            rows, lanes, edge, edge, edge, edge, rows,
            lanes, rows, gru, lanes, lanes, rows, rows, gru, gru,
        ),
        out_specs=(rows, rows, lanes) + (lanes,) * 4 + (rows,) * 4 + (gru,) * 4,
        check_vma=False,
    )
```

```python
import functools

import jax
import jax.numpy as jnp
from jax import lax
from jax.experimental import pallas as pl
from jax.experimental.pallas import tpu as pltpu
from jax.sharding import PartitionSpec as P

HID = 128
EFEAT = 16
MA = 29
ME = 812
PADA = 32
STEP = 5
DXC = 4
MESH = pl.DeviceIdType.MESH
VMEM_LIMIT = 60 << 20
bf = jnp.bfloat16
f32 = jnp.float32
NT = (((1,), (1,)), ((), ()))
TN = (((0,), (0,)), ((), ()))
NN = (((1,), (0,)), ((), ()))


def dot(a, b, dims):
    return lax.dot_general(a, b, dims, preferred_element_type=f32)


def roll(x, src, dst):
    shift = (dst - src) % HID
    return pltpu.roll(x, shift, 1) if shift else x


def sig(v):
    return 0.5 + 0.5 * jnp.tanh(0.5 * v)


def rcopy(src, dst, ssem, rsem, dev):
    return pltpu.make_async_remote_copy(
        src_ref=src, dst_ref=dst, send_sem=ssem, recv_sem=rsem, device_id=dev, device_id_type=MESH
    )


class Shape:
    def __init__(self, ndp, nmp, node_state, edge_feat, edge_in, edge_out, gru):
        self.ndp, self.nmp, self.half = ndp, nmp, ndp // 2
        self.atoms, self.uw = node_state.shape
        self.edges = edge_feat.shape[1]
        self.mols = self.atoms // MA
        self.nm = self.mols // nmp
        self.rows = self.nm * PADA
        self.hl, self.il, self.ew = edge_out.shape[0], gru.shape[2], edge_in.shape[1]
        self.rw = edge_out.shape[1] // HID
        self.wr = self.hl * self.rw
        self.rb = self.wr + 32
        self.per = self.nm * ME
        self.starts = [self.per * j // 128 * 128 for j in range(nmp)]
        self.bases = [ME * i // 128 * 128 for i in range(self.nm)]
        self.win = self.bases[-1] + 1024
        self.full = self.edges // 128 * 128
        shift = max(self.per * j - s for j, s in enumerate(self.starts))
        assert all(ME * i + shift + ME <= b + 1024 for i, b in enumerate(self.bases))
        assert self.starts[-1] + self.win - 128 == self.full
        assert all(b - a == self.win - 128 for a, b in zip(self.starts, self.starts[1:]))


def kernel(
    z,
    eo_ref, ei_ref, gw_ref, xc_ref, feat_ref, snd_ref, rcv_ref, msk_ref,
    go_ref, gg_ref, gi_ref, at_ref, ge_ref,
    wall, xsb, xo, wis, stage, stage2, wtmp, stmp, itmp, featw, keyw,
    featp, kron, emat, hid, slope, bmat, cmat, dpre, gacc, gfull, gin, geacc,
    grads, rc, sb, rp, zs, rz, fin, osb, oso, geo, gis, giz, giz_s,
    zsem, psem, csem, rsem, xs_s, xs_r, wi_s, wi_r, lsem,
    cs, cr, ps, pr, z2, zr, os_s, os_r, ge_s, ge_r, gi_s, gi_r, gz_s, gz_r,
):
    ndp, nmp, half, nm = z.ndp, z.nmp, z.half, z.nm
    hl, il, wr, rb, rw = z.hl, z.il, z.wr, z.rb, z.rw
    d = lax.axis_index("dp")
    m = lax.axis_index("mp")
    u = d // 2
    c = d % 2
    zp = [(d, (m + i) % nmp) for i in range(1, nmp)]
    pp = [(2 * ((u + t) % half) + c, m) for t in range(1, half)]
    cp = (2 * u + (1 - c), m)
    dpp = [((d + i) % ndp, m) for i in range(1, ndp)]
    bar = pltpu.get_barrier_semaphore()
    for p in zp + dpp:
        pl.semaphore_signal(bar, inc=1, device_id=p, device_id_type=MESH)
    lane = lax.broadcasted_iota(jnp.int32, (1, HID), 1)
    for r in range(rw):
        wtmp[:, r, :] = eo_ref[:, r * HID : (r + 1) * HID]
    wall[d, m, 0:wr, :] = wtmp[...].reshape(wr, HID).astype(bf)
    stmp[...] = jnp.zeros(stmp.shape, f32)
    for s in range(2):
        for g in range(3):
            stmp[16 * s : 16 * s + il, g * z.uw : (g + 1) * z.uw] = gw_ref[s, g]
    wall[d, m, wr:rb, :] = stmp[...].astype(bf)
    itmp[...] = jnp.zeros(itmp.shape, f32)
    itmp[:, 0 : z.ew] = ei_ref[...]
    wis[d] = pltpu.roll(itmp[...], d * z.ew, 1).astype(bf)
    stage[...] = xc_ref[...].astype(f32)
    stage2[...] = jnp.zeros(stage2.shape, f32)
    for i in range(z.mols):
        stage2[i * PADA : i * PADA + MA, 0 : 2 * z.uw] = stage[i * MA : (i + 1) * MA, :]
    for j in range(nmp):
        xsb[j] = stage2[j * z.rows : (j + 1) * z.rows, :].astype(bf)
    pl.semaphore_wait(bar, len(zp + dpp))

    sends = []

    def go(*copies):
        for x in copies:
            x.start()
        sends.extend(copies)

    for i, p in enumerate(dpp):
        go(rcopy(wis.at[d], wis.at[d], wi_s.at[i], wi_r.at[d], p))

    def push(n, row, col, plane):
        src = wall.at[row, col]
        if plane:
            for t, p in enumerate(pp):
                go(rcopy(src, src, psem.at[n, t], rsem.at[row, col], p))
        go(rcopy(src, src, csem.at[n if plane else nmp + n], rsem.at[row, col], cp))

    def arrived(row, col):
        here = wall.at[row, col]
        rcopy(here, here, zsem.at[0], rsem.at[row, col], cp).wait_recv()

    for i, p in enumerate(zp):
        go(rcopy(wall.at[d, m], wall.at[d, m], zsem.at[i], rsem.at[d, m], p))
    push(0, d, m, True)
    for i, p in enumerate(zp):
        go(rcopy(xsb.at[p[1]], xo.at[m], xs_s.at[i], xs_r.at[m], p))
    xo[m] = xsb[m]

    start = pl.multiple_of(z.per * m // 128 * 128, 128)
    shift = z.per * m - start
    main = z.win - 128
    featw[:, 0:main] = feat_ref[:, pl.ds(start, main)]
    for n, ref in enumerate((snd_ref, rcv_ref, msk_ref)):
        keyw[n : n + 1, 0:main] = ref[:, pl.ds(start, main)]

    @pl.when(m < nmp - 1)
    def _():
        after = pl.multiple_of(start + main, 128)
        featw[:, main:] = feat_ref[:, pl.ds(after, 128)]
        for n, ref in enumerate((snd_ref, rcv_ref, msk_ref)):
            keyw[n : n + 1, main:] = ref[:, pl.ds(after, 128)]

    @pl.when(m == nmp - 1)
    def _():
        featw[:, main:] = jnp.zeros((EFEAT, 128), bf)
        keyw[:, main:] = jnp.zeros((3, 128), jnp.int32)
        tail = z.edges - z.full
        if tail:
            featw[:, main : main + tail] = feat_ref[:, z.full :]
            for n, ref in enumerate((snd_ref, rcv_ref, msk_ref)):
                keyw[n : n + 1, main : main + tail] = ref[:, z.full :]

    def sender_key(i, lo, count):
        place = lax.broadcasted_iota(jnp.int32, (1, count), 1) + (lo - ME * i) - shift
        ok = (keyw[2:3, lo : lo + count] == 1) & (place >= 0) & (place < ME)
        return jnp.where(ok, keyw[0:1, lo : lo + count], -1)

    wio = lax.broadcasted_iota(jnp.int32, (PADA, 1024), 0)

    def permute(i):
        b = z.bases[i]
        st = wio == sender_key(i, b, 1024)
        rt = jnp.where(wio == keyw[1:2, b : b + 1024], 1.0, 0.0).astype(bf)
        ff = featw[:, b : b + 1024].astype(f32)
        for q in range(4):
            zz = jnp.concatenate(
                [jnp.where(st, ff[f : f + 1, :], 0.0).astype(bf) for f in range(4 * q, 4 * q + 4)], axis=0
            )
            featp[i * PADA : (i + 1) * PADA, q * 128 : (q + 1) * 128] = dot(rt, zz, NT).astype(bf)

    for i in range(nm):
        permute(i)
        if i == nm - 1:
            arrived(d, (m - 1 + nmp) % nmp)
            push(1, d, (m - 1 + nmp) % nmp, True)

    for i in range(1, ndp):
        row = (d - i + ndp) % ndp
        rcopy(wis.at[row], wis.at[row], wi_s.at[0], wi_r.at[row], cp).wait_recv()
    w_in = wis[...].astype(f32).sum(axis=0).astype(bf)
    delta = (
        lax.broadcasted_iota(jnp.int32, (PADA, 256), 0)
        == lax.broadcasted_iota(jnp.int32, (PADA, 256), 1) % PADA
    )

    @pl.loop(0, 16)
    def _(k):
        e = jnp.where(
            lax.broadcasted_iota(jnp.int32, (HID, 256), 0)
            == k * 8 + lax.broadcasted_iota(jnp.int32, (HID, 256), 1) // PADA,
            1.0,
            0.0,
        ).astype(bf)
        emat[k] = e
        wexp = dot(w_in, e, NN)
        for f in range(EFEAT):
            kron[k, f * PADA : (f + 1) * PADA, :] = jnp.where(delta, wexp[f : f + 1, :], 0.0).astype(bf)

    for i in range(2, nmp):
        arrived(d, (m - i + nmp) % nmp)
        push(i, d, (m - i + nmp) % nmp, True)
    fp = featp[...]

    @pl.loop(0, 16)
    def _(k):
        p = dot(fp, kron[k], NN)
        s = sig(p)
        h = p * s
        hid[k] = h.astype(bf)
        slope[k] = (s + h - h * s).astype(bf)

    for i in range(1, nmp):
        col = (m - i + nmp) % nmp
        rcopy(xo.at[col], xo.at[col], xs_s.at[0], xs_r.at[col], cp).wait_recv()
    xf = jnp.zeros((z.rows, HID), f32)
    cf = jnp.zeros((z.rows, HID), f32)
    for j in range(nmp):
        sl = xo[j].astype(f32)
        here = (lane >= z.uw * j) & (lane < z.uw * (j + 1))
        xf = jnp.where(here, roll(sl, 0, z.uw * j), xf)
        cf = jnp.where(here, roll(sl, z.uw, z.uw * j), cf)
    x = xf.astype(bf)

    n = 0
    for i in range(nmp):
        col = (m - i + nmp) % nmp
        for t in range(1, half):
            row = 2 * ((u - t + half) % half) + c
            arrived(row, col)
            push(n, row, col, False)
            n += 1

    def rows_of(row, qs):
        return jnp.concatenate(
            [wall[row, j, q * rw : (q + 1) * rw, :] for q in qs for j in range(nmp)], axis=0
        )

    def make_b(row):
        for q in range(hl // 2):
            o = dot(x, rows_of(row, (2 * q, 2 * q + 1)), NT).astype(bf)
            bmat[row * hl + 2 * q] = o[:, :HID]
            bmat[row * hl + 2 * q + 1] = o[:, HID:]

    @pl.loop(0, half)
    def _(t):
        make_b(2 * t + c)

    for i in range(nmp):
        for t in range(half):
            arrived(2 * ((u - t + half) % half) + (1 - c), (m - i + nmp) % nmp)

    @pl.loop(0, half)
    def _(t):
        make_b(2 * t + (1 - c))

    sums = []
    for i in range(nm):
        hm = jnp.concatenate([hid[k, i * PADA : (i + 1) * PADA, :] for k in range(16)], axis=1)
        sums.append(dot(hm, bmat[:, i * PADA : (i + 1) * PADA, :].reshape(PADA * HID, HID), NN))
    summed = jnp.concatenate(sums, axis=0).astype(bf)

    def gru_rows(s, j):
        for k in range(ndp):
            gfull[k * il : (k + 1) * il, 0:HID] = wall[k, j, wr + 16 * s : wr + 16 * s + 16, :].astype(f32)[:il]
        return gfull[0:HID, 0:HID].astype(bf)

    wg = [[gru_rows(s, j) for j in range(nmp)] for s in range(2)]

    def gates(a, s):
        outs = [dot(a, wg[s][j], NN) for j in range(nmp)]
        res = []
        for g in range(3):
            t = None
            for j in range(nmp):
                y = roll(outs[j], z.uw * g, z.uw * j)
                here = (lane >= z.uw * j) & (lane < z.uw * (j + 1))
                t = y if t is None else jnp.where(here, y, t)
            res.append(t)
        return res

    gi = gates(summed, 0)
    gs = gates(x, 1)
    reset = sig(gi[0] + gs[0])
    update = sig(gi[1] + gs[1])
    cand = jnp.tanh(gi[2] + reset * gs[2])
    ostate = (1.0 - update) * cand + update * xf
    dc = cf * (1.0 - update) * (1.0 - cand * cand)
    du = cf * (xf - cand) * update * (1.0 - update)
    dr = dc * gs[2] * reset * (1.0 - reset)

    def pack(gl, j):
        t = jnp.zeros((z.rows, HID), f32)
        for g in range(3):
            here = (lane >= z.uw * g) & (lane < z.uw * (g + 1))
            t = jnp.where(here, roll(gl[g], z.uw * j, z.uw * g), t)
        return t.astype(bf)

    al = [pack([dr, du, dc], j) for j in range(nmp)]
    bl = [pack([dr, du, dc * reset], j) for j in range(nmp)]
    ds = dot(jnp.concatenate(al, axis=1), jnp.concatenate(wg[0], axis=1), NT).astype(bf)
    gfull[:, HID : 2 * HID] = cf * update
    gfull[:, 0:HID] = dot(jnp.concatenate(bl, axis=1), jnp.concatenate(wg[1], axis=1), NT)
    for j in range(nmp):
        for s, (l, r) in enumerate(((summed, al[j]), (x, bl[j]))):
            gg = dot(l, r, TN)
            for k in range(ndp):
                part = gg[k * il : (k + 1) * il]
                if il < 16:
                    part = jnp.concatenate([part, jnp.zeros((16 - il, HID), f32)], axis=0)
                grads[k, j, wr + 16 * s : wr + 16 * s + 16, :] = part.astype(bf)

    zero = jnp.zeros((PADA, HID), bf)
    for p in range(nm // 2):
        lo = p * 64
        blk = jnp.concatenate(
            [
                jnp.concatenate([ds[lo : lo + 32], zero], axis=1),
                jnp.concatenate([zero, ds[lo + 32 : lo + 64]], axis=1),
            ],
            axis=0,
        )

        @pl.loop(0, 16)
        def _(k):
            o = dot(hid[k, lo : lo + 64, :], blk, TN).astype(bf)
            cmat[pl.ds(k * 8, 8), lo : lo + 32, :] = o[:, :HID].reshape(8, PADA, HID)
            cmat[pl.ds(k * 8, 8), lo + 32 : lo + 64, :] = o[:, HID:].reshape(8, PADA, HID)

    def grad_w(row):
        for q in range(hl):
            o = dot(cmat[row * hl + q], x, TN).astype(bf)
            for j in range(nmp):
                grads[row, j, q * rw : (q + 1) * rw, :] = o[rw * j : rw * (j + 1)]

    order = list(range(1, half)) + [0]
    cols = [(m + i) % nmp for i in range(1, nmp)] + [m]

    def core_arrived(t):
        rcopy(rc.at[t], rc.at[t], cs.at[t], cr.at[t], cp).wait_recv()
        if t == 0:
            return
        row = 2 * ((u + t) % half) + c
        for i, col in enumerate(cols):
            sb[t - 1, i] = (grads[row, col].astype(f32) + rc[t, col].astype(f32)).astype(bf)
            go(rcopy(sb.at[t - 1, i], rp.at[t - 1, col], ps.at[t - 1, i], pr.at[t - 1, col], pp[t - 1]))

    for n, t in enumerate(order):
        row = 2 * ((u + t) % half) + (1 - c)
        grad_w(row)
        go(rcopy(grads.at[row], rc.at[t], cs.at[t], cr.at[t], cp))
        grad_w(2 * ((u + t) % half) + c)
        if n > 0:
            core_arrived(order[n - 1])
    core_arrived(0)

    gacc[...] = jnp.zeros(gacc.shape, f32)
    step = min(DXC, hl)

    @pl.loop(0, ndp)
    def _(row):
        for q in range(0, hl, step):
            qs = range(q, q + step)
            cc = jnp.concatenate([cmat[row * hl + k] for k in qs], axis=1)
            gacc[...] += dot(cc, rows_of(row, qs), NN)

    gfin = gacc[...] + gfull[:, 0:HID] + gfull[:, HID : 2 * HID]
    for j in range(nmp):
        a = roll(ostate, z.uw * j, 0)
        b = roll(gfin, z.uw * j, z.uw)
        osb[j] = jnp.where(lane < z.uw, a, b).astype(bf)
    for i, p in enumerate(zp):
        go(rcopy(osb.at[p[1]], oso.at[m], os_s.at[i], os_r.at[m], p))
    oso[m] = osb[m]

    for i in range(nm):
        dm = ds[i * PADA : (i + 1) * PADA]
        for k in range(16):
            o = dot(dm, bmat[k * 8 : (k + 1) * 8, i * PADA : (i + 1) * PADA, :].reshape(256, HID), NT)
            dpre[k, i * PADA : (i + 1) * PADA, :] = (
                o * slope[k, i * PADA : (i + 1) * PADA, :].astype(f32)
            ).astype(bf)
    gfull[...] = jnp.zeros(gfull.shape, f32)
    gin[...] = jnp.zeros(gin.shape, f32)

    @pl.loop(0, 16)
    def _(k):
        dp_ = dpre[k]
        gfull[...] += dot(dp_, kron[k], NT)
        full = dot(fp, dp_, TN)
        full = jnp.where(delta[None], full.reshape(EFEAT, PADA, 256), 0.0).sum(axis=1)
        gin[...] += dot(full.astype(bf), emat[k], NT)

    gis[d] = gin[...].astype(bf)
    for i, p in enumerate(dpp):
        go(rcopy(gis.at[d], gis.at[d], gi_s.at[i], gi_r.at[d], p))

    def to_z(i):
        col = cols[i]
        q = grads[d, col].astype(f32) + rc[0, col].astype(f32)
        for t in range(1, half):
            here = rp.at[t - 1, col]
            rcopy(here, here, ps.at[0, 0], pr.at[t - 1, col], cp).wait_recv()
            q = q + rp[t - 1, col].astype(f32)
        if i < nmp - 1:
            zs[i] = q.astype(bf)
            go(rcopy(zs.at[i], rz.at[m], z2.at[i], zr.at[m], zp[i]))
        else:
            fin[...] = q

    gb = gfull[...].astype(bf)
    geacc[...] = jnp.zeros(geacc.shape, f32)
    w2 = wio[:, :256]
    for i in range(nm):
        for n in range(4):
            lo = z.bases[i] + n * 256
            st = w2 == sender_key(i, lo, 256)
            rt = jnp.where(w2 == keyw[1:2, lo : lo + 256], 1.0, 0.0).astype(bf)
            o = dot(gb[i * PADA : (i + 1) * PADA], rt, TN).reshape(EFEAT, PADA, 256)
            geacc[:, lo : lo + 256] += jnp.where(st[None], o, 0.0).sum(axis=1)
    geo[m] = geacc[...].astype(bf)
    for i, p in enumerate(zp):
        go(rcopy(geo.at[m], geo.at[m], ge_s.at[i], ge_r.at[m], p))

    gi_sum = gis[d].astype(f32)
    for i in range(1, ndp):
        row = (d - i + ndp) % ndp
        rcopy(gis.at[row], gis.at[row], gi_s.at[0], gi_r.at[row], cp).wait_recv()
        gi_sum = gi_sum + gis[row].astype(f32)
    giz_s[...] = gi_sum.astype(bf)
    for i, p in enumerate(zp):
        go(rcopy(giz_s, giz.at[m], gz_s.at[i], gz_r.at[m], p))
    for i in range(nmp):
        to_z(i)

    for i in range(1, nmp):
        col = (m - i + nmp) % nmp
        rcopy(oso.at[col], oso.at[col], os_s.at[0], os_r.at[col], cp).wait_recv()
    for j in range(nmp):
        stage2[j * z.rows : (j + 1) * z.rows, :] = oso[j].astype(f32)
    for i in range(z.mols):
        at_ref[i * MA : (i + 1) * MA, :] = stage2[i * PADA : i * PADA + MA, :]

    for i in range(1, nmp):
        col = (m - i + nmp) % nmp
        rcopy(giz.at[col], giz.at[col], gz_s.at[0], gz_r.at[col], cp).wait_recv()
        gi_sum = gi_sum + giz[col].astype(f32)
    gi_ref[...] = pltpu.roll(gi_sum, HID - d * z.ew, 1)[:, 0 : z.ew]
    for i in range(1, nmp):
        col = (m - i + nmp) % nmp
        rcopy(rz.at[col], rz.at[col], z2.at[0], zr.at[col], cp).wait_recv()
        fin[...] += rz[col].astype(f32)
    for s in range(2):
        for g in range(3):
            gg_ref[s, g] = fin[wr + 16 * s : wr + 16 * s + il, g * z.uw : (g + 1) * z.uw]
    wtmp[...] = fin[0:wr, :].reshape(hl, rw, HID)
    for r in range(rw):
        go_ref[:, r * HID : (r + 1) * HID] = wtmp[:, r, :]

    for i in range(1, nmp):
        col = (m - i + nmp) % nmp
        rcopy(geo.at[col], geo.at[col], ge_s.at[0], ge_r.at[col], cp).wait_recv()
    for j, lo in enumerate(z.starts):
        first = geo[j, :, 0:128]
        if j:
            first = (first.astype(f32) + geo[j - 1, :, main:].astype(f32)).astype(bf)
        ge_ref[:, lo : lo + 128] = first
        ge_ref[:, lo + 128 : lo + main] = geo[j, :, 128:main]
    if z.edges > z.full:
        ge_ref[:, z.full :] = geo[nmp - 1, :, main : main + z.edges - z.full]
    for y in sends:
        y.wait_send()


def whole_step(z, eo, ei, gw, xc, feat, snd, rcv, msk):
    dma = pltpu.SemaphoreType.DMA
    ndp, nmp, half = z.ndp, z.nmp, z.half
    rows, rb, win = z.rows, z.rb, z.win
    vm = pltpu.VMEM
    return pl.pallas_call(
        functools.partial(kernel, z),
        out_shape=(
            jax.ShapeDtypeStruct(eo.shape, f32),
            jax.ShapeDtypeStruct(gw.shape, f32),
            jax.ShapeDtypeStruct(ei.shape, f32),
            jax.ShapeDtypeStruct((z.atoms, HID), f32),
            jax.ShapeDtypeStruct(feat.shape, bf),
        ),
        in_specs=[pl.BlockSpec(memory_space=vm)] * 8,
        out_specs=(pl.BlockSpec(memory_space=vm),) * 5,
        scratch_shapes=[
            vm((ndp, nmp, rb, HID), bf),
            vm((nmp, rows, HID), bf),
            vm((nmp, rows, HID), bf),
            vm((ndp, EFEAT, HID), bf),
            vm(xc.shape, f32),
            vm((nmp * rows, HID), f32),
            vm((z.hl, z.rw, HID), f32),
            vm((32, HID), f32),
            vm((EFEAT, HID), f32),
            vm((EFEAT, win), bf),
            vm((3, win), jnp.int32),
            vm((rows, 512), bf),
            vm((16, 512, 256), bf),
            vm((16, HID, 256), bf),
            vm((16, rows, 256), bf),
            vm((16, rows, 256), bf),
            vm((HID, rows, HID), bf),
            vm((HID, rows, HID), bf),
            vm((16, rows, 256), bf),
            vm((rows, HID), f32),
            vm((rows, 512), f32),
            vm((EFEAT, HID), f32),
            vm((EFEAT, win), f32),
            vm((ndp, nmp, rb, HID), bf),
            vm((half, nmp, rb, HID), bf),
            vm((half - 1, nmp, rb, HID), bf),
            vm((half - 1, nmp, rb, HID), bf),
            vm((nmp - 1, rb, HID), bf),
            vm((nmp, rb, HID), bf),
            vm((rb, HID), f32),
            vm((nmp, rows, HID), bf),
            vm((nmp, rows, HID), bf),
            vm((nmp, EFEAT, win), bf),
            vm((ndp, EFEAT, HID), bf),
            vm((nmp, EFEAT, HID), bf),
            vm((EFEAT, HID), bf),
            dma((nmp - 1,)),
            dma((nmp, half - 1)),
            dma((nmp + nmp * (half - 1),)),
            dma((ndp, nmp)),
            dma((nmp - 1,)), dma((nmp,)),
            dma((ndp - 1,)), dma((ndp,)),
            dma((2,)),
            dma((half,)), dma((half,)),
            dma((half - 1, nmp)), dma((half - 1, nmp)),
            dma((nmp - 1,)), dma((nmp,)),
            dma((nmp - 1,)), dma((nmp,)),
            dma((nmp - 1,)), dma((nmp,)),
            dma((ndp - 1,)), dma((ndp,)),
            dma((nmp - 1,)), dma((nmp,)),
        ],
        compiler_params=pltpu.CompilerParams(
            collective_id=0, has_side_effects=True, vmem_limit_bytes=VMEM_LIMIT
        ),
    )(eo, ei, gw, xc, feat, snd, rcv, msk)


beta_one = 0.5
beta_two = 0.5
learn_rate = 0.05
decay_rate = 0.01
epsilon = 1e-08


def adam_update(weight, gradient, first_moment, second_moment):
    first_new = beta_one * first_moment + (1.0 - beta_one) * gradient
    second_new = beta_two * second_moment + (1.0 - beta_two) * gradient * gradient
    mean_hat = first_new / (1.0 - beta_one**STEP)
    square_hat = second_new / (1.0 - beta_two**STEP)
    weight_new = weight - learn_rate * (
        mean_hat / (jnp.sqrt(square_hat) + epsilon) + decay_rate * weight
    )
    return (first_new, second_new, weight_new, weight_new.astype(bf))


def body(
    ndp, nmp,
    node_state, edge_feat, sender, receiver, edge_mask, node_mask, out_grad,
    edge_in, edge_out, gru_weight,
    edge_in_m1, edge_in_m2, edge_out_m1, edge_out_m2, gru_m1, gru_m2,
):
    z = Shape(ndp, nmp, node_state, edge_feat, edge_in, edge_out, gru_weight)
    live = node_mask.astype(f32)[:, None]
    xc = jnp.concatenate([node_state, (out_grad * live).astype(bf)], axis=1)
    g_out, g_gru, g_in, at, ge = whole_step(
        z, edge_out, edge_in, gru_weight, xc, edge_feat,
        sender[None], receiver[None], edge_mask[None],
    )
    return (
        (at[:, : z.uw] * live, at[:, z.uw : 2 * z.uw], ge.astype(f32))
        + adam_update(edge_in, g_in, edge_in_m1, edge_in_m2)
        + adam_update(edge_out, g_out, edge_out_m1, edge_out_m2)
        + adam_update(gru_weight, g_gru, gru_m1, gru_m2)
    )


def solution(mesh):
    ndp, nmp = mesh.shape["dp"], mesh.shape["mp"]
    rows, lanes, gru = P("dp", "mp"), P(None, "dp"), P(None, None, "dp", "mp")
    edge = P("dp")
    return jax.shard_map(
        functools.partial(body, ndp, nmp),
        mesh=mesh,
        in_specs=(
            rows, lanes, edge, edge, edge, edge, rows,
            lanes, rows, gru, lanes, lanes, rows, rows, gru, gru,
        ),
        out_specs=(rows, rows, lanes) + (lanes,) * 4 + (rows,) * 4 + (gru,) * 4,
        check_vma=False,
    )
```

```python
import functools

import jax
import jax.numpy as jnp
from jax import lax
from jax.experimental import pallas as pl
from jax.experimental.pallas import tpu as pltpu
from jax.sharding import PartitionSpec as P

HID = 128
EFEAT = 16
MA = 29
ME = 812
PADA = 32
STEP = 5
DXC = 4
GEU = 19
MESH = pl.DeviceIdType.MESH
VMEM_LIMIT = 60 << 20
bf = jnp.bfloat16
f32 = jnp.float32
NT = (((1,), (1,)), ((), ()))
TN = (((0,), (0,)), ((), ()))
NN = (((1,), (0,)), ((), ()))


def dot(a, b, dims):
    return lax.dot_general(a, b, dims, preferred_element_type=f32)


def roll(x, src, dst):
    shift = (dst - src) % HID
    return pltpu.roll(x, shift, 1) if shift else x


def sig(v):
    return 0.5 + 0.5 * jnp.tanh(0.5 * v)


def rcopy(src, dst, ssem, rsem, dev):
    return pltpu.make_async_remote_copy(
        src_ref=src, dst_ref=dst, send_sem=ssem, recv_sem=rsem, device_id=dev, device_id_type=MESH
    )


class Shape:
    def __init__(self, ndp, nmp, node_state, edge_feat, edge_in, edge_out, gru):
        self.ndp, self.nmp, self.half = ndp, nmp, ndp // 2
        self.atoms, self.uw = node_state.shape
        self.edges = edge_feat.shape[1]
        self.mols = self.atoms // MA
        self.nm = self.mols // nmp
        self.rows = self.nm * PADA
        self.hl, self.il, self.ew = edge_out.shape[0], gru.shape[2], edge_in.shape[1]
        self.rw = edge_out.shape[1] // HID
        self.wr = self.hl * self.rw
        self.rb = self.wr + 32
        self.per = self.nm * ME
        self.starts = [self.per * j // 128 * 128 for j in range(nmp)]
        self.bases = [ME * i // 128 * 128 for i in range(self.nm)]
        self.win = self.bases[-1] + 1024
        self.full = self.edges // 128 * 128
        shift = max(self.per * j - s for j, s in enumerate(self.starts))
        assert all(ME * i + shift + ME <= b + 1024 for i, b in enumerate(self.bases))
        assert self.starts[-1] + self.win - 128 == self.full
        assert all(b - a == self.win - 128 for a, b in zip(self.starts, self.starts[1:]))


def kernel(
    z,
    eo_ref, ei_ref, gw_ref, ns_ref, og_ref, nm_ref, feat_ref, code_ref,
    go_ref, gg_ref, gi_ref, at_ref, ge_ref,
    wall, xsb, xo, wis, stage, stage1, stage2, wtmp, stmp, itmp, featw, keyw,
    featp, featt, kron, emat, hid, hidt, slope, bmat, cmat, dsb, dpre, gacc, gfull, eights,
    grads, rc, sb, rp, ta, tb, r2a, r2b, zs, rz, fin, osb, oso, geo, gis, giz, giz_s,
    zsem, zfsem, psem, csem, rsem, hsem, xs_s, xs_r, wi_s, wi_r,
    cs, cr, ps, pr, p2s, p2r, z2, zr, os_s, os_r, ge_s, ge_r, gi_s, gi_r, gz_s, gz_r,
):
    ndp, nmp, half, nm = z.ndp, z.nmp, z.half, z.nm
    hl, il, wr, rb, rw = z.hl, z.il, z.wr, z.rb, z.rw
    d = lax.axis_index("dp")
    m = lax.axis_index("mp")
    u = d // 2
    c = d % 2
    relay = half == 4
    low = jnp.where(2 * m < nmp, 1, 0)
    side = low * m + (1 - low) * (nmp - 1 - m)
    near = [jnp.where(i <= side, i - 1, i) for i in range(1, nmp)]
    zcols = [low * i + (1 - low) * (nmp - 1 - i) for i in near]
    zp = [(d, col) for col in zcols]
    if relay:
        ux = u + 1 - 2 * (u % 2)
        uy = (u + 2) % half
        ud = (ux + 2) % half
        chips = [ud, ux, uy, u]
        px, py = (2 * ux + c, m), (2 * uy + c, m)
        pp = [px, py]
    else:
        chips = [(u + t) % half for t in range(1, half)] + [u]
        pp = [(2 * v + c, m) for v in chips[:-1]]
    ra = rb // 2
    cp = (2 * u + (1 - c), m)
    dpp = [((d + i) % ndp, m) for i in range(1, ndp)]
    bar = pltpu.get_barrier_semaphore()
    for p in zp + dpp:
        pl.semaphore_signal(bar, inc=1, device_id=p, device_id_type=MESH)
    lane = lax.broadcasted_iota(jnp.int32, (1, HID), 1)

    def two_up(v):
        return jnp.where(lane < 64, v[: z.rows // 2], pltpu.roll(v[z.rows // 2 :], 64, 1))

    def one_up(v):
        return jnp.concatenate([v, pltpu.roll(v, 64, 1)], axis=0)

    for r in range(rw):
        wtmp[:, r, :] = eo_ref[:, r * HID : (r + 1) * HID]
    wall[d, m, 0:wr, :] = wtmp[...].reshape(wr, HID).astype(bf)
    stmp[...] = jnp.zeros(stmp.shape, f32)
    for s in range(2):
        for g in range(3):
            stmp[16 * s : 16 * s + il, g * z.uw : (g + 1) * z.uw] = gw_ref[s, g]
    wall[d, m, wr:rb, :] = stmp[...].astype(bf)
    itmp[...] = jnp.zeros(itmp.shape, f32)
    itmp[:, 0 : z.ew] = ei_ref[...]
    wis[d] = pltpu.roll(itmp[...], d * z.ew, 1).astype(bf)
    stage[...] = jnp.zeros(stage.shape, f32)
    stage[0 : z.uw, 0 : z.atoms] = ns_ref[...].astype(f32)
    stage[z.uw : 2 * z.uw, 0 : z.atoms] = og_ref[...] * nm_ref[...]
    stage1[...] = stage[...].T
    stage2[...] = jnp.zeros(stage2.shape, f32)
    for i in range(z.mols):
        stage2[i * PADA : i * PADA + MA, :] = stage1[i * MA : (i + 1) * MA, :]
    for j in range(nmp):
        xsb[j] = two_up(stage2[j * z.rows : (j + 1) * z.rows, :]).astype(bf)
    pl.semaphore_wait(bar, len(zp + dpp))

    sends = []
    maybe = []

    def go(*copies):
        for x in copies:
            x.start()
        sends.extend(copies)

    def go_if(ok, x):
        pl.when(ok)(x.start)
        maybe.append((ok, x))

    def inside(col):
        return (col >= 0) & (col < nmp)

    def apart(col, n):
        return (col - m == n) | (col - m == -n)

    for i, p in enumerate(dpp):
        go(rcopy(wis.at[d], wis.at[d], wi_s.at[i], wi_r.at[d], p))

    def push(n, row, col, plane):
        src = wall.at[row, col]
        if plane:
            for t, p in enumerate(pp):
                go(rcopy(src, src, psem.at[n, t], rsem.at[row, col], p))
        go(rcopy(src, src, csem.at[n if plane else nmp + n], rsem.at[row, col], cp))

    def arrived(row, col):
        here = wall.at[row, col]
        rcopy(here, here, zsem.at[0], rsem.at[row, col], cp).wait_recv()

    def along_z(i):
        col = zcols[i - 1]
        arrived(d, col)
        if i < 3:
            beyond = 2 * m - col
            src = wall.at[d, col]
            go_if(inside(beyond) & apart(col, 1), rcopy(src, src, zfsem.at[i - 1], rsem.at[d, col], (d, beyond)))
        push(i, d, col, True)

    def in_plane(n):
        col = ([m] + zcols)[n]
        if not relay:
            for t in range(1, half):
                row = 2 * ((u - t + half) % half) + c
                arrived(row, col)
                push(n * (half - 1) + t - 1, row, col, False)
            return
        for t, (row, dev, lo) in enumerate(((2 * ux + c, py, ra), (2 * uy + c, px, 0))):
            arrived(row, col)
            part = wall.at[row, col, pl.ds(lo, ra), :]
            go(rcopy(part, part, psem.at[n, 2 + t], hsem.at[t, col], dev))
            push(3 * n + t, row, col, False)

    def from_diagonal(n):
        if relay:
            col = ([m] + zcols)[n]
            row = 2 * ud + c
            for t, lo in enumerate((ra, 0)):
                part = wall.at[row, col, pl.ds(lo, ra), :]
                rcopy(part, part, zsem.at[0], hsem.at[t, col], cp).wait_recv()
            push(3 * n + 2, row, col, False)

    for i, col in enumerate(zcols):
        go_if(
            (col - m != 2) & (col - m != -2),
            rcopy(wall.at[d, m], wall.at[d, m], zsem.at[i], rsem.at[d, m], (d, col)),
        )
    push(0, d, m, True)
    xo[m] = xsb[m]

    start = pl.multiple_of(z.per * m // 128 * 128, 128)
    main = z.win - 128
    featw[:, 0:main] = feat_ref[:, pl.ds(start, main)]
    keyw[0:1, 0:main] = code_ref[:, pl.ds(start, main)]

    @pl.when(m < nmp - 1)
    def _():
        after = pl.multiple_of(start + main, 128)
        featw[:, main:] = feat_ref[:, pl.ds(after, 128)]
        keyw[0:1, main:] = code_ref[:, pl.ds(after, 128)]

    @pl.when(m == nmp - 1)
    def _():
        featw[:, main:] = jnp.zeros((EFEAT, 128), bf)
        keyw[0:1, main:] = jnp.zeros((1, 128), jnp.int32)
        tail = z.edges - z.full
        if tail:
            featw[:, main : main + tail] = feat_ref[:, z.full :]
            keyw[0:1, main : main + tail] = code_ref[:, z.full :]

    code = keyw[0:1, :]
    place = lax.broadcasted_iota(jnp.int32, (1, z.win), 1) + (start - z.per * m)
    valid = (place >= 0) & (place < z.per)
    mol = jnp.zeros((1, z.win), jnp.int32)
    for i in range(1, nm):
        mol = mol + jnp.where(place >= ME * i, PADA, 0)
    live = lax.shift_right_logical(code, 10)
    code = code - live * 1024
    from_ = lax.shift_right_logical(code, 5)
    keyw[0:1, :] = jnp.where(valid & (live == 1), from_, -1)
    keyw[1:2, :] = jnp.where(valid, code - from_ * 32 + mol, -1)

    wio = lax.broadcasted_iota(jnp.int32, (PADA, 1024), 0)

    def permute(i):
        b = z.bases[i]
        st = wio == keyw[0:1, b : b + 1024]
        rt = jnp.where(wio + PADA * i == keyw[1:2, b : b + 1024], 1.0, 0.0).astype(bf)
        ff = featw[:, b : b + 1024].astype(f32)
        for q in range(4):
            zz = jnp.concatenate(
                [jnp.where(st, ff[f : f + 1, :], 0.0).astype(bf) for f in range(4 * q, 4 * q + 4)], axis=0
            )
            featp[i * PADA : (i + 1) * PADA, q * 128 : (q + 1) * 128] = dot(rt, zz, NT).astype(bf)

    for i in range(nm):
        permute(i)

    for i in range(1, ndp):
        row = (d - i + ndp) % ndp
        rcopy(wis.at[row], wis.at[row], wi_s.at[0], wi_r.at[row], cp).wait_recv()
    w_in = wis[...].astype(f32).sum(axis=0).astype(bf)
    delta = (
        lax.broadcasted_iota(jnp.int32, (PADA, 256), 0)
        == lax.broadcasted_iota(jnp.int32, (PADA, 256), 1) % PADA
    )

    @pl.loop(0, 16, unroll=4)
    def _(k):
        e = jnp.where(
            lax.broadcasted_iota(jnp.int32, (HID, 256), 0)
            == k * 8 + lax.broadcasted_iota(jnp.int32, (HID, 256), 1) // PADA,
            1.0,
            0.0,
        ).astype(bf)
        emat[k] = e
        wexp = dot(w_in, e, NN)
        for f in range(EFEAT):
            kron[k, f * PADA : (f + 1) * PADA, :] = jnp.where(delta, wexp[f : f + 1, :], 0.0).astype(bf)

    along_z(1)
    for i, p in enumerate(zp):
        go(rcopy(xsb.at[p[1]], xo.at[m], xs_s.at[i], xs_r.at[m], p))
    fp = featp[...]
    featt[...] = fp.T

    def hidden(lo):
        @pl.loop(lo, lo + 8, unroll=4)
        def _(k):
            p = dot(fp, kron[k], NN)
            s = sig(p)
            h = p * s
            hid[k] = h.astype(bf)
            hidt[k] = h.T.astype(bf)
            slope[k] = (s + h - h * s).astype(bf)

    hidden(0)
    in_plane(0)
    along_z(2)
    hidden(8)

    in_plane(1)
    from_diagonal(0)
    for i in range(3, nmp):
        along_z(i)
    for n in range(2, nmp):
        in_plane(n)
        from_diagonal(n - 1)
    from_diagonal(nmp - 1)

    for col in zcols:
        rcopy(xo.at[col], xo.at[col], xs_s.at[0], xs_r.at[col], cp).wait_recv()
    xf = jnp.zeros((z.rows, HID), f32)
    cf = jnp.zeros((z.rows, HID), f32)
    for j in range(nmp):
        sl = one_up(xo[j].astype(f32))
        here = (lane >= z.uw * j) & (lane < z.uw * (j + 1))
        xf = jnp.where(here, roll(sl, 0, z.uw * j), xf)
        cf = jnp.where(here, roll(sl, z.uw, z.uw * j), cf)
    x = xf.astype(bf)

    def rows_of(row, qs):
        return jnp.concatenate(
            [wall[row, j, q * rw : (q + 1) * rw, :] for q in qs for j in range(nmp)], axis=0
        )

    def make_b(row):
        for q in range(hl // 2):
            o = dot(x, rows_of(row, (2 * q, 2 * q + 1)), NT).astype(bf)
            bmat[row * hl + 2 * q] = o[:, :HID]
            bmat[row * hl + 2 * q + 1] = o[:, HID:]

    @pl.loop(0, half, unroll=2)
    def _(t):
        make_b(2 * t + c)

    for col in [m] + zcols:
        for t in range(half):
            arrived(2 * t + (1 - c), col)

    @pl.loop(0, half, unroll=2)
    def _(t):
        make_b(2 * t + (1 - c))

    sums = []
    for i in range(nm):
        hm = jnp.concatenate([hid[k, i * PADA : (i + 1) * PADA, :] for k in range(16)], axis=1)
        sums.append(dot(hm, bmat[:, i * PADA : (i + 1) * PADA, :].reshape(PADA * HID, HID), NN))
    summed = jnp.concatenate(sums, axis=0).astype(bf)

    def gru_rows(s, j):
        if il == 16:
            return jnp.concatenate([wall[k, j, wr + 16 * s : wr + 16 * s + 16, :] for k in range(ndp)], axis=0)
        for k in range(ndp):
            gfull[k * il : (k + 1) * il, 0:HID] = wall[k, j, wr + 16 * s : wr + 16 * s + 16, :].astype(f32)[:il]
        return gfull[0:HID, 0:HID].astype(bf)

    wg = [[gru_rows(s, j) for j in range(nmp)] for s in range(2)]

    def gates(a, s):
        outs = [dot(a, wg[s][j], NN) for j in range(nmp)]
        res = []
        for g in range(3):
            t = None
            for j in range(nmp):
                y = roll(outs[j], z.uw * g, z.uw * j)
                here = (lane >= z.uw * j) & (lane < z.uw * (j + 1))
                t = y if t is None else jnp.where(here, y, t)
            res.append(t)
        return res

    gi = gates(summed, 0)
    gs = gates(x, 1)
    reset = sig(gi[0] + gs[0])
    update = sig(gi[1] + gs[1])
    cand = jnp.tanh(gi[2] + reset * gs[2])
    ostate = (1.0 - update) * cand + update * xf
    dc = cf * (1.0 - update) * (1.0 - cand * cand)
    du = cf * (xf - cand) * update * (1.0 - update)
    dr = dc * gs[2] * reset * (1.0 - reset)

    def pack(gl, j):
        t = jnp.zeros((z.rows, HID), f32)
        for g in range(3):
            here = (lane >= z.uw * g) & (lane < z.uw * (g + 1))
            t = jnp.where(here, roll(gl[g], z.uw * j, z.uw * g), t)
        return t.astype(bf)

    al = [pack([dr, du, dc], j) for j in range(nmp)]
    bl = [pack([dr, du, dc * reset], j) for j in range(nmp)]
    ds = dot(jnp.concatenate(al, axis=1), jnp.concatenate(wg[0], axis=1), NT).astype(bf)
    gfull[:, HID : 2 * HID] = cf * update
    gfull[:, 0:HID] = dot(jnp.concatenate(bl, axis=1), jnp.concatenate(wg[1], axis=1), NT)
    for j in range(nmp):
        for s, (l, r) in enumerate(((summed, al[j]), (x, bl[j]))):
            gg = dot(l, r, TN)
            for k in range(ndp):
                part = gg[k * il : (k + 1) * il]
                if il < 16:
                    part = jnp.concatenate([part, jnp.zeros((16 - il, HID), f32)], axis=0)
                grads[k, j, wr + 16 * s : wr + 16 * s + 16, :] = part.astype(bf)

    dsb[...] = jnp.zeros(dsb.shape, bf)
    for i in range(nm):
        dsb[i * PADA : (i + 1) * PADA, i * HID : (i + 1) * HID] = ds[i * PADA : (i + 1) * PADA]

    @pl.loop(0, 16, unroll=8)
    def _(k):
        for p in range(nm // 2):
            o = dot(hidt[k], dsb[:, p * 256 : (p + 1) * 256], NN).astype(bf)
            for i in range(2):
                at = (2 * p + i) * PADA
                cmat[pl.ds(k * 8, 8), at : at + PADA, :] = o[:, i * HID : (i + 1) * HID].reshape(8, PADA, HID)

    def grad_w(row):
        for q in range(hl):
            o = dot(cmat[row * hl + q], x, TN).astype(bf)
            for j in range(nmp):
                grads[row, j, q * rw : (q + 1) * rw, :] = o[rw * j : rw * (j + 1)]

    cols = zcols[::-1] + [m]

    def core_arrived(t):
        rcopy(rc.at[t], rc.at[t], cs.at[t], cr.at[t], cp).wait_recv()
        if t == half - 1:
            return
        row = 2 * chips[t] + c
        for i, col in enumerate(cols):
            sb[t, i] = (grads[row, col].astype(f32) + rc[t, col].astype(f32)).astype(bf)
            if not relay:
                go(rcopy(sb.at[t, i], rp.at[t, col], ps.at[t, i], pr.at[t, col], pp[t]))
                continue
            if t < 2:
                go(rcopy(sb.at[t, i, pl.ds(0, ra), :], rp.at[t, col, pl.ds(0, ra), :], ps.at[t, i], pr.at[t, col], px))
            if t != 1:
                k = t // 2 + 2
                go(rcopy(sb.at[t, i, pl.ds(ra, ra), :], rp.at[k % 3, col, pl.ds(ra, ra), :], ps.at[k, i], pr.at[k, col], py))

    for t in range(half):
        grad_w(2 * chips[t] + (1 - c))
        go(rcopy(grads.at[2 * chips[t] + (1 - c)], rc.at[t], cs.at[t], cr.at[t], cp))
        grad_w(2 * chips[t] + c)
        if t > 0:
            core_arrived(t - 1)
    core_arrived(half - 1)

    def part_arrived(slot, lo, col, k):
        here = rp.at[slot, col, pl.ds(lo, ra), :]
        rcopy(here, here, zsem.at[0], pr.at[k, col], cp).wait_recv()
        return rp[slot, col, lo : lo + ra, :].astype(f32)

    def turn(i):
        if not relay:
            return
        col = cols[i]
        ta[i] = (sb[2, i, 0:ra, :].astype(f32) + part_arrived(0, 0, col, 0)).astype(bf)
        go(rcopy(ta.at[i], r2a.at[col], p2s.at[0, i], p2r.at[0, col], py))
        tb[i] = (sb[1, i, ra:, :].astype(f32) + part_arrived(2, ra, col, 2)).astype(bf)
        go(rcopy(tb.at[i], r2b.at[col], p2s.at[1, i], p2r.at[1, col], px))

    def to_z(i):
        col = cols[i]
        q = grads[d, col].astype(f32) + rc[half - 1, col].astype(f32)
        if relay:
            rcopy(r2a.at[col], r2a.at[col], zsem.at[0], p2r.at[0, col], cp).wait_recv()
            rcopy(r2b.at[col], r2b.at[col], zsem.at[0], p2r.at[1, col], cp).wait_recv()
            qa = q[:ra] + part_arrived(1, 0, col, 1) + r2a[col].astype(f32)
            qb = q[ra:] + part_arrived(0, ra, col, 3) + r2b[col].astype(f32)
            q = jnp.concatenate([qa, qb], axis=0)
        else:
            for t in range(half - 1):
                here = rp.at[t, col]
                rcopy(here, here, zsem.at[0], pr.at[t, col], cp).wait_recv()
                q = q + rp[t, col].astype(f32)
        if i < nmp - 1:
            zs[i] = q.astype(bf)
            go(rcopy(zs.at[i], rz.at[m], z2.at[i], zr.at[m], (d, col)))
        else:
            fin[...] = q

    for i in range(nm):
        dm = ds[i * PADA : (i + 1) * PADA]
        for k in range(16):
            o = dot(dm, bmat[k * 8 : (k + 1) * 8, i * PADA : (i + 1) * PADA, :].reshape(256, HID), NT)
            dpre[k, i * PADA : (i + 1) * PADA, :] = (
                o * slope[k, i * PADA : (i + 1) * PADA, :].astype(f32)
            ).astype(bf)
    turn(0)
    gb = dot(
        jnp.concatenate([dpre[k] for k in range(16)], axis=1),
        jnp.concatenate([kron[k] for k in range(16)], axis=1),
        NT,
    ).astype(bf)

    def by_eight(v, mask):
        v = jnp.where(mask[None], v.reshape(EFEAT, PADA, -1), 0.0)
        return (v[:, 0:8] + v[:, 8:16] + v[:, 16:24] + v[:, 24:32]).reshape(EFEAT * 8, -1).astype(bf)

    @pl.loop(0, 16, unroll=16)
    def _(k):
        eights[k] = by_eight(dot(featt[...], dpre[k], NN), delta)

    gin = dot(
        jnp.concatenate([eights[k] for k in range(16)], axis=1),
        jnp.concatenate([emat[k] for k in range(16)], axis=1),
        NT,
    )
    gis[d] = gin.reshape(EFEAT, 8, HID).sum(axis=1).astype(bf)
    for i, p in enumerate(dpp):
        go(rcopy(gis.at[d], gis.at[d], gi_s.at[i], gi_r.at[d], p))

    turn(1)
    eight = jnp.where(
        lax.broadcasted_iota(jnp.int32, (EFEAT, EFEAT * 8), 0)
        == lax.broadcasted_iota(jnp.int32, (EFEAT, EFEAT * 8), 1) // 8,
        1.0,
        0.0,
    ).astype(bf)

    featt[...] = gb.T

    def edges_back(n, count):
        at = pl.ds(pl.multiple_of(n * 256, 256), count)
        all_rows = lax.broadcasted_iota(jnp.int32, (z.rows, count), 0)
        rt = jnp.where(all_rows == keyw[1:2, at], 1.0, 0.0).astype(bf)
        eights[n, :, 0:count] = by_eight(dot(featt[...], rt, NN), wio[:, :count] == keyw[0:1, at])

    pairs = z.win // 256
    pl.loop(0, pairs, unroll=GEU)(lambda n: edges_back(n, 256))
    if z.win % 256:
        edges_back(pairs, 128)
    for n in range(pairs):
        geo[m, :, n * 256 : (n + 1) * 256] = dot(eight, eights[n], NN).astype(bf)
    if z.win % 256:
        geo[m, :, pairs * 256 :] = dot(eight, eights[pairs, :, 0:128], NN).astype(bf)

    def edges_on(s):
        for way in (0, 1):
            col = m - s if way == 0 else m + s
            nxt = m + 1 if way == 0 else m - 1
            src = geo.at[col]
            if s:
                pl.when(inside(col))(rcopy(src, src, zsem.at[0], ge_r.at[col], cp).wait_recv)
            if s < nmp - 1:
                go_if(inside(col) & inside(nxt), rcopy(src, src, ge_s.at[s, way], ge_r.at[col], (d, nxt)))

    edges_on(0)
    turn(2)
    to_z(0)

    gacc[...] = jnp.zeros(gacc.shape, f32)
    step = min(DXC, hl)

    @pl.loop(0, ndp, unroll=2)
    def _(row):
        for q in range(0, hl, step):
            qs = range(q, q + step)
            cc = jnp.concatenate([cmat[row * hl + k] for k in qs], axis=1)
            gacc[...] += dot(cc, rows_of(row, qs), NN)

    gfin = gacc[...] + gfull[:, 0:HID] + gfull[:, HID : 2 * HID]
    for j in range(nmp):
        a = roll(ostate, z.uw * j, 0)
        b = roll(gfin, z.uw * j, z.uw)
        osb[j] = two_up(jnp.where(lane < z.uw, a, b)).astype(bf)
    for i, p in enumerate(zp):
        go(rcopy(osb.at[p[1]], oso.at[m], os_s.at[i], os_r.at[m], p))
    oso[m] = osb[m]
    turn(3)
    to_z(1)
    edges_on(1)

    gi_sum = gis[d].astype(f32)
    for i in range(1, ndp):
        row = (d - i + ndp) % ndp
        rcopy(gis.at[row], gis.at[row], gi_s.at[0], gi_r.at[row], cp).wait_recv()
        gi_sum = gi_sum + gis[row].astype(f32)
    giz_s[...] = gi_sum.astype(bf)
    for i, p in enumerate(zp):
        go(rcopy(giz_s, giz.at[m], gz_s.at[i], gz_r.at[m], p))
    to_z(2)
    edges_on(2)
    to_z(3)

    for col in zcols:
        rcopy(oso.at[col], oso.at[col], os_s.at[0], os_r.at[col], cp).wait_recv()
    for j in range(nmp):
        stage2[j * z.rows : (j + 1) * z.rows, :] = one_up(oso[j].astype(f32))
    for i in range(z.mols):
        stage1[i * MA : (i + 1) * MA, :] = stage2[i * PADA : i * PADA + MA, :]
    stage[...] = stage1[...].T
    at_ref[0 : z.uw, :] = stage[0 : z.uw, 0 : z.atoms] * nm_ref[...]
    at_ref[z.uw : 2 * z.uw, :] = stage[z.uw : 2 * z.uw, 0 : z.atoms]

    for col in zcols:
        rcopy(giz.at[col], giz.at[col], gz_s.at[0], gz_r.at[col], cp).wait_recv()
        gi_sum = gi_sum + giz[col].astype(f32)
    gi_ref[...] = pltpu.roll(gi_sum, HID - d * z.ew, 1)[:, 0 : z.ew]
    for col in zcols:
        rcopy(rz.at[col], rz.at[col], z2.at[0], zr.at[col], cp).wait_recv()
        fin[...] += rz[col].astype(f32)
    for s in range(2):
        for g in range(3):
            gg_ref[s, g] = fin[wr + 16 * s : wr + 16 * s + il, g * z.uw : (g + 1) * z.uw]
    wtmp[...] = fin[0:wr, :].reshape(hl, rw, HID)
    for r in range(rw):
        go_ref[:, r * HID : (r + 1) * HID] = wtmp[:, r, :]

    edges_on(3)
    for j, lo in enumerate(z.starts):
        first = geo[j, :, 0:128]
        if j:
            first = (first.astype(f32) + geo[j - 1, :, main:].astype(f32)).astype(bf)
        ge_ref[:, lo : lo + 128] = first
        ge_ref[:, lo + 128 : lo + main] = geo[j, :, 128:main]
    if z.edges > z.full:
        ge_ref[:, z.full :] = geo[nmp - 1, :, main : main + z.edges - z.full]
    for y in sends:
        y.wait_send()
    for ok, y in maybe:
        pl.when(ok)(y.wait_send)


def whole_step(z, eo, ei, gw, ns, og, live, feat, code):
    dma = pltpu.SemaphoreType.DMA
    ndp, nmp, half = z.ndp, z.nmp, z.half
    rows, rb, win = z.rows, z.rb, z.win
    vm = pltpu.VMEM
    ra = rb // 2
    relay = half == 4
    return pl.pallas_call(
        functools.partial(kernel, z),
        out_shape=(
            jax.ShapeDtypeStruct(eo.shape, f32),
            jax.ShapeDtypeStruct(gw.shape, f32),
            jax.ShapeDtypeStruct(ei.shape, f32),
            jax.ShapeDtypeStruct((2 * z.uw, z.atoms), f32),
            jax.ShapeDtypeStruct(feat.shape, bf),
        ),
        in_specs=[pl.BlockSpec(memory_space=vm)] * 8,
        out_specs=(pl.BlockSpec(memory_space=vm),) * 5,
        scratch_shapes=[
            vm((ndp, nmp, rb, HID), bf),
            vm((nmp, rows // 2, HID), bf),
            vm((nmp, rows // 2, HID), bf),
            vm((ndp, EFEAT, HID), bf),
            vm((HID, -(-z.atoms // 128) * 128), f32),
            vm((-(-z.atoms // 128) * 128, HID), f32),
            vm((nmp * rows, HID), f32),
            vm((z.hl, z.rw, HID), f32),
            vm((32, HID), f32),
            vm((EFEAT, HID), f32),
            vm((EFEAT, win), bf),
            vm((2, win), jnp.int32),
            vm((rows, 512), bf),
            vm((512, rows), bf),
            vm((16, 512, 256), bf),
            vm((16, HID, 256), bf),
            vm((16, rows, 256), bf),
            vm((16, 256, rows), bf),
            vm((16, rows, 256), bf),
            vm((HID, rows, HID), bf),
            vm((HID, rows, HID), bf),
            vm((rows, z.nm * HID), bf),
            vm((16, rows, 256), bf),
            vm((rows, HID), f32),
            vm((rows, 512), f32),
            vm((max(16, -(-win // 256)), EFEAT * 8, 256), bf),
            vm((ndp, nmp, rb, HID), bf),
            vm((half, nmp, rb, HID), bf),
            vm((half - 1, nmp, rb, HID), bf),
            vm((half - 1, nmp, rb, HID), bf),
            vm((nmp, ra, HID), bf),
            vm((nmp, ra, HID), bf),
            vm((nmp, ra, HID), bf),
            vm((nmp, ra, HID), bf),
            vm((nmp - 1, rb, HID), bf),
            vm((nmp, rb, HID), bf),
            vm((rb, HID), f32),
            vm((nmp, rows // 2, HID), bf),
            vm((nmp, rows // 2, HID), bf),
            vm((nmp, EFEAT, win), bf),
            vm((ndp, EFEAT, HID), bf),
            vm((nmp, EFEAT, HID), bf),
            vm((EFEAT, HID), bf),
            dma((nmp - 1,)),
            dma((2,)),
            dma((nmp, max(half - 1, 4))),
            dma((nmp + nmp * (half - 1),)),
            dma((ndp, nmp)),
            dma((2, nmp)),
            dma((nmp - 1,)), dma((nmp,)),
            dma((ndp - 1,)), dma((ndp,)),
            dma((half,)), dma((half,)),
            dma((max(half - 1, 4), nmp)), dma((max(half - 1, 4), nmp)),
            dma((2, nmp)), dma((2, nmp)),
            dma((nmp - 1,)), dma((nmp,)),
            dma((nmp - 1,)), dma((nmp,)),
            dma((nmp - 1, 2)), dma((nmp,)),
            dma((ndp - 1,)), dma((ndp,)),
            dma((nmp - 1,)), dma((nmp,)),
        ],
        compiler_params=pltpu.CompilerParams(
            collective_id=0, has_side_effects=True, vmem_limit_bytes=VMEM_LIMIT
        ),
    )(eo, ei, gw, ns, og, live, feat, code)


beta_one = 0.5
beta_two = 0.5
learn_rate = 0.05
decay_rate = 0.01
epsilon = 1e-08


def adam_update(weight, gradient, first_moment, second_moment):
    first_new = beta_one * first_moment + (1.0 - beta_one) * gradient
    second_new = beta_two * second_moment + (1.0 - beta_two) * gradient * gradient
    mean_hat = first_new / (1.0 - beta_one**STEP)
    square_hat = second_new / (1.0 - beta_two**STEP)
    weight_new = weight - learn_rate * (
        mean_hat / (jnp.sqrt(square_hat) + epsilon) + decay_rate * weight
    )
    return (first_new, second_new, weight_new, weight_new.astype(bf))


def body(
    ndp, nmp,
    node_state, edge_feat, sender, receiver, edge_mask, node_mask, out_grad,
    edge_in, edge_out, gru_weight,
    edge_in_m1, edge_in_m2, edge_out_m1, edge_out_m2, gru_m1, gru_m2,
):
    z = Shape(ndp, nmp, node_state, edge_feat, edge_in, edge_out, gru_weight)
    code = (edge_mask * 1024 + sender * 32 + receiver)[None]
    g_out, g_gru, g_in, at, ge = whole_step(
        z, edge_out, edge_in, gru_weight, node_state.T, out_grad.T,
        node_mask.astype(f32)[None], edge_feat, code,
    )
    return (
        (at[: z.uw].T, at[z.uw :].T, ge.astype(f32))
        + adam_update(edge_in, g_in, edge_in_m1, edge_in_m2)
        + adam_update(edge_out, g_out, edge_out_m1, edge_out_m2)
        + adam_update(gru_weight, g_gru, gru_m1, gru_m2)
    )


def solution(mesh):
    ndp, nmp = mesh.shape["dp"], mesh.shape["mp"]
    rows, lanes, gru = P("dp", "mp"), P(None, "dp"), P(None, None, "dp", "mp")
    edge = P("dp")
    return jax.shard_map(
        functools.partial(body, ndp, nmp),
        mesh=mesh,
        in_specs=(
            rows, lanes, edge, edge, edge, edge, rows,
            lanes, rows, gru, lanes, lanes, rows, rows, gru, gru,
        ),
        out_specs=(rows, rows, lanes) + (lanes,) * 4 + (rows,) * 4 + (gru,) * 4,
        check_vma=False,
    )
```

```python
import functools

import jax
import jax.numpy as jnp
from jax import lax
from jax.experimental import pallas as pl
from jax.experimental.pallas import tpu as pltpu
from jax.sharding import PartitionSpec as P

HID = 128
EFEAT = 16
MA = 29
ME = 812
PADA = 32
STEP = 5
DXC = 4
MESH = pl.DeviceIdType.MESH
VMEM_LIMIT = 60 << 20
bf = jnp.bfloat16
f32 = jnp.float32
NT = (((1,), (1,)), ((), ()))
TN = (((0,), (0,)), ((), ()))
NN = (((1,), (0,)), ((), ()))


def dot(a, b, dims):
    return lax.dot_general(a, b, dims, preferred_element_type=f32)


def roll(x, src, dst):
    shift = (dst - src) % HID
    return pltpu.roll(x, shift, 1) if shift else x


def sig(v):
    return 0.5 + 0.5 * jnp.tanh(0.5 * v)


def rcopy(src, dst, ssem, rsem, dev):
    return pltpu.make_async_remote_copy(
        src_ref=src, dst_ref=dst, send_sem=ssem, recv_sem=rsem, device_id=dev, device_id_type=MESH
    )


class Shape:
    def __init__(self, ndp, nmp, node_state, edge_feat, edge_in, edge_out, gru):
        self.ndp, self.nmp, self.half = ndp, nmp, ndp // 2
        self.atoms, self.uw = node_state.shape
        self.edges = edge_feat.shape[1]
        self.mols = self.atoms // MA
        self.nm = self.mols // nmp
        self.rows = self.nm * PADA
        self.hl, self.il, self.ew = edge_out.shape[0], gru.shape[2], edge_in.shape[1]
        self.rw = edge_out.shape[1] // HID
        self.wr = self.hl * self.rw
        self.rb = self.wr + 32
        self.per = self.nm * ME
        self.starts = [self.per * j // 128 * 128 for j in range(nmp)]
        self.bases = [ME * i // 128 * 128 for i in range(self.nm)]
        self.win = self.bases[-1] + 1024
        self.full = self.edges // 128 * 128
        shift = max(self.per * j - s for j, s in enumerate(self.starts))
        assert all(ME * i + shift + ME <= b + 1024 for i, b in enumerate(self.bases))
        assert self.starts[-1] + self.win - 128 == self.full
        assert all(b - a == self.win - 128 for a, b in zip(self.starts, self.starts[1:]))


def kernel(
    z,
    eo_ref, ei_ref, gw_ref, ns_ref, og_ref, nm_ref, feat_hbm, snd_ref, rcv_ref, msk_ref,
    go_ref, gg_ref, gi_ref, at_ref, ge_ref,
    wall, xsb, xo, wis, stage, stage1, stage2, wtmp, stmp, itmp, nmrow, feat_ref, featw, keyw,
    featp, featt, gbt, kron, emat, hid, hidt, slope, bmat, cmat, dsb, dpre, gacc, gfull, eights,
    grads, rc, sb, rp, ta, tb, r2a, r2b, zs, rz, fin, osb, oso, geo, gis, giz, giz_s,
    fsem, zsem, zfsem, psem, csem, rsem, hsem, xs_s, xs_r, wi_s, wi_r,
    cs, cr, ps, pr, p2s, p2r, z2, zr, os_s, os_r, ge_s, ge_r, gi_s, gi_r, gz_s, gz_r,
):
    ndp, nmp, half, nm = z.ndp, z.nmp, z.half, z.nm
    hl, il, wr, rb, rw = z.hl, z.il, z.wr, z.rb, z.rw
    d = lax.axis_index("dp")
    m = lax.axis_index("mp")
    u = d // 2
    c = d % 2
    relay = half == 4
    low = jnp.where(2 * m < nmp, 1, 0)
    side = low * m + (1 - low) * (nmp - 1 - m)
    near = [jnp.where(i <= side, i - 1, i) for i in range(1, nmp)]
    zcols = [low * i + (1 - low) * (nmp - 1 - i) for i in near]
    zp = [(d, col) for col in zcols]
    if relay:
        ux = u + 1 - 2 * (u % 2)
        uy = (u + 2) % half
        ud = (ux + 2) % half
        chips = [ud, ux, uy, u]
        px, py = (2 * ux + c, m), (2 * uy + c, m)
        pp = [px, py]
    else:
        chips = [(u + t) % half for t in range(1, half)] + [u]
        pp = [(2 * v + c, m) for v in chips[:-1]]
    ra = rb // 2
    cp = (2 * u + (1 - c), m)
    dpp = [((d + i) % ndp, m) for i in range(1, ndp)]
    bar = pltpu.get_barrier_semaphore()
    feat_in = pltpu.make_async_copy(feat_hbm, feat_ref, fsem)
    feat_in.start()
    for p in zp + dpp:
        pl.semaphore_signal(bar, inc=1, device_id=p, device_id_type=MESH)
    lane = lax.broadcasted_iota(jnp.int32, (1, HID), 1)

    def two_up(v):
        return jnp.where(lane < 64, v[: z.rows // 2], pltpu.roll(v[z.rows // 2 :], 64, 1))

    def one_up(v):
        return jnp.concatenate([v, pltpu.roll(v, 64, 1)], axis=0)

    for r in range(rw):
        wtmp[:, r, :] = eo_ref[:, r * HID : (r + 1) * HID]
    wall[d, m, 0:wr, :] = wtmp[...].reshape(wr, HID).astype(bf)
    stmp[...] = jnp.zeros(stmp.shape, f32)
    for s in range(2):
        for g in range(3):
            stmp[16 * s : 16 * s + il, g * z.uw : (g + 1) * z.uw] = gw_ref[s, g]
    wall[d, m, wr:rb, :] = stmp[...].astype(bf)
    itmp[...] = jnp.zeros(itmp.shape, f32)
    itmp[:, 0 : z.ew] = ei_ref[...]
    wis[d] = pltpu.roll(itmp[...], d * z.ew, 1).astype(bf)
    stage[...] = jnp.zeros(stage.shape, f32)
    stage[0 : z.uw, 0 : z.atoms] = ns_ref[...].astype(f32)
    nmrow[0, :] = nm_ref[...].astype(f32)
    stage[z.uw : 2 * z.uw, 0 : z.atoms] = og_ref[...] * nmrow[...]
    stage1[...] = stage[...].T
    stage2[...] = jnp.zeros(stage2.shape, f32)
    for i in range(z.mols):
        stage2[i * PADA : i * PADA + MA, :] = stage1[i * MA : (i + 1) * MA, :]
    for j in range(nmp):
        xsb[j] = two_up(stage2[j * z.rows : (j + 1) * z.rows, :]).astype(bf)
    pl.semaphore_wait(bar, len(zp + dpp))

    sends = []
    maybe = []

    def go(*copies):
        for x in copies:
            x.start()
        sends.extend(copies)

    def go_if(ok, x):
        pl.when(ok)(x.start)
        maybe.append((ok, x))

    def inside(col):
        return (col >= 0) & (col < nmp)

    def apart(col, n):
        return (col - m == n) | (col - m == -n)

    for i, p in enumerate(dpp):
        go(rcopy(wis.at[d], wis.at[d], wi_s.at[i], wi_r.at[d], p))

    def push(n, row, col, plane):
        src = wall.at[row, col]
        if plane:
            for t, p in enumerate(pp):
                go(rcopy(src, src, psem.at[n, t], rsem.at[row, col], p))
        go(rcopy(src, src, csem.at[n if plane else nmp + n], rsem.at[row, col], cp))

    def arrived(row, col):
        here = wall.at[row, col]
        rcopy(here, here, zsem.at[0], rsem.at[row, col], cp).wait_recv()

    def along_z(i):
        col = zcols[i - 1]
        arrived(d, col)
        if i < 3:
            beyond = 2 * m - col
            src = wall.at[d, col]
            go_if(inside(beyond) & apart(col, 1), rcopy(src, src, zfsem.at[i - 1], rsem.at[d, col], (d, beyond)))
        push(i, d, col, True)

    def in_plane(n):
        col = ([m] + zcols)[n]
        if not relay:
            for t in range(1, half):
                row = 2 * ((u - t + half) % half) + c
                arrived(row, col)
                push(n * (half - 1) + t - 1, row, col, False)
            return
        for t, (row, dev, lo) in enumerate(((2 * ux + c, py, ra), (2 * uy + c, px, 0))):
            arrived(row, col)
            part = wall.at[row, col, pl.ds(lo, ra), :]
            go(rcopy(part, part, psem.at[n, 2 + t], hsem.at[t, col], dev))
            push(3 * n + t, row, col, False)

    def from_diagonal(n):
        if relay:
            col = ([m] + zcols)[n]
            row = 2 * ud + c
            for t, lo in enumerate((ra, 0)):
                part = wall.at[row, col, pl.ds(lo, ra), :]
                rcopy(part, part, zsem.at[0], hsem.at[t, col], cp).wait_recv()
            push(3 * n + 2, row, col, False)

    for i, col in enumerate(zcols):
        go_if(
            (col - m != 2) & (col - m != -2),
            rcopy(wall.at[d, m], wall.at[d, m], zsem.at[i], rsem.at[d, m], (d, col)),
        )
    push(0, d, m, True)
    xo[m] = xsb[m]

    start = pl.multiple_of(z.per * m // 128 * 128, 128)
    main = z.win - 128
    feat_in.wait()
    featw[:, 0:main] = feat_ref[:, pl.ds(start, main)]
    keys = (snd_ref, rcv_ref, msk_ref)
    for n, ref in enumerate(keys):
        keyw[n, 0:main] = ref[pl.ds(start, main)]

    @pl.when(m < nmp - 1)
    def _():
        after = pl.multiple_of(start + main, 128)
        featw[:, main:] = feat_ref[:, pl.ds(after, 128)]
        for n, ref in enumerate(keys):
            keyw[n, main:] = ref[pl.ds(after, 128)]

    @pl.when(m == nmp - 1)
    def _():
        featw[:, main:] = jnp.zeros((EFEAT, 128), bf)
        keyw[:, main:] = jnp.zeros((3, 128), jnp.int32)
        tail = z.edges - z.full
        if tail:
            featw[:, main : main + tail] = feat_ref[:, z.full :]
            for n, ref in enumerate(keys):
                keyw[n, main : main + tail] = ref[z.full :]

    place = lax.broadcasted_iota(jnp.int32, (1, z.win), 1) + (start - z.per * m)
    valid = (place >= 0) & (place < z.per)
    mol = jnp.zeros((1, z.win), jnp.int32)
    for i in range(1, nm):
        mol = mol + jnp.where(place >= ME * i, PADA, 0)
    keyw[0:1, :] = jnp.where(valid & (keyw[2:3, :] == 1), keyw[0:1, :], -1)
    keyw[1:2, :] = jnp.where(valid, keyw[1:2, :] + mol, -1)

    wio = lax.broadcasted_iota(jnp.int32, (PADA, 1024), 0)

    def permute(i):
        b = z.bases[i]
        st = wio == keyw[0:1, b : b + 1024]
        rt = jnp.where(wio + PADA * i == keyw[1:2, b : b + 1024], 1.0, 0.0).astype(bf)
        ff = featw[:, b : b + 1024].astype(f32)
        for q in range(4):
            zz = jnp.concatenate(
                [jnp.where(st, ff[f : f + 1, :], 0.0).astype(bf) for f in range(4 * q, 4 * q + 4)], axis=0
            )
            featp[i * PADA : (i + 1) * PADA, q * 128 : (q + 1) * 128] = dot(rt, zz, NT).astype(bf)

    for i in range(nm):
        permute(i)

    for i in range(1, ndp):
        row = (d - i + ndp) % ndp
        rcopy(wis.at[row], wis.at[row], wi_s.at[0], wi_r.at[row], cp).wait_recv()
    w_in = wis[...].astype(f32).sum(axis=0).astype(bf)
    delta = (
        lax.broadcasted_iota(jnp.int32, (PADA, 256), 0)
        == lax.broadcasted_iota(jnp.int32, (PADA, 256), 1) % PADA
    )

    @pl.loop(0, 16, unroll=4)
    def _(k):
        e = jnp.where(
            lax.broadcasted_iota(jnp.int32, (HID, 256), 0)
            == k * 8 + lax.broadcasted_iota(jnp.int32, (HID, 256), 1) // PADA,
            1.0,
            0.0,
        ).astype(bf)
        emat[k] = e
        wexp = dot(w_in, e, NN)
        for f in range(EFEAT):
            kron[k, f * PADA : (f + 1) * PADA, :] = jnp.where(delta, wexp[f : f + 1, :], 0.0).astype(bf)

    along_z(1)
    for i, p in enumerate(zp):
        go(rcopy(xsb.at[p[1]], xo.at[m], xs_s.at[i], xs_r.at[m], p))
    fp = featp[...]
    featt[...] = fp.T

    def hidden(lo):
        @pl.loop(lo, lo + 8, unroll=4)
        def _(k):
            p = dot(fp, kron[k], NN)
            s = sig(p)
            h = p * s
            hid[k] = h.astype(bf)
            hidt[k] = h.T.astype(bf)
            slope[k] = (s + h - h * s).astype(bf)

    hidden(0)
    in_plane(0)
    along_z(2)
    hidden(8)

    in_plane(1)
    from_diagonal(0)
    for i in range(3, nmp):
        along_z(i)
    for n in range(2, nmp):
        in_plane(n)
        from_diagonal(n - 1)
    from_diagonal(nmp - 1)

    for col in zcols:
        rcopy(xo.at[col], xo.at[col], xs_s.at[0], xs_r.at[col], cp).wait_recv()
    xf = jnp.zeros((z.rows, HID), f32)
    cf = jnp.zeros((z.rows, HID), f32)
    for j in range(nmp):
        sl = one_up(xo[j].astype(f32))
        here = (lane >= z.uw * j) & (lane < z.uw * (j + 1))
        xf = jnp.where(here, roll(sl, 0, z.uw * j), xf)
        cf = jnp.where(here, roll(sl, z.uw, z.uw * j), cf)
    x = xf.astype(bf)

    def rows_of(row, qs):
        return jnp.concatenate(
            [wall[row, j, q * rw : (q + 1) * rw, :] for q in qs for j in range(nmp)], axis=0
        )

    def make_b(row):
        for q in range(hl // 2):
            o = dot(x, rows_of(row, (2 * q, 2 * q + 1)), NT).astype(bf)
            bmat[row * hl + 2 * q] = o[:, :HID]
            bmat[row * hl + 2 * q + 1] = o[:, HID:]

    @pl.loop(0, half, unroll=2)
    def _(t):
        make_b(2 * t + c)

    for col in [m] + zcols:
        for t in range(half):
            arrived(2 * t + (1 - c), col)

    @pl.loop(0, half, unroll=2)
    def _(t):
        make_b(2 * t + (1 - c))

    sums = []
    for i in range(nm):
        hm = jnp.concatenate([hid[k, i * PADA : (i + 1) * PADA, :] for k in range(16)], axis=1)
        sums.append(dot(hm, bmat[:, i * PADA : (i + 1) * PADA, :].reshape(PADA * HID, HID), NN))
    summed = jnp.concatenate(sums, axis=0).astype(bf)

    def gru_rows(s, j):
        if il == 16:
            return jnp.concatenate([wall[k, j, wr + 16 * s : wr + 16 * s + 16, :] for k in range(ndp)], axis=0)
        for k in range(ndp):
            gfull[k * il : (k + 1) * il, 0:HID] = wall[k, j, wr + 16 * s : wr + 16 * s + 16, :].astype(f32)[:il]
        return gfull[0:HID, 0:HID].astype(bf)

    wg = [[gru_rows(s, j) for j in range(nmp)] for s in range(2)]

    def gates(a, s):
        outs = [dot(a, wg[s][j], NN) for j in range(nmp)]
        res = []
        for g in range(3):
            t = None
            for j in range(nmp):
                y = roll(outs[j], z.uw * g, z.uw * j)
                here = (lane >= z.uw * j) & (lane < z.uw * (j + 1))
                t = y if t is None else jnp.where(here, y, t)
            res.append(t)
        return res

    gi = gates(summed, 0)
    gs = gates(x, 1)
    reset = sig(gi[0] + gs[0])
    update = sig(gi[1] + gs[1])
    cand = jnp.tanh(gi[2] + reset * gs[2])
    ostate = (1.0 - update) * cand + update * xf
    dc = cf * (1.0 - update) * (1.0 - cand * cand)
    du = cf * (xf - cand) * update * (1.0 - update)
    dr = dc * gs[2] * reset * (1.0 - reset)

    def pack(gl, j):
        t = jnp.zeros((z.rows, HID), f32)
        for g in range(3):
            here = (lane >= z.uw * g) & (lane < z.uw * (g + 1))
            t = jnp.where(here, roll(gl[g], z.uw * j, z.uw * g), t)
        return t.astype(bf)

    al = [pack([dr, du, dc], j) for j in range(nmp)]
    bl = [pack([dr, du, dc * reset], j) for j in range(nmp)]
    ds = dot(jnp.concatenate(al, axis=1), jnp.concatenate(wg[0], axis=1), NT).astype(bf)
    gfull[:, HID : 2 * HID] = cf * update
    gfull[:, 0:HID] = dot(jnp.concatenate(bl, axis=1), jnp.concatenate(wg[1], axis=1), NT)
    for j in range(nmp):
        for s, (l, r) in enumerate(((summed, al[j]), (x, bl[j]))):
            gg = dot(l, r, TN)
            for k in range(ndp):
                part = gg[k * il : (k + 1) * il]
                if il < 16:
                    part = jnp.concatenate([part, jnp.zeros((16 - il, HID), f32)], axis=0)
                grads[k, j, wr + 16 * s : wr + 16 * s + 16, :] = part.astype(bf)

    dsb[...] = jnp.zeros(dsb.shape, bf)
    for i in range(nm):
        dsb[i * PADA : (i + 1) * PADA, i * HID : (i + 1) * HID] = ds[i * PADA : (i + 1) * PADA]

    def c_block(k):
        for p in range(nm // 2):
            o = dot(hidt[k], dsb[:, p * 256 : (p + 1) * 256], NN).astype(bf)
            for i in range(2):
                at = (2 * p + i) * PADA
                cmat[pl.ds(k * 8, 8), at : at + PADA, :] = o[:, i * HID : (i + 1) * HID].reshape(8, PADA, HID)

    if hl % 8:
        pl.loop(0, 16, unroll=8)(c_block)

    def grad_w(row):
        for k in range(hl // 8):
            c_block(row * (hl // 8) + k)
        for q in range(hl):
            o = dot(cmat[row * hl + q], x, TN).astype(bf)
            for j in range(nmp):
                grads[row, j, q * rw : (q + 1) * rw, :] = o[rw * j : rw * (j + 1)]

    cols = zcols[::-1] + [m]

    def core_arrived(t):
        rcopy(rc.at[t], rc.at[t], cs.at[t], cr.at[t], cp).wait_recv()
        if t == half - 1:
            return
        row = 2 * chips[t] + c
        for i, col in enumerate(cols):
            sb[t, i] = (grads[row, col].astype(f32) + rc[t, col].astype(f32)).astype(bf)
            if not relay:
                go(rcopy(sb.at[t, i], rp.at[t, col], ps.at[t, i], pr.at[t, col], pp[t]))
                continue
            if t < 2:
                go(rcopy(sb.at[t, i, pl.ds(0, ra), :], rp.at[t, col, pl.ds(0, ra), :], ps.at[t, i], pr.at[t, col], px))
            if t != 1:
                k = t // 2 + 2
                go(rcopy(sb.at[t, i, pl.ds(ra, ra), :], rp.at[k % 3, col, pl.ds(ra, ra), :], ps.at[k, i], pr.at[k, col], py))

    def rows_out(t):
        grad_w(2 * chips[t] + (1 - c))
        go(rcopy(grads.at[2 * chips[t] + (1 - c)], rc.at[t], cs.at[t], cr.at[t], cp))
        grad_w(2 * chips[t] + c)

    def part_arrived(slot, lo, col, k):
        here = rp.at[slot, col, pl.ds(lo, ra), :]
        rcopy(here, here, zsem.at[0], pr.at[k, col], cp).wait_recv()
        return rp[slot, col, lo : lo + ra, :].astype(f32)

    def turn(i):
        if not relay:
            return
        col = cols[i]
        ta[i] = (sb[2, i, 0:ra, :].astype(f32) + part_arrived(0, 0, col, 0)).astype(bf)
        go(rcopy(ta.at[i], r2a.at[col], p2s.at[0, i], p2r.at[0, col], py))
        tb[i] = (sb[1, i, ra:, :].astype(f32) + part_arrived(2, ra, col, 2)).astype(bf)
        go(rcopy(tb.at[i], r2b.at[col], p2s.at[1, i], p2r.at[1, col], px))

    def to_z(i):
        col = cols[i]
        q = grads[d, col].astype(f32) + rc[half - 1, col].astype(f32)
        if relay:
            rcopy(r2a.at[col], r2a.at[col], zsem.at[0], p2r.at[0, col], cp).wait_recv()
            rcopy(r2b.at[col], r2b.at[col], zsem.at[0], p2r.at[1, col], cp).wait_recv()
            qa = q[:ra] + part_arrived(1, 0, col, 1) + r2a[col].astype(f32)
            qb = q[ra:] + part_arrived(0, ra, col, 3) + r2b[col].astype(f32)
            q = jnp.concatenate([qa, qb], axis=0)
        else:
            for t in range(half - 1):
                here = rp.at[t, col]
                rcopy(here, here, zsem.at[0], pr.at[t, col], cp).wait_recv()
                q = q + rp[t, col].astype(f32)
        if i < nmp - 1:
            zs[i] = q.astype(bf)
            go(rcopy(zs.at[i], rz.at[m], z2.at[i], zr.at[m], (d, col)))
        else:
            fin[...] = q

    def by_eight(v, mask):
        v = jnp.where(mask[None], v.reshape(EFEAT, PADA, -1), 0.0)
        return (v[:, 0:8] + v[:, 8:16] + v[:, 16:24] + v[:, 24:32]).reshape(EFEAT * 8, -1).astype(bf)

    eight = jnp.where(
        lax.broadcasted_iota(jnp.int32, (EFEAT, EFEAT * 8), 0)
        == lax.broadcasted_iota(jnp.int32, (EFEAT, EFEAT * 8), 1) // 8,
        1.0,
        0.0,
    ).astype(bf)
    tiles = -(-z.win // 256)
    cuts = (0, tiles // 2, tiles)

    def edges_back(part):
        for n in range(cuts[part], cuts[part + 1]):
            count = min(256, z.win - n * 256)
            at = pl.ds(n * 256, count)
            all_rows = lax.broadcasted_iota(jnp.int32, (z.rows, count), 0)
            rt = jnp.where(all_rows == keyw[1:2, at], 1.0, 0.0).astype(bf)
            eights[n, :, 0:count] = by_eight(dot(gbt[...], rt, NN), wio[:, :count] == keyw[0:1, at])
        for n in range(cuts[part], cuts[part + 1]):
            count = min(256, z.win - n * 256)
            geo[m, :, n * 256 : n * 256 + count] = dot(eight, eights[n, :, 0:count], NN).astype(bf)

    def edges_on(s):
        for part in (0, 1):
            edges_on_part(s, part)

    def edges_on_part(s, part):
        lo, hi = 256 * cuts[part], min(256 * cuts[part + 1], z.win)
        for way in (0, 1):
            col = m - s if way == 0 else m + s
            nxt = m + 1 if way == 0 else m - 1
            src = geo.at[col, :, pl.ds(lo, hi - lo)]
            if s:
                pl.when(inside(col))(rcopy(src, src, zsem.at[0], ge_r.at[part, col], cp).wait_recv)
            if s < nmp - 1:
                go_if(
                    inside(col) & inside(nxt),
                    rcopy(src, src, ge_s.at[part, s, way], ge_r.at[part, col], (d, nxt)),
                )

    step = min(DXC, hl)

    def state_grad(lo, hi):
        @pl.loop(lo, hi, unroll=2)
        def _(row):
            for q in range(0, hl, step):
                qs = range(q, q + step)
                cc = jnp.concatenate([cmat[row * hl + k] for k in qs], axis=1)
                gacc[...] += dot(cc, rows_of(row, qs), NN)

    rows_out(0)
    for i in range(nm):
        dm = ds[i * PADA : (i + 1) * PADA]
        for k in range(16):
            o = dot(dm, bmat[k * 8 : (k + 1) * 8, i * PADA : (i + 1) * PADA, :].reshape(256, HID), NT)
            dpre[k, i * PADA : (i + 1) * PADA, :] = (
                o * slope[k, i * PADA : (i + 1) * PADA, :].astype(f32)
            ).astype(bf)
    core_arrived(0)
    for t in range(1, half - 1):
        rows_out(t)
    gb = dot(
        jnp.concatenate([dpre[k] for k in range(16)], axis=1),
        jnp.concatenate([kron[k] for k in range(16)], axis=1),
        NT,
    ).astype(bf)
    gbt[...] = gb.T
    edges_back(0)
    edges_on_part(0, 0)
    for t in range(1, half - 1):
        core_arrived(t)
    edges_back(1)
    edges_on_part(0, 1)
    rows_out(half - 1)
    turn(0)

    @pl.loop(0, 16, unroll=16)
    def _(k):
        eights[k] = by_eight(dot(featt[...], dpre[k], NN), delta)

    gin = dot(
        jnp.concatenate([eights[k] for k in range(16)], axis=1),
        jnp.concatenate([emat[k] for k in range(16)], axis=1),
        NT,
    )
    gis[d] = gin.reshape(EFEAT, 8, HID).sum(axis=1).astype(bf)
    for i, p in enumerate(dpp):
        go(rcopy(gis.at[d], gis.at[d], gi_s.at[i], gi_r.at[d], p))
    turn(1)
    edges_on(1)

    gacc[...] = jnp.zeros(gacc.shape, f32)
    state_grad(0, ndp // 2)
    turn(2)
    core_arrived(half - 1)
    to_z(0)
    state_grad(ndp // 2, ndp)
    gfin = gacc[...] + gfull[:, 0:HID] + gfull[:, HID : 2 * HID]
    for j in range(nmp):
        a = roll(ostate, z.uw * j, 0)
        b = roll(gfin, z.uw * j, z.uw)
        osb[j] = two_up(jnp.where(lane < z.uw, a, b)).astype(bf)
    for i, p in enumerate(zp):
        go(rcopy(osb.at[p[1]], oso.at[m], os_s.at[i], os_r.at[m], p))
    oso[m] = osb[m]
    turn(3)
    edges_on(2)
    to_z(1)

    gi_sum = gis[d].astype(f32)
    for i in range(1, ndp):
        row = (d - i + ndp) % ndp
        rcopy(gis.at[row], gis.at[row], gi_s.at[0], gi_r.at[row], cp).wait_recv()
        gi_sum = gi_sum + gis[row].astype(f32)
    giz_s[...] = gi_sum.astype(bf)
    for i, p in enumerate(zp):
        go(rcopy(giz_s, giz.at[m], gz_s.at[i], gz_r.at[m], p))
    to_z(2)
    to_z(3)

    for col in zcols:
        rcopy(oso.at[col], oso.at[col], os_s.at[0], os_r.at[col], cp).wait_recv()
    for j in range(nmp):
        stage2[j * z.rows : (j + 1) * z.rows, :] = one_up(oso[j].astype(f32))
    for i in range(z.mols):
        stage1[i * MA : (i + 1) * MA, :] = stage2[i * PADA : i * PADA + MA, :]
    stage[...] = stage1[...].T
    at_ref[0 : z.uw, :] = stage[0 : z.uw, 0 : z.atoms] * nmrow[...]
    at_ref[z.uw : 2 * z.uw, :] = stage[z.uw : 2 * z.uw, 0 : z.atoms]

    for col in zcols:
        rcopy(giz.at[col], giz.at[col], gz_s.at[0], gz_r.at[col], cp).wait_recv()
        gi_sum = gi_sum + giz[col].astype(f32)
    gi_ref[...] = pltpu.roll(gi_sum, HID - d * z.ew, 1)[:, 0 : z.ew]
    for col in zcols:
        rcopy(rz.at[col], rz.at[col], z2.at[0], zr.at[col], cp).wait_recv()
        fin[...] += rz[col].astype(f32)
    for s in range(2):
        for g in range(3):
            gg_ref[s, g] = fin[wr + 16 * s : wr + 16 * s + il, g * z.uw : (g + 1) * z.uw]
    wtmp[...] = fin[0:wr, :].reshape(hl, rw, HID)
    for r in range(rw):
        go_ref[:, r * HID : (r + 1) * HID] = wtmp[:, r, :]

    edges_on(3)
    for j, lo in enumerate(z.starts):
        first = geo[j, :, 0:128]
        if j:
            first = (first.astype(f32) + geo[j - 1, :, main:].astype(f32)).astype(bf)
        ge_ref[:, lo : lo + 128] = first
        ge_ref[:, lo + 128 : lo + main] = geo[j, :, 128:main]
    if z.edges > z.full:
        ge_ref[:, z.full :] = geo[nmp - 1, :, main : main + z.edges - z.full]
    for y in sends:
        y.wait_send()
    for ok, y in maybe:
        pl.when(ok)(y.wait_send)


def whole_step(z, eo, ei, gw, ns, og, live, feat, snd, rcv, msk):
    dma = pltpu.SemaphoreType.DMA
    ndp, nmp, half = z.ndp, z.nmp, z.half
    rows, rb, win = z.rows, z.rb, z.win
    vm = pltpu.VMEM
    ra = rb // 2
    relay = half == 4
    return pl.pallas_call(
        functools.partial(kernel, z),
        out_shape=(
            jax.ShapeDtypeStruct(eo.shape, f32),
            jax.ShapeDtypeStruct(gw.shape, f32),
            jax.ShapeDtypeStruct(ei.shape, f32),
            jax.ShapeDtypeStruct((2 * z.uw, z.atoms), f32),
            jax.ShapeDtypeStruct(feat.shape, bf),
        ),
        in_specs=[pl.BlockSpec(memory_space=vm)] * 6 + [pl.BlockSpec(memory_space=pl.ANY)] + [pl.BlockSpec(memory_space=vm)] * 3,
        out_specs=(pl.BlockSpec(memory_space=vm),) * 5,
        scratch_shapes=[
            vm((ndp, nmp, rb, HID), bf),
            vm((nmp, rows // 2, HID), bf),
            vm((nmp, rows // 2, HID), bf),
            vm((ndp, EFEAT, HID), bf),
            vm((HID, -(-z.atoms // 128) * 128), f32),
            vm((-(-z.atoms // 128) * 128, HID), f32),
            vm((nmp * rows, HID), f32),
            vm((z.hl, z.rw, HID), f32),
            vm((32, HID), f32),
            vm((EFEAT, HID), f32),
            vm((1, z.atoms), f32),
            vm(feat.shape, bf),
            vm((EFEAT, win), bf),
            vm((3, win), jnp.int32),
            vm((rows, 512), bf),
            vm((512, rows), bf),
            vm((512, rows), bf),
            vm((16, 512, 256), bf),
            vm((16, HID, 256), bf),
            vm((16, rows, 256), bf),
            vm((16, 256, rows), bf),
            vm((16, rows, 256), bf),
            vm((HID, rows, HID), bf),
            vm((HID, rows, HID), bf),
            vm((rows, z.nm * HID), bf),
            vm((16, rows, 256), bf),
            vm((rows, HID), f32),
            vm((rows, 512), f32),
            vm((max(16, -(-win // 256)), EFEAT * 8, 256), bf),
            vm((ndp, nmp, rb, HID), bf),
            vm((half, nmp, rb, HID), bf),
            vm((half - 1, nmp, rb, HID), bf),
            vm((half - 1, nmp, rb, HID), bf),
            vm((nmp, ra, HID), bf),
            vm((nmp, ra, HID), bf),
            vm((nmp, ra, HID), bf),
            vm((nmp, ra, HID), bf),
            vm((nmp - 1, rb, HID), bf),
            vm((nmp, rb, HID), bf),
            vm((rb, HID), f32),
            vm((nmp, rows // 2, HID), bf),
            vm((nmp, rows // 2, HID), bf),
            vm((nmp, EFEAT, win), bf),
            vm((ndp, EFEAT, HID), bf),
            vm((nmp, EFEAT, HID), bf),
            vm((EFEAT, HID), bf),
            dma(()),
            dma((nmp - 1,)),
            dma((2,)),
            dma((nmp, max(half - 1, 4))),
            dma((nmp + nmp * (half - 1),)),
            dma((ndp, nmp)),
            dma((2, nmp)),
            dma((nmp - 1,)), dma((nmp,)),
            dma((ndp - 1,)), dma((ndp,)),
            dma((half,)), dma((half,)),
            dma((max(half - 1, 4), nmp)), dma((max(half - 1, 4), nmp)),
            dma((2, nmp)), dma((2, nmp)),
            dma((nmp - 1,)), dma((nmp,)),
            dma((nmp - 1,)), dma((nmp,)),
            dma((2, nmp - 1, 2)), dma((2, nmp)),
            dma((ndp - 1,)), dma((ndp,)),
            dma((nmp - 1,)), dma((nmp,)),
        ],
        compiler_params=pltpu.CompilerParams(
            collective_id=0, has_side_effects=True, vmem_limit_bytes=VMEM_LIMIT
        ),
    )(eo, ei, gw, ns, og, live, feat, snd, rcv, msk)


beta_one = 0.5
beta_two = 0.5
learn_rate = 0.05
decay_rate = 0.01
epsilon = 1e-08


def adam_update(weight, gradient, first_moment, second_moment):
    first_new = beta_one * first_moment + (1.0 - beta_one) * gradient
    second_new = beta_two * second_moment + (1.0 - beta_two) * gradient * gradient
    mean_hat = first_new / (1.0 - beta_one**STEP)
    square_hat = second_new / (1.0 - beta_two**STEP)
    weight_new = weight - learn_rate * (
        mean_hat / (jnp.sqrt(square_hat) + epsilon) + decay_rate * weight
    )
    return (first_new, second_new, weight_new, weight_new.astype(bf))


def finish_kernel(at_ref, ge_ref, *refs):
    gs_uw = at_ref.shape[0] // 2
    ins, outs = refs[:12], refs[12:]
    outs[0][...] = at_ref[0:gs_uw, :]
    outs[1][...] = at_ref[gs_uw:, :]
    outs[2][...] = ge_ref[...].astype(f32)
    for n in range(3):
        new = adam_update(*[r[...] for r in ins[4 * n : 4 * n + 4]])
        for ref, v in zip(outs[3 + 4 * n : 7 + 4 * n], new):
            ref[...] = v


def finish(at, ge, *layers):
    half = jax.ShapeDtypeStruct((at.shape[0] // 2, at.shape[1]), f32)
    results = [half, half, jax.ShapeDtypeStruct(ge.shape, f32)]
    for n in range(3):
        results += [jax.ShapeDtypeStruct(layers[4 * n].shape, t) for t in (f32, f32, f32, bf)]
    return pl.pallas_call(
        finish_kernel,
        out_shape=tuple(results),
        in_specs=[pl.BlockSpec(memory_space=pltpu.VMEM)] * 14,
        out_specs=(pl.BlockSpec(memory_space=pltpu.VMEM),) * 15,
        compiler_params=pltpu.CompilerParams(vmem_limit_bytes=VMEM_LIMIT),
    )(at, ge, *layers)


def body(
    ndp, nmp,
    node_state, edge_feat, sender, receiver, edge_mask, node_mask, out_grad,
    edge_in, edge_out, gru_weight,
    edge_in_m1, edge_in_m2, edge_out_m1, edge_out_m2, gru_m1, gru_m2,
):
    z = Shape(ndp, nmp, node_state, edge_feat, edge_in, edge_out, gru_weight)
    g_out, g_gru, g_in, at, ge = whole_step(
        z, edge_out, edge_in, gru_weight, node_state.T, out_grad.T, node_mask,
        edge_feat, sender, receiver, edge_mask,
    )
    out_state, grad_state, *rest = finish(
        at, ge,
        edge_in, g_in, edge_in_m1, edge_in_m2,
        edge_out, g_out, edge_out_m1, edge_out_m2,
        gru_weight, g_gru, gru_m1, gru_m2,
    )
    return (out_state.T, grad_state.T, *rest)


def solution(mesh):
    ndp, nmp = mesh.shape["dp"], mesh.shape["mp"]
    rows, lanes, gru = P("dp", "mp"), P(None, "dp"), P(None, None, "dp", "mp")
    edge = P("dp")
    return jax.shard_map(
        functools.partial(body, ndp, nmp),
        mesh=mesh,
        in_specs=(
            rows, lanes, edge, edge, edge, edge, rows,
            lanes, rows, gru, lanes, lanes, rows, rows, gru, gru,
        ),
        out_specs=(rows, rows, lanes) + (lanes,) * 4 + (rows,) * 4 + (gru,) * 4,
        check_vma=False,
    )
```

```python
import functools

import jax
import jax.numpy as jnp
from jax import lax
from jax.experimental import pallas as pl
from jax.experimental.pallas import tpu as pltpu
from jax.sharding import PartitionSpec as P

HID = 128
EFEAT = 16
MA = 29
ME = 812
PADA = 32
STEP = 5
DXC = 4
MESH = pl.DeviceIdType.MESH
VMEM_LIMIT = 60 << 20
bf = jnp.bfloat16
f32 = jnp.float32
NT = (((1,), (1,)), ((), ()))
TN = (((0,), (0,)), ((), ()))
NN = (((1,), (0,)), ((), ()))


def dot(a, b, dims):
    return lax.dot_general(a, b, dims, preferred_element_type=f32)


def roll(x, src, dst):
    shift = (dst - src) % HID
    return pltpu.roll(x, shift, 1) if shift else x


def sig(v):
    return 0.5 + 0.5 * jnp.tanh(0.5 * v)


def rcopy(src, dst, ssem, rsem, dev):
    return pltpu.make_async_remote_copy(
        src_ref=src, dst_ref=dst, send_sem=ssem, recv_sem=rsem, device_id=dev, device_id_type=MESH
    )


class Shape:
    def __init__(self, ndp, nmp, node_state, edge_feat, edge_in, edge_out, gru):
        self.ndp, self.nmp, self.half = ndp, nmp, ndp // 2
        self.atoms, self.uw = node_state.shape
        self.edges = edge_feat.shape[1]
        self.mols = self.atoms // MA
        self.nm = self.mols // nmp
        self.rows = self.nm * PADA
        self.hl, self.il, self.ew = edge_out.shape[0], gru.shape[2], edge_in.shape[1]
        self.rw = edge_out.shape[1] // HID
        self.wr = self.hl * self.rw
        self.rb = self.wr + 32
        self.per = self.nm * ME
        self.starts = [self.per * j // 128 * 128 for j in range(nmp)]
        self.bases = [ME * i // 128 * 128 for i in range(self.nm)]
        self.win = self.bases[-1] + 1024
        self.full = self.edges // 128 * 128
        shift = max(self.per * j - s for j, s in enumerate(self.starts))
        assert all(ME * i + shift + ME <= b + 1024 for i, b in enumerate(self.bases))
        assert self.starts[-1] + self.win - 128 == self.full
        assert all(b - a == self.win - 128 for a, b in zip(self.starts, self.starts[1:]))


def kernel(
    z,
    eo_ref, ei_ref, gw_ref, ns_ref, og_ref, nm_ref, feat_hbm, snd_ref, rcv_ref, msk_ref,
    go_ref, gg_ref, gi_ref, at_ref, ge_ref,
    wall, xsb, xo, wis, stage, stage1, stage2, wtmp, stmp, itmp, nmrow, feat_ref, featw, keyw,
    featp, featt, gbt, kron, emat, hid, hidt, slope, bmat, cmat, dsb, dpre, gacc, sacc, gfull, eights,
    grads, rc, sb, rp, ta, tb, r2a, r2b, zs, rz, fin, osb, oso, geo, gis, giz, giz_s,
    fsem, zsem, zfsem, psem, csem, rsem, xs_s, xs_r, wi_s, wi_r,
    cs, cr, ps, pr, p2s, p2r, z2, zr, os_s, os_r, ge_s, ge_r, gi_s, gi_r, gz_s, gz_r,
):
    ndp, nmp, half, nm = z.ndp, z.nmp, z.half, z.nm
    hl, il, wr, rb, rw = z.hl, z.il, z.wr, z.rb, z.rw
    d = lax.axis_index("dp")
    m = lax.axis_index("mp")
    u = d // 2
    c = d % 2
    relay = half == 4
    low = jnp.where(2 * m < nmp, 1, 0)
    side = low * m + (1 - low) * (nmp - 1 - m)
    near = [jnp.where(i <= side, i - 1, i) for i in range(1, nmp)]
    zcols = [low * i + (1 - low) * (nmp - 1 - i) for i in near]
    zp = [(d, col) for col in zcols]
    if relay:
        ux = u + 1 - 2 * (u % 2)
        uy = (u + 2) % half
        ud = (ux + 2) % half
        chips = [ud, ux, uy, u]
        px, py = (2 * ux + c, m), (2 * uy + c, m)
        pp = [px, py]
    else:
        chips = [(u + t) % half for t in range(1, half)] + [u]
        pp = [(2 * v + c, m) for v in chips[:-1]]
    ra = rb // 2
    cp = (2 * u + (1 - c), m)
    dpp = [((d + i) % ndp, m) for i in range(1, ndp)]
    bar = pltpu.get_barrier_semaphore()
    feat_in = pltpu.make_async_copy(feat_hbm, feat_ref, fsem)
    feat_in.start()
    for p in zp + dpp:
        pl.semaphore_signal(bar, inc=1, device_id=p, device_id_type=MESH)
    lane = lax.broadcasted_iota(jnp.int32, (1, HID), 1)

    def two_up(v):
        return jnp.where(lane < 64, v[: z.rows // 2], pltpu.roll(v[z.rows // 2 :], 64, 1))

    def one_up(v):
        return jnp.concatenate([v, pltpu.roll(v, 64, 1)], axis=0)

    for r in range(rw):
        wtmp[:, r, :] = eo_ref[:, r * HID : (r + 1) * HID]
    wall[d, m, 0:wr, :] = wtmp[...].reshape(wr, HID).astype(bf)
    stmp[...] = jnp.zeros(stmp.shape, f32)
    for s in range(2):
        for g in range(3):
            stmp[16 * s : 16 * s + il, g * z.uw : (g + 1) * z.uw] = gw_ref[s, g]
    wall[d, m, wr:rb, :] = stmp[...].astype(bf)
    itmp[...] = jnp.zeros(itmp.shape, f32)
    itmp[:, 0 : z.ew] = ei_ref[...]
    wis[d] = pltpu.roll(itmp[...], d * z.ew, 1).astype(bf)
    stage[...] = jnp.zeros(stage.shape, f32)
    stage[0 : z.uw, 0 : z.atoms] = ns_ref[...].astype(f32)
    nmrow[0, :] = nm_ref[...].astype(f32)
    stage[z.uw : 2 * z.uw, 0 : z.atoms] = og_ref[...] * nmrow[...]
    stage1[...] = stage[...].T
    stage2[...] = jnp.zeros(stage2.shape, f32)
    for i in range(z.mols):
        stage2[i * PADA : i * PADA + MA, :] = stage1[i * MA : (i + 1) * MA, :]
    for j in range(nmp):
        xsb[j] = two_up(stage2[j * z.rows : (j + 1) * z.rows, :]).astype(bf)
    pl.semaphore_wait(bar, len(zp + dpp))

    sends = []
    maybe = []

    def go(*copies):
        for x in copies:
            x.start()
        sends.extend(copies)

    def go_if(ok, x):
        pl.when(ok)(x.start)
        maybe.append((ok, x))

    def inside(col):
        return (col >= 0) & (col < nmp)

    def apart(col, n):
        return (col - m == n) | (col - m == -n)

    for i, p in enumerate(dpp):
        go(rcopy(wis.at[d], wis.at[d], wi_s.at[i], wi_r.at[d], p))

    rows_x = [2 * ux + c, 2 * uy + c] if relay else [2 * v + c for v in chips[:-1]]
    here_cols = [m] + zcols
    turns = [0]

    def piece(row, col, k):
        return wall.at[row, col, pl.ds(k * ra, ra), :]

    def arrived(row, col, k):
        src = piece(row, col, k)
        rcopy(src, src, fsem, rsem.at[row, col, k], cp).wait_recv()

    def give(row, col, k, sem, dev):
        src = piece(row, col, k)
        go(rcopy(src, src, sem, rsem.at[row, col, k], dev))

    def to_core(row, col, k):
        give(row, col, k, csem.at[turns[0]], cp)
        turns[0] += 1

    def push(n, k):
        col = here_cols[n]
        for t in range(len(pp)):
            t = t if k == 0 else len(pp) - 1 - t
            give(d, col, k, psem.at[n, k, t], pp[len(pp) - 1 - t])
        if relay and last_direct(n, k):
            give(d, col, k, psem.at[n, k, 2], (2 * ud + c, m))
        to_core(d, col, k)

    def last_direct(n, k):
        return n == nmp - 1 and k == 1

    def along_z(n):
        col = here_cols[n]
        for k in (0, 1):
            arrived(d, col, k)
            if n < 3:
                beyond = 2 * m - col
                src = piece(d, col, k)
                go_if(
                    inside(beyond) & apart(col, 1),
                    rcopy(src, src, zfsem.at[n - 1, k], rsem.at[d, col, k], (d, beyond)),
                )
            push(n, k)

    def in_plane(n):
        col = here_cols[n]
        if not relay:
            for row in rows_x:
                for k in (0, 1):
                    arrived(row, col, k)
                    to_core(row, col, k)
            return
        for k in (0, 1):
            for t in (k, 1 - k):
                row = rows_x[1 - t]
                arrived(row, col, k)
                if t == k and not last_direct(n, k):
                    give(row, col, k, psem.at[n, k, 3], (px, py)[k])
                to_core(row, col, k)

    def from_diagonal(n):
        if relay:
            for k in (0, 1):
                arrived(2 * ud + c, here_cols[n], k)
                to_core(2 * ud + c, here_cols[n], k)

    for k in (0, 1):
        for i, col in enumerate(zcols):
            src = piece(d, m, k)
            go_if(
                (col - m != 2) & (col - m != -2),
                rcopy(src, src, zsem.at[i, k], rsem.at[d, m, k], (d, col)),
            )
        push(0, k)
    xo[m] = xsb[m]

    start = pl.multiple_of(z.per * m // 128 * 128, 128)
    main = z.win - 128
    feat_in.wait()
    featw[:, 0:main] = feat_ref[:, pl.ds(start, main)]
    keys = (snd_ref, rcv_ref, msk_ref)
    for n, ref in enumerate(keys):
        keyw[n, 0:main] = ref[pl.ds(start, main)]

    @pl.when(m < nmp - 1)
    def _():
        after = pl.multiple_of(start + main, 128)
        featw[:, main:] = feat_ref[:, pl.ds(after, 128)]
        for n, ref in enumerate(keys):
            keyw[n, main:] = ref[pl.ds(after, 128)]

    @pl.when(m == nmp - 1)
    def _():
        featw[:, main:] = jnp.zeros((EFEAT, 128), bf)
        keyw[:, main:] = jnp.zeros((3, 128), jnp.int32)
        tail = z.edges - z.full
        if tail:
            featw[:, main : main + tail] = feat_ref[:, z.full :]
            for n, ref in enumerate(keys):
                keyw[n, main : main + tail] = ref[z.full :]

    place = lax.broadcasted_iota(jnp.int32, (1, z.win), 1) + (start - z.per * m)
    valid = (place >= 0) & (place < z.per)
    mol = jnp.zeros((1, z.win), jnp.int32)
    for i in range(1, nm):
        mol = mol + jnp.where(place >= ME * i, PADA, 0)
    keyw[0:1, :] = jnp.where(valid & (keyw[2:3, :] == 1), keyw[0:1, :], -1)
    keyw[1:2, :] = jnp.where(valid, keyw[1:2, :] + mol, -1)

    wio = lax.broadcasted_iota(jnp.int32, (PADA, 1024), 0)

    def permute(i):
        b = z.bases[i]
        st = wio == keyw[0:1, b : b + 1024]
        rt = jnp.where(wio + PADA * i == keyw[1:2, b : b + 1024], 1.0, 0.0).astype(bf)
        ff = featw[:, b : b + 1024].astype(f32)
        for q in range(4):
            zz = jnp.concatenate(
                [jnp.where(st, ff[f : f + 1, :], 0.0).astype(bf) for f in range(4 * q, 4 * q + 4)], axis=0
            )
            featp[i * PADA : (i + 1) * PADA, q * 128 : (q + 1) * 128] = dot(rt, zz, NT).astype(bf)

    for i in range(nm):
        permute(i)

    for i in range(1, ndp):
        row = (d - i + ndp) % ndp
        rcopy(wis.at[row], wis.at[row], wi_s.at[0], wi_r.at[row], cp).wait_recv()
    w_in = wis[...].astype(f32).sum(axis=0).astype(bf)
    delta = (
        lax.broadcasted_iota(jnp.int32, (PADA, 256), 0)
        == lax.broadcasted_iota(jnp.int32, (PADA, 256), 1) % PADA
    )

    @pl.loop(0, 16, unroll=4)
    def _(k):
        e = jnp.where(
            lax.broadcasted_iota(jnp.int32, (HID, 256), 0)
            == k * 8 + lax.broadcasted_iota(jnp.int32, (HID, 256), 1) // PADA,
            1.0,
            0.0,
        ).astype(bf)
        emat[k] = e
        wexp = dot(w_in, e, NN)
        for f in range(EFEAT):
            kron[k, f * PADA : (f + 1) * PADA, :] = jnp.where(delta, wexp[f : f + 1, :], 0.0).astype(bf)

    along_z(1)
    in_plane(0)
    fp = featp[...]
    featt[...] = fp.T

    def hidden(lo):
        @pl.loop(lo, lo + 8, unroll=4)
        def _(k):
            p = dot(fp, kron[k], NN)
            s = sig(p)
            h = p * s
            hid[k] = h.astype(bf)
            hidt[k] = h.T.astype(bf)
            slope[k] = (s + h - h * s).astype(bf)

    hidden(0)
    along_z(2)
    in_plane(1)
    for i, p in enumerate(zp):
        go(rcopy(xsb.at[p[1]], xo.at[m], xs_s.at[i], xs_r.at[m], p))
    hidden(8)

    from_diagonal(0)
    along_z(3)
    in_plane(2)
    from_diagonal(1)

    for col in zcols:
        rcopy(xo.at[col], xo.at[col], xs_s.at[0], xs_r.at[col], cp).wait_recv()
    xf = jnp.zeros((z.rows, HID), f32)
    cf = jnp.zeros((z.rows, HID), f32)
    for j in range(nmp):
        sl = one_up(xo[j].astype(f32))
        here = (lane >= z.uw * j) & (lane < z.uw * (j + 1))
        xf = jnp.where(here, roll(sl, 0, z.uw * j), xf)
        cf = jnp.where(here, roll(sl, z.uw, z.uw * j), cf)
    x = xf.astype(bf)

    def rows_of(row, qs):
        return jnp.concatenate(
            [wall[row, j, q * rw : (q + 1) * rw, :] for q in qs for j in range(nmp)], axis=0
        )

    def make_b(row):
        for q in range(hl // 2):
            o = dot(x, rows_of(row, (2 * q, 2 * q + 1)), NT).astype(bf)
            bmat[row * hl + 2 * q] = o[:, :HID]
            bmat[row * hl + 2 * q + 1] = o[:, HID:]

    sacc[...] = jnp.zeros(sacc.shape, f32)

    def use_row(row):
        make_b(row)
        if hl % 8 == 0:
            parts = [row * (hl // 8) + k for k in range(hl // 8)]
            for i in range(nm):
                at = pl.ds(i * PADA, PADA)
                hm = jnp.concatenate([hid[k, at, :] for k in parts], axis=1)
                sacc[at, :] += dot(hm, bmat[pl.ds(row * hl, hl), at, :].reshape(PADA * hl, HID), NN)

    def from_core(row):
        for col in here_cols:
            for k in (0, 1):
                arrived(row, col, k)
        use_row(row)

    use_row(d)
    in_plane(3)
    for row in rows_x:
        use_row(row)
    from_core(cp[0])
    from_diagonal(2)
    from_diagonal(3)
    if relay:
        use_row(2 * ud + c)
    for row in rows_x + ([2 * ud + c] if relay else []):
        from_core(row + 1 - 2 * c)
    if hl % 8:
        for i in range(nm):
            hm = jnp.concatenate([hid[k, i * PADA : (i + 1) * PADA, :] for k in range(16)], axis=1)
            sacc[i * PADA : (i + 1) * PADA, :] = dot(
                hm, bmat[:, i * PADA : (i + 1) * PADA, :].reshape(PADA * HID, HID), NN
            )
    summed = sacc[...].astype(bf)

    def gru_rows(s, j):
        if il == 16:
            return jnp.concatenate([wall[k, j, wr + 16 * s : wr + 16 * s + 16, :] for k in range(ndp)], axis=0)
        for k in range(ndp):
            gfull[k * il : (k + 1) * il, 0:HID] = wall[k, j, wr + 16 * s : wr + 16 * s + 16, :].astype(f32)[:il]
        return gfull[0:HID, 0:HID].astype(bf)

    wg = [[gru_rows(s, j) for j in range(nmp)] for s in range(2)]

    def gates(a, s):
        outs = [dot(a, wg[s][j], NN) for j in range(nmp)]
        res = []
        for g in range(3):
            t = None
            for j in range(nmp):
                y = roll(outs[j], z.uw * g, z.uw * j)
                here = (lane >= z.uw * j) & (lane < z.uw * (j + 1))
                t = y if t is None else jnp.where(here, y, t)
            res.append(t)
        return res

    gi = gates(summed, 0)
    gs = gates(x, 1)
    reset = sig(gi[0] + gs[0])
    update = sig(gi[1] + gs[1])
    cand = jnp.tanh(gi[2] + reset * gs[2])
    ostate = (1.0 - update) * cand + update * xf
    dc = cf * (1.0 - update) * (1.0 - cand * cand)
    du = cf * (xf - cand) * update * (1.0 - update)
    dr = dc * gs[2] * reset * (1.0 - reset)

    def pack(gl, j):
        t = jnp.zeros((z.rows, HID), f32)
        for g in range(3):
            here = (lane >= z.uw * g) & (lane < z.uw * (g + 1))
            t = jnp.where(here, roll(gl[g], z.uw * j, z.uw * g), t)
        return t.astype(bf)

    al = [pack([dr, du, dc], j) for j in range(nmp)]
    bl = [pack([dr, du, dc * reset], j) for j in range(nmp)]
    ds = dot(jnp.concatenate(al, axis=1), jnp.concatenate(wg[0], axis=1), NT).astype(bf)
    gfull[:, HID : 2 * HID] = cf * update
    gfull[:, 0:HID] = dot(jnp.concatenate(bl, axis=1), jnp.concatenate(wg[1], axis=1), NT)
    for j in range(nmp):
        for s, (l, r) in enumerate(((summed, al[j]), (x, bl[j]))):
            gg = dot(l, r, TN)
            for k in range(ndp):
                part = gg[k * il : (k + 1) * il]
                if il < 16:
                    part = jnp.concatenate([part, jnp.zeros((16 - il, HID), f32)], axis=0)
                grads[k, j, wr + 16 * s : wr + 16 * s + 16, :] = part.astype(bf)

    dsb[...] = jnp.zeros(dsb.shape, bf)
    for i in range(nm):
        dsb[i * PADA : (i + 1) * PADA, i * HID : (i + 1) * HID] = ds[i * PADA : (i + 1) * PADA]

    def c_block(k):
        for p in range(nm // 2):
            o = dot(hidt[k], dsb[:, p * 256 : (p + 1) * 256], NN).astype(bf)
            for i in range(2):
                at = (2 * p + i) * PADA
                cmat[pl.ds(k * 8, 8), at : at + PADA, :] = o[:, i * HID : (i + 1) * HID].reshape(8, PADA, HID)

    if hl % 8:
        pl.loop(0, 16, unroll=8)(c_block)

    def grad_w(row):
        for k in range(hl // 8):
            c_block(row * (hl // 8) + k)
        for q in range(hl):
            o = dot(cmat[row * hl + q], x, TN).astype(bf)
            for j in range(nmp):
                grads[row, j, q * rw : (q + 1) * rw, :] = o[rw * j : rw * (j + 1)]

    cols = zcols[::-1] + [m]

    def core_arrived(t, col):
        rcopy(rc.at[t, col], rc.at[t, col], fsem, cr.at[t, col], cp).wait_recv()

    def plane_out(t, *which):
        row = 2 * chips[t] + c
        for i in which:
            col = cols[i]
            core_arrived(t, col)
            sb[t, i] = (grads[row, col].astype(f32) + rc[t, col].astype(f32)).astype(bf)
            if not relay:
                go(rcopy(sb.at[t, i], rp.at[t, col], ps.at[t, i], pr.at[t, col], pp[t]))
                continue
            if t < 2:
                go(rcopy(sb.at[t, i, pl.ds(0, ra), :], rp.at[t, col, pl.ds(0, ra), :], ps.at[t, i], pr.at[t, col], px))
            if t != 1:
                k = t // 2 + 2
                go(rcopy(sb.at[t, i, pl.ds(ra, ra), :], rp.at[k % 3, col, pl.ds(ra, ra), :], ps.at[k, i], pr.at[k, col], py))

    def row_out(t):
        row = 2 * chips[t] + (1 - c)
        grad_w(row)
        for i, col in enumerate(cols):
            go(rcopy(grads.at[row, col], rc.at[t, col], cs.at[t, i], cr.at[t, col], cp))

    def row_own(t):
        grad_w(2 * chips[t] + c)

    def part_arrived(slot, lo, col, k):
        here = rp.at[slot, col, pl.ds(lo, ra), :]
        rcopy(here, here, fsem, pr.at[k, col], cp).wait_recv()
        return rp[slot, col, lo : lo + ra, :].astype(f32)

    def turn(i):
        if not relay:
            return
        col = cols[i]
        ta[i] = (sb[2, i, 0:ra, :].astype(f32) + part_arrived(0, 0, col, 0)).astype(bf)
        go(rcopy(ta.at[i], r2a.at[col], p2s.at[0, i], p2r.at[0, col], py))
        tb[i] = (sb[1, i, ra:, :].astype(f32) + part_arrived(2, ra, col, 2)).astype(bf)
        go(rcopy(tb.at[i], r2b.at[col], p2s.at[1, i], p2r.at[1, col], px))

    def column(i):
        col = cols[i]
        core_arrived(half - 1, col)
        q = grads[d, col].astype(f32) + rc[half - 1, col].astype(f32)
        if not relay:
            for t in range(half - 1):
                here = rp.at[t, col]
                rcopy(here, here, fsem, pr.at[t, col], cp).wait_recv()
                q = q + rp[t, col].astype(f32)
            return q
        rcopy(r2a.at[col], r2a.at[col], fsem, p2r.at[0, col], cp).wait_recv()
        rcopy(r2b.at[col], r2b.at[col], fsem, p2r.at[1, col], cp).wait_recv()
        qa = q[:ra] + part_arrived(1, 0, col, 1) + r2a[col].astype(f32)
        qb = q[ra:] + part_arrived(0, ra, col, 3) + r2b[col].astype(f32)
        return jnp.concatenate([qa, qb], axis=0)

    at_end = (m == 0) | (m == nmp - 1)
    between = (m > 0) & (m < nmp - 1)

    def z_piece(ref, k):
        return ref.at[pl.ds(k * ra, ra), :]

    def z_arrived(way, col):
        for k in (0, 1):
            here = z_piece(rz.at[way, col], k)
            rcopy(here, here, fsem, zr.at[way, col, k], cp).wait_recv()
        return rz[way, col].astype(f32)

    def z_copies(i):
        col = cols[i]
        up = jnp.where(col > m, 1, 0)
        way = 1 - up
        return way, [
            rcopy(z_piece(zs.at[i], k), z_piece(rz.at[way, col], k), z2.at[i, k], zr.at[way, col, k], (d, m + 2 * up - 1))
            for k in (0, 1)
        ]

    def to_z(i, when, chained):
        @pl.when(when)
        def _():
            q = column(i)
            way, copies = z_copies(i)
            if chained:
                q = q + z_arrived(way, cols[i])
            zs[i] = q.astype(bf)
            for x in copies:
                x.start()

    def by_eight(v, mask):
        v = jnp.where(mask[None], v.reshape(EFEAT, PADA, -1), 0.0)
        return (v[:, 0:8] + v[:, 8:16] + v[:, 16:24] + v[:, 24:32]).reshape(EFEAT * 8, -1).astype(bf)

    eight = jnp.where(
        lax.broadcasted_iota(jnp.int32, (EFEAT, EFEAT * 8), 0)
        == lax.broadcasted_iota(jnp.int32, (EFEAT, EFEAT * 8), 1) // 8,
        1.0,
        0.0,
    ).astype(bf)
    tiles = -(-z.win // 256)
    cuts = (0, tiles // 2, tiles)

    def edges_back(part):
        for n in range(cuts[part], cuts[part + 1]):
            count = min(256, z.win - n * 256)
            at = pl.ds(n * 256, count)
            all_rows = lax.broadcasted_iota(jnp.int32, (z.rows, count), 0)
            rt = jnp.where(all_rows == keyw[1:2, at], 1.0, 0.0).astype(bf)
            eights[n, :, 0:count] = by_eight(dot(gbt[...], rt, NN), wio[:, :count] == keyw[0:1, at])
        for n in range(cuts[part], cuts[part + 1]):
            count = min(256, z.win - n * 256)
            geo[m, :, n * 256 : n * 256 + count] = dot(eight, eights[n, :, 0:count], NN).astype(bf)

    def edges_on(s):
        for part in (0, 1):
            edges_on_part(s, part)

    def edges_on_part(s, part):
        lo, hi = 256 * cuts[part], min(256 * cuts[part + 1], z.win)
        for way in (0, 1):
            col = m - s if way == 0 else m + s
            nxt = m + 1 if way == 0 else m - 1
            src = geo.at[col, :, pl.ds(lo, hi - lo)]
            if s:
                pl.when(inside(col))(rcopy(src, src, fsem, ge_r.at[part, col], cp).wait_recv)
            if s < nmp - 1:
                go_if(
                    inside(col) & inside(nxt),
                    rcopy(src, src, ge_s.at[part, s, way], ge_r.at[part, col], (d, nxt)),
                )

    step = min(DXC, hl)

    def state_grad(lo, hi):
        @pl.loop(lo, hi, unroll=2)
        def _(row):
            for q in range(0, hl, step):
                qs = range(q, q + step)
                cc = jnp.concatenate([cmat[row * hl + k] for k in qs], axis=1)
                gacc[...] += dot(cc, rows_of(row, qs), NN)

    def hidden_grad(lo, hi):
        for i in range(nm):
            dm = ds[i * PADA : (i + 1) * PADA]
            for k in range(lo, hi):
                o = dot(dm, bmat[k * 8 : (k + 1) * 8, i * PADA : (i + 1) * PADA, :].reshape(256, HID), NT)
                dpre[k, i * PADA : (i + 1) * PADA, :] = (
                    o * slope[k, i * PADA : (i + 1) * PADA, :].astype(f32)
                ).astype(bf)

    others = range(half - 1)
    row_out(0)
    row_own(0)
    row_out(1)
    plane_out(0, 0)
    row_own(1)
    for t in others[2:]:
        row_out(t)
        plane_out(t - 1, 0)
        row_own(t)
    plane_out(0, 1)
    hidden_grad(0, 8)
    plane_out(half - 2, 0)
    hidden_grad(8, 16)
    gb = dot(
        jnp.concatenate([dpre[k] for k in range(16)], axis=1),
        jnp.concatenate([kron[k] for k in range(16)], axis=1),
        NT,
    ).astype(bf)
    gbt[...] = gb.T
    turn(0)
    for t in others[1:]:
        plane_out(t, 1)
    plane_out(0, 2)
    edges_back(0)
    edges_on_part(0, 0)
    edges_back(1)
    edges_on_part(0, 1)
    turn(1)
    for t in others[1:]:
        plane_out(t, 2)
    plane_out(0, 3)
    row_out(half - 1)
    row_own(half - 1)

    @pl.loop(0, 16, unroll=16)
    def _(k):
        eights[k] = by_eight(dot(featt[...], dpre[k], NN), delta)

    gin = dot(
        jnp.concatenate([eights[k] for k in range(16)], axis=1),
        jnp.concatenate([emat[k] for k in range(16)], axis=1),
        NT,
    )
    gis[d] = gin.reshape(EFEAT, 8, HID).sum(axis=1).astype(bf)
    for i, p in enumerate(dpp):
        go(rcopy(gis.at[d], gis.at[d], gi_s.at[i], gi_r.at[d], p))
    to_z(0, at_end, False)

    gacc[...] = jnp.zeros(gacc.shape, f32)
    state_grad(0, ndp // 2)
    turn(2)
    for t in others[1:]:
        plane_out(t, 3)
    edges_on(1)
    state_grad(ndp // 2, ndp)
    to_z(1, at_end, False)
    to_z(0, between, True)
    gfin = gacc[...] + gfull[:, 0:HID] + gfull[:, HID : 2 * HID]
    for j in range(nmp):
        a = roll(ostate, z.uw * j, 0)
        b = roll(gfin, z.uw * j, z.uw)
        osb[j] = two_up(jnp.where(lane < z.uw, a, b)).astype(bf)
    for i, p in enumerate(zp):
        go(rcopy(osb.at[p[1]], oso.at[m], os_s.at[i], os_r.at[m], p))
    oso[m] = osb[m]

    gi_sum = gis[d].astype(f32)
    for i in range(1, ndp):
        row = (d - i + ndp) % ndp
        rcopy(gis.at[row], gis.at[row], gi_s.at[0], gi_r.at[row], cp).wait_recv()
        gi_sum = gi_sum + gis[row].astype(f32)
    giz_s[...] = gi_sum.astype(bf)
    for i, p in enumerate(zp):
        go(rcopy(giz_s, giz.at[m], gz_s.at[i], gz_r.at[m], p))
    turn(3)
    edges_on(2)
    to_z(2, at_end, False)
    to_z(1, between, True)
    to_z(2, between, True)

    for col in zcols:
        rcopy(oso.at[col], oso.at[col], os_s.at[0], os_r.at[col], cp).wait_recv()
    for j in range(nmp):
        stage2[j * z.rows : (j + 1) * z.rows, :] = one_up(oso[j].astype(f32))
    for i in range(z.mols):
        stage1[i * MA : (i + 1) * MA, :] = stage2[i * PADA : i * PADA + MA, :]
    stage[...] = stage1[...].T
    at_ref[0 : z.uw, :] = stage[0 : z.uw, 0 : z.atoms] * nmrow[...]
    at_ref[z.uw : 2 * z.uw, :] = stage[z.uw : 2 * z.uw, 0 : z.atoms]

    fin[...] = column(nmp - 1)

    for col in zcols:
        rcopy(giz.at[col], giz.at[col], gz_s.at[0], gz_r.at[col], cp).wait_recv()
        gi_sum = gi_sum + giz[col].astype(f32)
    gi_ref[...] = pltpu.roll(gi_sum, HID - d * z.ew, 1)[:, 0 : z.ew]

    @pl.when(m > 0)
    def _():
        fin[...] += z_arrived(0, m)

    @pl.when(m < nmp - 1)
    def _():
        fin[...] += z_arrived(1, m)

    for s in range(2):
        for g in range(3):
            gg_ref[s, g] = fin[wr + 16 * s : wr + 16 * s + il, g * z.uw : (g + 1) * z.uw]
    wtmp[...] = fin[0:wr, :].reshape(hl, rw, HID)
    for r in range(rw):
        go_ref[:, r * HID : (r + 1) * HID] = wtmp[:, r, :]

    edges_on(3)
    for j, lo in enumerate(z.starts):
        first = geo[j, :, 0:128]
        if j:
            first = (first.astype(f32) + geo[j - 1, :, main:].astype(f32)).astype(bf)
        ge_ref[:, lo : lo + 128] = first
        ge_ref[:, lo + 128 : lo + main] = geo[j, :, 128:main]
    if z.edges > z.full:
        ge_ref[:, z.full :] = geo[nmp - 1, :, main : main + z.edges - z.full]
    for i in range(nmp - 1):
        sends.extend(z_copies(i)[1])
    for y in sends:
        y.wait_send()
    for ok, y in maybe:
        pl.when(ok)(y.wait_send)


def whole_step(z, eo, ei, gw, ns, og, live, feat, snd, rcv, msk):
    dma = pltpu.SemaphoreType.DMA
    ndp, nmp, half = z.ndp, z.nmp, z.half
    rows, rb, win = z.rows, z.rb, z.win
    vm = pltpu.VMEM
    ra = rb // 2
    relay = half == 4
    return pl.pallas_call(
        functools.partial(kernel, z),
        out_shape=(
            jax.ShapeDtypeStruct(eo.shape, f32),
            jax.ShapeDtypeStruct(gw.shape, f32),
            jax.ShapeDtypeStruct(ei.shape, f32),
            jax.ShapeDtypeStruct((2 * z.uw, z.atoms), f32),
            jax.ShapeDtypeStruct(feat.shape, bf),
        ),
        in_specs=[pl.BlockSpec(memory_space=vm)] * 6 + [pl.BlockSpec(memory_space=pl.ANY)] + [pl.BlockSpec(memory_space=vm)] * 3,
        out_specs=(pl.BlockSpec(memory_space=vm),) * 5,
        scratch_shapes=[
            vm((ndp, nmp, rb, HID), bf),
            vm((nmp, rows // 2, HID), bf),
            vm((nmp, rows // 2, HID), bf),
            vm((ndp, EFEAT, HID), bf),
            vm((HID, -(-z.atoms // 128) * 128), f32),
            vm((-(-z.atoms // 128) * 128, HID), f32),
            vm((nmp * rows, HID), f32),
            vm((z.hl, z.rw, HID), f32),
            vm((32, HID), f32),
            vm((EFEAT, HID), f32),
            vm((1, z.atoms), f32),
            vm(feat.shape, bf),
            vm((EFEAT, win), bf),
            vm((3, win), jnp.int32),
            vm((rows, 512), bf),
            vm((512, rows), bf),
            vm((512, rows), bf),
            vm((16, 512, 256), bf),
            vm((16, HID, 256), bf),
            vm((16, rows, 256), bf),
            vm((16, 256, rows), bf),
            vm((16, rows, 256), bf),
            vm((HID, rows, HID), bf),
            vm((HID, rows, HID), bf),
            vm((rows, z.nm * HID), bf),
            vm((16, rows, 256), bf),
            vm((rows, HID), f32),
            vm((rows, HID), f32),
            vm((rows, 512), f32),
            vm((max(16, -(-win // 256)), EFEAT * 8, 256), bf),
            vm((ndp, nmp, rb, HID), bf),
            vm((half, nmp, rb, HID), bf),
            vm((half - 1, nmp, rb, HID), bf),
            vm((half - 1, nmp, rb, HID), bf),
            vm((nmp, ra, HID), bf),
            vm((nmp, ra, HID), bf),
            vm((nmp, ra, HID), bf),
            vm((nmp, ra, HID), bf),
            vm((nmp - 1, rb, HID), bf),
            vm((2, nmp, rb, HID), bf),
            vm((rb, HID), f32),
            vm((nmp, rows // 2, HID), bf),
            vm((nmp, rows // 2, HID), bf),
            vm((nmp, EFEAT, win), bf),
            vm((ndp, EFEAT, HID), bf),
            vm((nmp, EFEAT, HID), bf),
            vm((EFEAT, HID), bf),
            dma(()),
            dma((nmp - 1, 2)),
            dma((2, 2)),
            dma((nmp, 2, max(half - 1, 4))),
            dma((2 * nmp * half,)),
            dma((ndp, nmp, 2)),
            dma((nmp - 1,)), dma((nmp,)),
            dma((ndp - 1,)), dma((ndp,)),
            dma((half, nmp)), dma((half, nmp)),
            dma((max(half - 1, 4), nmp)), dma((max(half - 1, 4), nmp)),
            dma((2, nmp)), dma((2, nmp)),
            dma((nmp - 1, 2)), dma((2, nmp, 2)),
            dma((nmp - 1,)), dma((nmp,)),
            dma((2, nmp - 1, 2)), dma((2, nmp)),
            dma((ndp - 1,)), dma((ndp,)),
            dma((nmp - 1,)), dma((nmp,)),
        ],
        compiler_params=pltpu.CompilerParams(
            collective_id=0, has_side_effects=True, vmem_limit_bytes=VMEM_LIMIT
        ),
    )(eo, ei, gw, ns, og, live, feat, snd, rcv, msk)


beta_one = 0.5
beta_two = 0.5
learn_rate = 0.05
decay_rate = 0.01
epsilon = 1e-08


def adam_update(weight, gradient, first_moment, second_moment):
    first_new = beta_one * first_moment + (1.0 - beta_one) * gradient
    second_new = beta_two * second_moment + (1.0 - beta_two) * gradient * gradient
    mean_hat = first_new / (1.0 - beta_one**STEP)
    square_hat = second_new / (1.0 - beta_two**STEP)
    weight_new = weight - learn_rate * (
        mean_hat / (jnp.sqrt(square_hat) + epsilon) + decay_rate * weight
    )
    return (first_new, second_new, weight_new, weight_new.astype(bf))


def finish_kernel(at_ref, ge_ref, *refs):
    gs_uw = at_ref.shape[0] // 2
    ins, outs = refs[:12], refs[12:]
    outs[0][...] = at_ref[0:gs_uw, :]
    outs[1][...] = at_ref[gs_uw:, :]
    outs[2][...] = ge_ref[...].astype(f32)
    for n in range(3):
        new = adam_update(*[r[...] for r in ins[4 * n : 4 * n + 4]])
        for ref, v in zip(outs[3 + 4 * n : 7 + 4 * n], new):
            ref[...] = v


def finish(at, ge, *layers):
    half = jax.ShapeDtypeStruct((at.shape[0] // 2, at.shape[1]), f32)
    results = [half, half, jax.ShapeDtypeStruct(ge.shape, f32)]
    for n in range(3):
        results += [jax.ShapeDtypeStruct(layers[4 * n].shape, t) for t in (f32, f32, f32, bf)]
    return pl.pallas_call(
        finish_kernel,
        out_shape=tuple(results),
        in_specs=[pl.BlockSpec(memory_space=pltpu.VMEM)] * 14,
        out_specs=(pl.BlockSpec(memory_space=pltpu.VMEM),) * 15,
        compiler_params=pltpu.CompilerParams(vmem_limit_bytes=VMEM_LIMIT),
    )(at, ge, *layers)


def body(
    ndp, nmp,
    node_state, edge_feat, sender, receiver, edge_mask, node_mask, out_grad,
    edge_in, edge_out, gru_weight,
    edge_in_m1, edge_in_m2, edge_out_m1, edge_out_m2, gru_m1, gru_m2,
):
    z = Shape(ndp, nmp, node_state, edge_feat, edge_in, edge_out, gru_weight)
    g_out, g_gru, g_in, at, ge = whole_step(
        z, edge_out, edge_in, gru_weight, node_state.T, out_grad.T, node_mask,
        edge_feat, sender, receiver, edge_mask,
    )
    out_state, grad_state, *rest = finish(
        at, ge,
        edge_in, g_in, edge_in_m1, edge_in_m2,
        edge_out, g_out, edge_out_m1, edge_out_m2,
        gru_weight, g_gru, gru_m1, gru_m2,
    )
    return (out_state.T, grad_state.T, *rest)


def solution(mesh):
    ndp, nmp = mesh.shape["dp"], mesh.shape["mp"]
    rows, lanes, gru = P("dp", "mp"), P(None, "dp"), P(None, None, "dp", "mp")
    edge = P("dp")
    return jax.shard_map(
        functools.partial(body, ndp, nmp),
        mesh=mesh,
        in_specs=(
            rows, lanes, edge, edge, edge, edge, rows,
            lanes, rows, gru, lanes, lanes, rows, rows, gru, gru,
        ),
        out_specs=(rows, rows, lanes) + (lanes,) * 4 + (rows,) * 4 + (gru,) * 4,
        check_vma=False,
    )
```

```python
import functools

import jax
import jax.numpy as jnp
from jax import lax
from jax.experimental import pallas as pl
from jax.experimental.pallas import tpu as pltpu
from jax.sharding import PartitionSpec as P

HID = 128
EFEAT = 16
MA = 29
ME = 812
PADA = 32
STEP = 5
DXC = 4
MESH = pl.DeviceIdType.MESH
VMEM_LIMIT = 60 << 20
bf = jnp.bfloat16
f32 = jnp.float32
NT = (((1,), (1,)), ((), ()))
TN = (((0,), (0,)), ((), ()))
NN = (((1,), (0,)), ((), ()))


def dot(a, b, dims):
    return lax.dot_general(a, b, dims, preferred_element_type=f32)


def roll(x, src, dst):
    shift = (dst - src) % HID
    return pltpu.roll(x, shift, 1) if shift else x


def sig(v):
    return 0.5 + 0.5 * jnp.tanh(0.5 * v)


def rcopy(src, dst, ssem, rsem, dev):
    return pltpu.make_async_remote_copy(
        src_ref=src, dst_ref=dst, send_sem=ssem, recv_sem=rsem, device_id=dev, device_id_type=MESH
    )


class Shape:
    def __init__(self, ndp, nmp, node_state, edge_feat, edge_in, edge_out, gru):
        self.ndp, self.nmp, self.half = ndp, nmp, ndp // 2
        self.atoms, self.uw = node_state.shape
        self.edges = edge_feat.shape[1]
        self.mols = self.atoms // MA
        self.nm = self.mols // nmp
        self.rows = self.nm * PADA
        self.hl, self.il, self.ew = edge_out.shape[0], gru.shape[2], edge_in.shape[1]
        self.rw = edge_out.shape[1] // HID
        self.wr = self.hl * self.rw
        self.rb = self.wr + 32
        self.per = self.nm * ME
        self.starts = [self.per * j // 128 * 128 for j in range(nmp)]
        self.bases = [ME * i // 128 * 128 for i in range(self.nm)]
        self.win = self.bases[-1] + 1024
        self.full = self.edges // 128 * 128
        shift = max(self.per * j - s for j, s in enumerate(self.starts))
        assert all(ME * i + shift + ME <= b + 1024 for i, b in enumerate(self.bases))
        assert self.starts[-1] + self.win - 128 == self.full
        assert all(b - a == self.win - 128 for a, b in zip(self.starts, self.starts[1:]))


def kernel(
    z,
    eo_hbm, ei_hbm, gw_hbm, ns_hbm, og_hbm, nm_hbm, feat_hbm, snd_hbm, rcv_hbm, msk_hbm,
    go_ref, gg_ref, gi_ref, at_ref, ge_ref,
    eo_ref, ei_ref, gw_ref, ns_ref, og_ref, nm_ref, feat_ref, snd_ref, rcv_ref, msk_ref,
    wall, xsb, xo, wis, stage, stage1, stage2, wtmp, stmp, itmp, nmrow, featw, keyw,
    featp, featt, gbt, kron, emat, hid, hidt, slope, bmat, cmat, dsb, dpre, gacc, sacc, gfull, eights,
    grads, rc, sb, rp, ta, tb, r2a, r2b, zs, rz, fin, osb, oso, geo, gis, giz, giz_s,
    lsem, fsem, zsem, zfsem, psem, csem, rsem, xs_s, xs_r, wi_s, wi_r,
    cs, cr, ps, pr, p2s, p2r, z2, zr, os_s, os_r, ge_s, ge_r, gi_s, gi_r, gz_s, gz_r,
):
    ndp, nmp, half, nm = z.ndp, z.nmp, z.half, z.nm
    hl, il, wr, rb, rw = z.hl, z.il, z.wr, z.rb, z.rw
    d = lax.axis_index("dp")
    m = lax.axis_index("mp")
    u = d // 2
    c = d % 2
    relay = half == 4
    low = jnp.where(2 * m < nmp, 1, 0)
    side = low * m + (1 - low) * (nmp - 1 - m)
    near = [jnp.where(i <= side, i - 1, i) for i in range(1, nmp)]
    zcols = [low * i + (1 - low) * (nmp - 1 - i) for i in near]
    zp = [(d, col) for col in zcols]
    if relay:
        ux = u + 1 - 2 * (u % 2)
        uy = (u + 2) % half
        ud = (ux + 2) % half
        chips = [ud, ux, uy, u]
        px, py = (2 * ux + c, m), (2 * uy + c, m)
        pp = [px, py]
    else:
        chips = [(u + t) % half for t in range(1, half)] + [u]
        pp = [(2 * v + c, m) for v in chips[:-1]]
    ra = rb // 2
    cp = (2 * u + (1 - c), m)
    dpp = [((d + i) % ndp, m) for i in range(1, ndp)]
    pairs = (
        (eo_hbm, eo_ref), (gw_hbm, gw_ref), (ei_hbm, ei_ref), (ns_hbm, ns_ref), (og_hbm, og_ref), (nm_hbm, nm_ref),
        (feat_hbm, feat_ref), (snd_hbm, snd_ref), (rcv_hbm, rcv_ref), (msk_hbm, msk_ref),
    )
    loads = [pltpu.make_async_copy(a, b, lsem.at[i]) for i, (a, b) in enumerate(pairs)]
    for x in loads:
        x.start()
    bar = pltpu.get_barrier_semaphore()
    near_by = [cp] + pp if relay else dpp
    for p in near_by:
        pl.semaphore_signal(bar, inc=1, device_id=p, device_id_type=MESH)
    for col in (m - 1, m + 1):

        @pl.when((col >= 0) & (col < nmp))
        def _():
            pl.semaphore_signal(bar, inc=1, device_id=(d, col), device_id_type=MESH)

    lane = lax.broadcasted_iota(jnp.int32, (1, HID), 1)

    def two_up(v):
        return jnp.where(lane < 64, v[: z.rows // 2], pltpu.roll(v[z.rows // 2 :], 64, 1))

    def one_up(v):
        return jnp.concatenate([v, pltpu.roll(v, 64, 1)], axis=0)

    for x in loads[:3]:
        x.wait()
    for r in range(rw):
        wtmp[:, r, :] = eo_ref[:, r * HID : (r + 1) * HID]
    wall[d, m, 0:wr, :] = wtmp[...].reshape(wr, HID).astype(bf)
    stmp[...] = jnp.zeros(stmp.shape, f32)
    for s in range(2):
        for g in range(3):
            stmp[16 * s : 16 * s + il, g * z.uw : (g + 1) * z.uw] = gw_ref[s, g]
    wall[d, m, wr:rb, :] = stmp[...].astype(bf)
    itmp[...] = jnp.zeros(itmp.shape, f32)
    itmp[:, 0 : z.ew] = ei_ref[...]
    wis[d] = pltpu.roll(itmp[...], d * z.ew, 1).astype(bf)
    for x in loads[3:6]:
        x.wait()
    stage[...] = jnp.zeros(stage.shape, f32)
    stage[0 : z.uw, 0 : z.atoms] = ns_ref[...].astype(f32)
    nmrow[0, :] = nm_ref[...].astype(f32)
    stage[z.uw : 2 * z.uw, 0 : z.atoms] = og_ref[...] * nmrow[...]
    stage1[...] = stage[...].T
    stage2[...] = jnp.zeros(stage2.shape, f32)
    for i in range(z.mols):
        stage2[i * PADA : i * PADA + MA, :] = stage1[i * MA : (i + 1) * MA, :]
    for j in range(nmp):
        xsb[j] = two_up(stage2[j * z.rows : (j + 1) * z.rows, :]).astype(bf)
    pl.semaphore_wait(bar, len(near_by) + jnp.where(m > 0, 1, 0) + jnp.where(m < nmp - 1, 1, 0))

    sends = []
    maybe = []

    def go(*copies):
        for x in copies:
            x.start()
        sends.extend(copies)

    def go_if(ok, x):
        pl.when(ok)(x.start)
        maybe.append((ok, x))

    def inside(col):
        return (col >= 0) & (col < nmp)

    def w_in_to(n, row, *devs):
        for i, p in enumerate(devs):
            go(rcopy(wis.at[row], wis.at[row], wi_s.at[n + i], wi_r.at[row], p))

    def w_in_from(row):
        rcopy(wis.at[row], wis.at[row], fsem, wi_r.at[row], cp).wait_recv()

    w_in_to(0, d, *(near_by if relay else dpp))

    rows_x = [2 * ux + c, 2 * uy + c] if relay else [2 * v + c for v in chips[:-1]]
    here_cols = [m] + zcols
    turns = [0]

    def piece(row, col, k):
        return wall.at[row, col, pl.ds(k * ra, ra), :]

    def arrived(row, col, k):
        src = piece(row, col, k)
        rcopy(src, src, fsem, rsem.at[row, col, k], cp).wait_recv()

    def give(row, col, k, sem, dev):
        src = piece(row, col, k)
        go(rcopy(src, src, sem, rsem.at[row, col, k], dev))

    def to_core(row, col, k):
        give(row, col, k, csem.at[turns[0]], cp)
        turns[0] += 1

    def push(n, k):
        col = here_cols[n]
        for t in range(len(pp)):
            t = t if k == 0 else len(pp) - 1 - t
            give(d, col, k, psem.at[n, k, t], pp[len(pp) - 1 - t])
        to_core(d, col, k)

    def along_z(n):
        col = here_cols[n]
        for k in (0, 1):
            arrived(d, col, k)
            beyond = m + 1 - 2 * jnp.where(col > m, 1, 0)
            src = piece(d, col, k)
            go_if(inside(beyond), rcopy(src, src, zfsem.at[n - 1, k], rsem.at[d, col, k], (d, beyond)))
            push(n, k)

    def in_plane(n):
        col = here_cols[n]
        if not relay:
            for row in rows_x:
                for k in (0, 1):
                    arrived(row, col, k)
                    to_core(row, col, k)
            return
        for k in (0, 1):
            for t in (k, 1 - k):
                row = rows_x[1 - t]
                arrived(row, col, k)
                if t == k:
                    give(row, col, k, psem.at[n, k, 3], (px, py)[k])
                to_core(row, col, k)

    def from_diagonal(n):
        if relay:
            for k in (0, 1):
                arrived(2 * ud + c, here_cols[n], k)
                to_core(2 * ud + c, here_cols[n], k)

    for k in (0, 1):
        for i, col in enumerate((m - 1, m + 1)):
            src = piece(d, m, k)
            go_if(inside(col), rcopy(src, src, zsem.at[i, k], rsem.at[d, m, k], (d, col)))
        push(0, k)
    xo[m] = xsb[m]

    start = pl.multiple_of(z.per * m // 128 * 128, 128)
    main = z.win - 128
    for x in loads[6:]:
        x.wait()
    featw[:, 0:main] = feat_ref[:, pl.ds(start, main)]
    keys = (snd_ref, rcv_ref, msk_ref)
    for n, ref in enumerate(keys):
        keyw[n, 0:main] = ref[pl.ds(start, main)]

    @pl.when(m < nmp - 1)
    def _():
        after = pl.multiple_of(start + main, 128)
        featw[:, main:] = feat_ref[:, pl.ds(after, 128)]
        for n, ref in enumerate(keys):
            keyw[n, main:] = ref[pl.ds(after, 128)]

    @pl.when(m == nmp - 1)
    def _():
        featw[:, main:] = jnp.zeros((EFEAT, 128), bf)
        keyw[:, main:] = jnp.zeros((3, 128), jnp.int32)
        tail = z.edges - z.full
        if tail:
            featw[:, main : main + tail] = feat_ref[:, z.full :]
            for n, ref in enumerate(keys):
                keyw[n, main : main + tail] = ref[z.full :]

    place = lax.broadcasted_iota(jnp.int32, (1, z.win), 1) + (start - z.per * m)
    valid = (place >= 0) & (place < z.per)
    mol = jnp.zeros((1, z.win), jnp.int32)
    for i in range(1, nm):
        mol = mol + jnp.where(place >= ME * i, PADA, 0)
    keyw[0:1, :] = jnp.where(valid & (keyw[2:3, :] == 1), keyw[0:1, :], -1)
    keyw[1:2, :] = jnp.where(valid, keyw[1:2, :] + mol, -1)

    wio = lax.broadcasted_iota(jnp.int32, (PADA, 1024), 0)

    def permute(i):
        b = z.bases[i]
        st = wio == keyw[0:1, b : b + 1024]
        rt = jnp.where(wio + PADA * i == keyw[1:2, b : b + 1024], 1.0, 0.0).astype(bf)
        ff = featw[:, b : b + 1024].astype(f32)
        for q in range(4):
            zz = jnp.concatenate(
                [jnp.where(st, ff[f : f + 1, :], 0.0).astype(bf) for f in range(4 * q, 4 * q + 4)], axis=0
            )
            featp[i * PADA : (i + 1) * PADA, q * 128 : (q + 1) * 128] = dot(rt, zz, NT).astype(bf)

    for i in range(nm):
        permute(i)

    if relay:
        for n, (v, devs) in enumerate(((ux, (py, cp)), (uy, (cp,)))):
            w_in_from(2 * v + c)
            w_in_to(3 + 2 * n, 2 * v + c, *devs)
    along_z(1)
    in_plane(0)
    fp = featp[...]
    featt[...] = fp.T
    if relay:
        w_in_from(2 * ud + c)
        w_in_to(7, 2 * ud + c, cp)
        for v in (u, ux, uy, ud):
            w_in_from(2 * v + 1 - c)
    else:
        for i in range(1, ndp):
            w_in_from((d - i + ndp) % ndp)
    w_in = wis[...].astype(f32).sum(axis=0).astype(bf)
    delta = (
        lax.broadcasted_iota(jnp.int32, (PADA, 256), 0)
        == lax.broadcasted_iota(jnp.int32, (PADA, 256), 1) % PADA
    )

    @pl.loop(0, 16, unroll=4)
    def _(k):
        e = jnp.where(
            lax.broadcasted_iota(jnp.int32, (HID, 256), 0)
            == k * 8 + lax.broadcasted_iota(jnp.int32, (HID, 256), 1) // PADA,
            1.0,
            0.0,
        ).astype(bf)
        emat[k] = e
        wexp = dot(w_in, e, NN)
        for f in range(EFEAT):
            kron[k, f * PADA : (f + 1) * PADA, :] = jnp.where(delta, wexp[f : f + 1, :], 0.0).astype(bf)


    def hidden(lo):
        @pl.loop(lo, lo + 8, unroll=4)
        def _(k):
            p = dot(fp, kron[k], NN)
            s = sig(p)
            h = p * s
            hid[k] = h.astype(bf)
            hidt[k] = h.T.astype(bf)
            slope[k] = (s + h - h * s).astype(bf)

    along_z(2)
    hidden(0)
    in_plane(1)
    for i, p in enumerate(zp):
        go(rcopy(xsb.at[p[1]], xo.at[m], xs_s.at[i], xs_r.at[m], p))

    along_z(3)
    hidden(8)
    from_diagonal(0)
    in_plane(2)
    from_diagonal(1)

    for col in zcols:
        rcopy(xo.at[col], xo.at[col], xs_s.at[0], xs_r.at[col], cp).wait_recv()
    xf = jnp.zeros((z.rows, HID), f32)
    cf = jnp.zeros((z.rows, HID), f32)
    for j in range(nmp):
        sl = one_up(xo[j].astype(f32))
        here = (lane >= z.uw * j) & (lane < z.uw * (j + 1))
        xf = jnp.where(here, roll(sl, 0, z.uw * j), xf)
        cf = jnp.where(here, roll(sl, z.uw, z.uw * j), cf)
    x = xf.astype(bf)

    def rows_of(row, qs):
        return jnp.concatenate(
            [wall[row, j, q * rw : (q + 1) * rw, :] for q in qs for j in range(nmp)], axis=0
        )

    def make_b(row):
        for q in range(hl // 2):
            o = dot(x, rows_of(row, (2 * q, 2 * q + 1)), NT).astype(bf)
            bmat[row * hl + 2 * q] = o[:, :HID]
            bmat[row * hl + 2 * q + 1] = o[:, HID:]

    sacc[...] = jnp.zeros(sacc.shape, f32)

    def use_row(row):
        make_b(row)
        if hl % 8 == 0:
            parts = [row * (hl // 8) + k for k in range(hl // 8)]
            for i in range(nm):
                at = pl.ds(i * PADA, PADA)
                hm = jnp.concatenate([hid[k, at, :] for k in parts], axis=1)
                sacc[at, :] += dot(hm, bmat[pl.ds(row * hl, hl), at, :].reshape(PADA * hl, HID), NN)

    def from_core(row):
        for col in here_cols:
            for k in (0, 1):
                arrived(row, col, k)
        use_row(row)

    use_row(d)
    in_plane(3)
    for row in rows_x:
        use_row(row)
    from_core(cp[0])
    from_diagonal(2)
    from_diagonal(3)
    if relay:
        use_row(2 * ud + c)
    for row in rows_x + ([2 * ud + c] if relay else []):
        from_core(row + 1 - 2 * c)
    if hl % 8:
        for i in range(nm):
            hm = jnp.concatenate([hid[k, i * PADA : (i + 1) * PADA, :] for k in range(16)], axis=1)
            sacc[i * PADA : (i + 1) * PADA, :] = dot(
                hm, bmat[:, i * PADA : (i + 1) * PADA, :].reshape(PADA * HID, HID), NN
            )
    summed = sacc[...].astype(bf)

    def gru_rows(s, j):
        if il == 16:
            return jnp.concatenate([wall[k, j, wr + 16 * s : wr + 16 * s + 16, :] for k in range(ndp)], axis=0)
        for k in range(ndp):
            gfull[k * il : (k + 1) * il, 0:HID] = wall[k, j, wr + 16 * s : wr + 16 * s + 16, :].astype(f32)[:il]
        return gfull[0:HID, 0:HID].astype(bf)

    wg = [[gru_rows(s, j) for j in range(nmp)] for s in range(2)]

    def gates(a, s):
        outs = [dot(a, wg[s][j], NN) for j in range(nmp)]
        res = []
        for g in range(3):
            t = None
            for j in range(nmp):
                y = roll(outs[j], z.uw * g, z.uw * j)
                here = (lane >= z.uw * j) & (lane < z.uw * (j + 1))
                t = y if t is None else jnp.where(here, y, t)
            res.append(t)
        return res

    gi = gates(summed, 0)
    gs = gates(x, 1)
    reset = sig(gi[0] + gs[0])
    update = sig(gi[1] + gs[1])
    cand = jnp.tanh(gi[2] + reset * gs[2])
    ostate = (1.0 - update) * cand + update * xf
    dc = cf * (1.0 - update) * (1.0 - cand * cand)
    du = cf * (xf - cand) * update * (1.0 - update)
    dr = dc * gs[2] * reset * (1.0 - reset)

    def pack(gl, j):
        t = jnp.zeros((z.rows, HID), f32)
        for g in range(3):
            here = (lane >= z.uw * g) & (lane < z.uw * (g + 1))
            t = jnp.where(here, roll(gl[g], z.uw * j, z.uw * g), t)
        return t.astype(bf)

    al = [pack([dr, du, dc], j) for j in range(nmp)]
    bl = [pack([dr, du, dc * reset], j) for j in range(nmp)]
    ds = dot(jnp.concatenate(al, axis=1), jnp.concatenate(wg[0], axis=1), NT).astype(bf)
    gfull[:, HID : 2 * HID] = cf * update
    gfull[:, 0:HID] = dot(jnp.concatenate(bl, axis=1), jnp.concatenate(wg[1], axis=1), NT)
    for j in range(nmp):
        for s, (l, r) in enumerate(((summed, al[j]), (x, bl[j]))):
            gg = dot(l, r, TN)
            for k in range(ndp):
                part = gg[k * il : (k + 1) * il]
                if il < 16:
                    part = jnp.concatenate([part, jnp.zeros((16 - il, HID), f32)], axis=0)
                grads[k, j, wr + 16 * s : wr + 16 * s + 16, :] = part.astype(bf)

    dsb[...] = jnp.zeros(dsb.shape, bf)
    for i in range(nm):
        dsb[i * PADA : (i + 1) * PADA, i * HID : (i + 1) * HID] = ds[i * PADA : (i + 1) * PADA]

    def c_block(k):
        for p in range(nm // 2):
            o = dot(hidt[k], dsb[:, p * 256 : (p + 1) * 256], NN).astype(bf)
            for i in range(2):
                at = (2 * p + i) * PADA
                cmat[pl.ds(k * 8, 8), at : at + PADA, :] = o[:, i * HID : (i + 1) * HID].reshape(8, PADA, HID)

    if hl % 8:
        pl.loop(0, 16, unroll=8)(c_block)

    def grad_w(row):
        for k in range(hl // 8):
            c_block(row * (hl // 8) + k)
        for q in range(hl):
            o = dot(cmat[row * hl + q], x, TN).astype(bf)
            for j in range(nmp):
                grads[row, j, q * rw : (q + 1) * rw, :] = o[rw * j : rw * (j + 1)]

    cols = zcols[::-1] + [m]

    def core_arrived(t, col):
        rcopy(rc.at[t, col], rc.at[t, col], fsem, cr.at[t, col], cp).wait_recv()

    def plane_out(t, *which):
        row = 2 * chips[t] + c
        for i in which:
            col = cols[i]
            core_arrived(t, col)
            sb[t, i] = (grads[row, col].astype(f32) + rc[t, col].astype(f32)).astype(bf)
            if not relay:
                go(rcopy(sb.at[t, i], rp.at[t, col], ps.at[t, i], pr.at[t, col], pp[t]))
                continue
            if t < 2:
                go(rcopy(sb.at[t, i, pl.ds(0, ra), :], rp.at[t, col, pl.ds(0, ra), :], ps.at[t, i], pr.at[t, col], px))
            if t != 1:
                k = t // 2 + 2
                go(rcopy(sb.at[t, i, pl.ds(ra, ra), :], rp.at[k % 3, col, pl.ds(ra, ra), :], ps.at[k, i], pr.at[k, col], py))

    def row_out(t):
        row = 2 * chips[t] + (1 - c)
        grad_w(row)
        for i, col in enumerate(cols):
            go(rcopy(grads.at[row, col], rc.at[t, col], cs.at[t, i], cr.at[t, col], cp))

    def row_own(t):
        grad_w(2 * chips[t] + c)

    def part_arrived(slot, lo, col, k):
        here = rp.at[slot, col, pl.ds(lo, ra), :]
        rcopy(here, here, fsem, pr.at[k, col], cp).wait_recv()
        return rp[slot, col, lo : lo + ra, :].astype(f32)

    def turn(i):
        if not relay:
            return
        col = cols[i]
        ta[i] = (sb[2, i, 0:ra, :].astype(f32) + part_arrived(0, 0, col, 0)).astype(bf)
        go(rcopy(ta.at[i], r2a.at[col], p2s.at[0, i], p2r.at[0, col], py))
        tb[i] = (sb[1, i, ra:, :].astype(f32) + part_arrived(2, ra, col, 2)).astype(bf)
        go(rcopy(tb.at[i], r2b.at[col], p2s.at[1, i], p2r.at[1, col], px))

    def column(i):
        col = cols[i]
        core_arrived(half - 1, col)
        q = grads[d, col].astype(f32) + rc[half - 1, col].astype(f32)
        if not relay:
            for t in range(half - 1):
                here = rp.at[t, col]
                rcopy(here, here, fsem, pr.at[t, col], cp).wait_recv()
                q = q + rp[t, col].astype(f32)
            return q
        rcopy(r2a.at[col], r2a.at[col], fsem, p2r.at[0, col], cp).wait_recv()
        rcopy(r2b.at[col], r2b.at[col], fsem, p2r.at[1, col], cp).wait_recv()
        qa = q[:ra] + part_arrived(1, 0, col, 1) + r2a[col].astype(f32)
        qb = q[ra:] + part_arrived(0, ra, col, 3) + r2b[col].astype(f32)
        return jnp.concatenate([qa, qb], axis=0)

    at_end = (m == 0) | (m == nmp - 1)
    between = (m > 0) & (m < nmp - 1)

    def z_piece(ref, k):
        return ref.at[pl.ds(k * ra, ra), :]

    def z_arrived(way, col):
        for k in (0, 1):
            here = z_piece(rz.at[way, col], k)
            rcopy(here, here, fsem, zr.at[way, col, k], cp).wait_recv()
        return rz[way, col].astype(f32)

    def z_copies(i):
        col = cols[i]
        up = jnp.where(col > m, 1, 0)
        way = 1 - up
        return way, [
            rcopy(z_piece(zs.at[i], k), z_piece(rz.at[way, col], k), z2.at[i, k], zr.at[way, col, k], (d, m + 2 * up - 1))
            for k in (0, 1)
        ]

    def to_z(i, when, chained):
        @pl.when(when)
        def _():
            q = column(i)
            way, copies = z_copies(i)
            if chained:
                q = q + z_arrived(way, cols[i])
            zs[i] = q.astype(bf)
            for x in copies:
                x.start()

    def by_eight(v, mask):
        v = jnp.where(mask[None], v.reshape(EFEAT, PADA, -1), 0.0)
        return (v[:, 0:8] + v[:, 8:16] + v[:, 16:24] + v[:, 24:32]).reshape(EFEAT * 8, -1).astype(bf)

    eight = jnp.where(
        lax.broadcasted_iota(jnp.int32, (EFEAT, EFEAT * 8), 0)
        == lax.broadcasted_iota(jnp.int32, (EFEAT, EFEAT * 8), 1) // 8,
        1.0,
        0.0,
    ).astype(bf)
    tiles = -(-z.win // 256)
    cuts = (0, tiles // 2, tiles)

    def edges_back(part):
        for n in range(cuts[part], cuts[part + 1]):
            count = min(256, z.win - n * 256)
            at = pl.ds(n * 256, count)
            all_rows = lax.broadcasted_iota(jnp.int32, (z.rows, count), 0)
            rt = jnp.where(all_rows == keyw[1:2, at], 1.0, 0.0).astype(bf)
            eights[n, :, 0:count] = by_eight(dot(gbt[...], rt, NN), wio[:, :count] == keyw[0:1, at])
        for n in range(cuts[part], cuts[part + 1]):
            count = min(256, z.win - n * 256)
            geo[m, :, n * 256 : n * 256 + count] = dot(eight, eights[n, :, 0:count], NN).astype(bf)

    def edges_on(s):
        for part in (0, 1):
            edges_on_part(s, part)

    def edges_on_part(s, part):
        lo, hi = 256 * cuts[part], min(256 * cuts[part + 1], z.win)
        for way in (0, 1):
            col = m - s if way == 0 else m + s
            nxt = m + 1 if way == 0 else m - 1
            src = geo.at[col, :, pl.ds(lo, hi - lo)]
            if s:
                pl.when(inside(col))(rcopy(src, src, fsem, ge_r.at[part, col], cp).wait_recv)
            if s < nmp - 1:
                go_if(
                    inside(col) & inside(nxt),
                    rcopy(src, src, ge_s.at[part, s, way], ge_r.at[part, col], (d, nxt)),
                )

    step = min(DXC, hl)

    def state_grad(lo, hi):
        @pl.loop(lo, hi, unroll=2)
        def _(row):
            for q in range(0, hl, step):
                qs = range(q, q + step)
                cc = jnp.concatenate([cmat[row * hl + k] for k in qs], axis=1)
                gacc[...] += dot(cc, rows_of(row, qs), NN)

    def hidden_grad(lo, hi):
        for i in range(nm):
            dm = ds[i * PADA : (i + 1) * PADA]
            for k in range(lo, hi):
                o = dot(dm, bmat[k * 8 : (k + 1) * 8, i * PADA : (i + 1) * PADA, :].reshape(256, HID), NT)
                dpre[k, i * PADA : (i + 1) * PADA, :] = (
                    o * slope[k, i * PADA : (i + 1) * PADA, :].astype(f32)
                ).astype(bf)

    others = range(half - 1)
    row_out(0)
    row_own(0)
    row_out(1)
    plane_out(0, 0)
    row_own(1)
    for t in others[2:]:
        row_out(t)
        plane_out(t - 1, 0)
        row_own(t)
    plane_out(0, 1)
    hidden_grad(0, 8)
    plane_out(half - 2, 0)
    hidden_grad(8, 16)
    gb = dot(
        jnp.concatenate([dpre[k] for k in range(16)], axis=1),
        jnp.concatenate([kron[k] for k in range(16)], axis=1),
        NT,
    ).astype(bf)
    gbt[...] = gb.T
    turn(0)
    for t in others[1:]:
        plane_out(t, 1)
    plane_out(0, 2)
    edges_back(0)
    edges_on_part(0, 0)
    edges_back(1)
    edges_on_part(0, 1)
    turn(1)
    for t in others[1:]:
        plane_out(t, 2)
    plane_out(0, 3)
    row_out(half - 1)
    row_own(half - 1)

    @pl.loop(0, 16, unroll=16)
    def _(k):
        eights[k] = by_eight(dot(featt[...], dpre[k], NN), delta)

    gin = dot(
        jnp.concatenate([eights[k] for k in range(16)], axis=1),
        jnp.concatenate([emat[k] for k in range(16)], axis=1),
        NT,
    )
    gis[d] = gin.reshape(EFEAT, 8, HID).sum(axis=1).astype(bf)
    for i, p in enumerate(dpp):
        go(rcopy(gis.at[d], gis.at[d], gi_s.at[i], gi_r.at[d], p))
    to_z(0, at_end, False)

    gacc[...] = jnp.zeros(gacc.shape, f32)
    state_grad(0, ndp // 2)
    turn(2)
    for t in others[1:]:
        plane_out(t, 3)
    edges_on(1)
    state_grad(ndp // 2, ndp)
    gfin = gacc[...] + gfull[:, 0:HID] + gfull[:, HID : 2 * HID]
    for j in range(nmp):
        a = roll(ostate, z.uw * j, 0)
        b = roll(gfin, z.uw * j, z.uw)
        osb[j] = two_up(jnp.where(lane < z.uw, a, b)).astype(bf)
    for i, p in enumerate(zp):
        go(rcopy(osb.at[p[1]], oso.at[m], os_s.at[i], os_r.at[m], p))
    oso[m] = osb[m]

    to_z(1, at_end, False)
    to_z(0, between, True)
    gi_sum = gis[d].astype(f32)
    for i in range(1, ndp):
        row = (d - i + ndp) % ndp
        rcopy(gis.at[row], gis.at[row], gi_s.at[0], gi_r.at[row], cp).wait_recv()
        gi_sum = gi_sum + gis[row].astype(f32)
    giz_s[...] = gi_sum.astype(bf)
    for i, p in enumerate(zp):
        go(rcopy(giz_s, giz.at[m], gz_s.at[i], gz_r.at[m], p))
    turn(3)
    edges_on(2)
    to_z(2, at_end, False)
    to_z(1, between, True)
    to_z(2, between, True)

    for col in zcols:
        rcopy(oso.at[col], oso.at[col], os_s.at[0], os_r.at[col], cp).wait_recv()
    for j in range(nmp):
        stage2[j * z.rows : (j + 1) * z.rows, :] = one_up(oso[j].astype(f32))
    for i in range(z.mols):
        stage1[i * MA : (i + 1) * MA, :] = stage2[i * PADA : i * PADA + MA, :]
    stage[...] = stage1[...].T
    at_ref[0 : z.uw, :] = stage[0 : z.uw, 0 : z.atoms] * nmrow[...]
    at_ref[z.uw : 2 * z.uw, :] = stage[z.uw : 2 * z.uw, 0 : z.atoms]

    fin[...] = column(nmp - 1)

    for col in zcols:
        rcopy(giz.at[col], giz.at[col], gz_s.at[0], gz_r.at[col], cp).wait_recv()
        gi_sum = gi_sum + giz[col].astype(f32)
    gi_ref[...] = pltpu.roll(gi_sum, HID - d * z.ew, 1)[:, 0 : z.ew]

    @pl.when(m > 0)
    def _():
        fin[...] += z_arrived(0, m)

    @pl.when(m < nmp - 1)
    def _():
        fin[...] += z_arrived(1, m)

    for s in range(2):
        for g in range(3):
            gg_ref[s, g] = fin[wr + 16 * s : wr + 16 * s + il, g * z.uw : (g + 1) * z.uw]
    wtmp[...] = fin[0:wr, :].reshape(hl, rw, HID)
    for r in range(rw):
        go_ref[:, r * HID : (r + 1) * HID] = wtmp[:, r, :]

    edges_on(3)
    for j, lo in enumerate(z.starts):
        first = geo[j, :, 0:128]
        if j:
            first = (first.astype(f32) + geo[j - 1, :, main:].astype(f32)).astype(bf)
        ge_ref[:, lo : lo + 128] = first
        ge_ref[:, lo + 128 : lo + main] = geo[j, :, 128:main]
    if z.edges > z.full:
        ge_ref[:, z.full :] = geo[nmp - 1, :, main : main + z.edges - z.full]
    for i in range(nmp - 1):
        sends.extend(z_copies(i)[1])
    for y in sends:
        y.wait_send()
    for ok, y in maybe:
        pl.when(ok)(y.wait_send)


def whole_step(z, eo, ei, gw, ns, og, live, feat, snd, rcv, msk):
    dma = pltpu.SemaphoreType.DMA
    ndp, nmp, half = z.ndp, z.nmp, z.half
    rows, rb, win = z.rows, z.rb, z.win
    vm = pltpu.VMEM
    ra = rb // 2
    relay = half == 4
    return pl.pallas_call(
        functools.partial(kernel, z),
        out_shape=(
            jax.ShapeDtypeStruct(eo.shape, f32),
            jax.ShapeDtypeStruct(gw.shape, f32),
            jax.ShapeDtypeStruct(ei.shape, f32),
            jax.ShapeDtypeStruct((2 * z.uw, z.atoms), f32),
            jax.ShapeDtypeStruct(feat.shape, bf),
        ),
        in_specs=[pl.BlockSpec(memory_space=pl.ANY)] * 10,
        out_specs=(pl.BlockSpec(memory_space=vm),) * 5,
        scratch_shapes=[
            *(vm(a.shape, a.dtype) for a in (eo, ei, gw, ns, og, live, feat, snd, rcv, msk)),
            vm((ndp, nmp, rb, HID), bf),
            vm((nmp, rows // 2, HID), bf),
            vm((nmp, rows // 2, HID), bf),
            vm((ndp, EFEAT, HID), bf),
            vm((HID, -(-z.atoms // 128) * 128), f32),
            vm((-(-z.atoms // 128) * 128, HID), f32),
            vm((nmp * rows, HID), f32),
            vm((z.hl, z.rw, HID), f32),
            vm((32, HID), f32),
            vm((EFEAT, HID), f32),
            vm((1, z.atoms), f32),
            vm((EFEAT, win), bf),
            vm((3, win), jnp.int32),
            vm((rows, 512), bf),
            vm((512, rows), bf),
            vm((512, rows), bf),
            vm((16, 512, 256), bf),
            vm((16, HID, 256), bf),
            vm((16, rows, 256), bf),
            vm((16, 256, rows), bf),
            vm((16, rows, 256), bf),
            vm((HID, rows, HID), bf),
            vm((HID, rows, HID), bf),
            vm((rows, z.nm * HID), bf),
            vm((16, rows, 256), bf),
            vm((rows, HID), f32),
            vm((rows, HID), f32),
            vm((rows, 512), f32),
            vm((max(16, -(-win // 256)), EFEAT * 8, 256), bf),
            vm((ndp, nmp, rb, HID), bf),
            vm((half, nmp, rb, HID), bf),
            vm((half - 1, nmp, rb, HID), bf),
            vm((half - 1, nmp, rb, HID), bf),
            vm((nmp, ra, HID), bf),
            vm((nmp, ra, HID), bf),
            vm((nmp, ra, HID), bf),
            vm((nmp, ra, HID), bf),
            vm((nmp - 1, rb, HID), bf),
            vm((2, nmp, rb, HID), bf),
            vm((rb, HID), f32),
            vm((nmp, rows // 2, HID), bf),
            vm((nmp, rows // 2, HID), bf),
            vm((nmp, EFEAT, win), bf),
            vm((ndp, EFEAT, HID), bf),
            vm((nmp, EFEAT, HID), bf),
            vm((EFEAT, HID), bf),
            dma((10,)),
            dma(()),
            dma((nmp - 1, 2)),
            dma((nmp - 1, 2)),
            dma((nmp, 2, max(half - 1, 4))),
            dma((2 * nmp * half,)),
            dma((ndp, nmp, 2)),
            dma((nmp - 1,)), dma((nmp,)),
            dma((max(ndp - 1, 8),)), dma((ndp,)),
            dma((half, nmp)), dma((half, nmp)),
            dma((max(half - 1, 4), nmp)), dma((max(half - 1, 4), nmp)),
            dma((2, nmp)), dma((2, nmp)),
            dma((nmp - 1, 2)), dma((2, nmp, 2)),
            dma((nmp - 1,)), dma((nmp,)),
            dma((2, nmp - 1, 2)), dma((2, nmp)),
            dma((ndp - 1,)), dma((ndp,)),
            dma((nmp - 1,)), dma((nmp,)),
        ],
        compiler_params=pltpu.CompilerParams(
            collective_id=0, has_side_effects=True, vmem_limit_bytes=VMEM_LIMIT
        ),
    )(eo, ei, gw, ns, og, live, feat, snd, rcv, msk)


beta_one = 0.5
beta_two = 0.5
learn_rate = 0.05
decay_rate = 0.01
epsilon = 1e-08


def adam_update(weight, gradient, first_moment, second_moment):
    first_new = beta_one * first_moment + (1.0 - beta_one) * gradient
    second_new = beta_two * second_moment + (1.0 - beta_two) * gradient * gradient
    mean_hat = first_new / (1.0 - beta_one**STEP)
    square_hat = second_new / (1.0 - beta_two**STEP)
    weight_new = weight - learn_rate * (
        mean_hat / (jnp.sqrt(square_hat) + epsilon) + decay_rate * weight
    )
    return (first_new, second_new, weight_new, weight_new.astype(bf))


def finish_kernel(at_ref, ge_ref, *refs):
    gs_uw = at_ref.shape[0] // 2
    ins, outs = refs[:12], refs[12:]
    outs[0][...] = at_ref[0:gs_uw, :]
    outs[1][...] = at_ref[gs_uw:, :]
    outs[2][...] = ge_ref[...].astype(f32)
    for n in range(3):
        new = adam_update(*[r[...] for r in ins[4 * n : 4 * n + 4]])
        for ref, v in zip(outs[3 + 4 * n : 7 + 4 * n], new):
            ref[...] = v


def finish(at, ge, *layers):
    half = jax.ShapeDtypeStruct((at.shape[0] // 2, at.shape[1]), f32)
    results = [half, half, jax.ShapeDtypeStruct(ge.shape, f32)]
    for n in range(3):
        results += [jax.ShapeDtypeStruct(layers[4 * n].shape, t) for t in (f32, f32, f32, bf)]
    return pl.pallas_call(
        finish_kernel,
        out_shape=tuple(results),
        in_specs=[pl.BlockSpec(memory_space=pltpu.VMEM)] * 14,
        out_specs=(pl.BlockSpec(memory_space=pltpu.VMEM),) * 15,
        compiler_params=pltpu.CompilerParams(vmem_limit_bytes=VMEM_LIMIT),
    )(at, ge, *layers)


def body(
    ndp, nmp,
    node_state, edge_feat, sender, receiver, edge_mask, node_mask, out_grad,
    edge_in, edge_out, gru_weight,
    edge_in_m1, edge_in_m2, edge_out_m1, edge_out_m2, gru_m1, gru_m2,
):
    z = Shape(ndp, nmp, node_state, edge_feat, edge_in, edge_out, gru_weight)
    g_out, g_gru, g_in, at, ge = whole_step(
        z, edge_out, edge_in, gru_weight, node_state.T, out_grad.T, node_mask,
        edge_feat, sender, receiver, edge_mask,
    )
    out_state, grad_state, *rest = finish(
        at, ge,
        edge_in, g_in, edge_in_m1, edge_in_m2,
        edge_out, g_out, edge_out_m1, edge_out_m2,
        gru_weight, g_gru, gru_m1, gru_m2,
    )
    return (out_state.T, grad_state.T, *rest)


def solution(mesh):
    ndp, nmp = mesh.shape["dp"], mesh.shape["mp"]
    rows, lanes, gru = P("dp", "mp"), P(None, "dp"), P(None, None, "dp", "mp")
    edge = P("dp")
    return jax.shard_map(
        functools.partial(body, ndp, nmp),
        mesh=mesh,
        in_specs=(
            rows, lanes, edge, edge, edge, edge, rows,
            lanes, rows, gru, lanes, lanes, rows, rows, gru, gru,
        ),
        out_specs=(rows, rows, lanes) + (lanes,) * 4 + (rows,) * 4 + (gru,) * 4,
        check_vma=False,
    )
```

```python
import functools

import jax
import jax.numpy as jnp
from jax import lax
from jax.experimental import pallas as pl
from jax.experimental.pallas import tpu as pltpu
from jax.sharding import PartitionSpec as P

HID = 128
EFEAT = 16
MA = 29
ME = 812
PADA = 32
STEP = 5
DXC = 4
MESH = pl.DeviceIdType.MESH
VMEM_LIMIT = 60 << 20
bf = jnp.bfloat16
f32 = jnp.float32
NT = (((1,), (1,)), ((), ()))
TN = (((0,), (0,)), ((), ()))
NN = (((1,), (0,)), ((), ()))


def dot(a, b, dims):
    return lax.dot_general(a, b, dims, preferred_element_type=f32)


def roll(x, src, dst):
    shift = (dst - src) % HID
    return pltpu.roll(x, shift, 1) if shift else x


def sig(v):
    return 0.5 + 0.5 * jnp.tanh(0.5 * v)


def rcopy(src, dst, ssem, rsem, dev):
    return pltpu.make_async_remote_copy(
        src_ref=src, dst_ref=dst, send_sem=ssem, recv_sem=rsem, device_id=dev, device_id_type=MESH
    )


class Shape:
    def __init__(self, ndp, nmp, node_state, edge_feat, edge_in, edge_out, gru):
        self.ndp, self.nmp, self.half = ndp, nmp, ndp // 2
        self.atoms, self.uw = node_state.shape
        self.edges = edge_feat.shape[1]
        self.mols = self.atoms // MA
        self.nm = self.mols // nmp
        self.rows = self.nm * PADA
        self.hl, self.il, self.ew = edge_out.shape[0], gru.shape[2], edge_in.shape[1]
        self.rw = edge_out.shape[1] // HID
        self.wr = self.hl * self.rw
        self.rb = self.wr + 32
        self.per = self.nm * ME
        self.starts = [self.per * j // 128 * 128 for j in range(nmp)]
        self.bases = [ME * i // 128 * 128 for i in range(self.nm)]
        self.win = self.bases[-1] + 1024
        self.full = self.edges // 128 * 128
        shift = max(self.per * j - s for j, s in enumerate(self.starts))
        assert all(ME * i + shift + ME <= b + 1024 for i, b in enumerate(self.bases))
        assert self.starts[-1] + self.win - 128 == self.full
        assert all(b - a == self.win - 128 for a, b in zip(self.starts, self.starts[1:]))


def kernel(
    z,
    eo_hbm, ei_hbm, gw_hbm, ns_hbm, og_hbm, nm_hbm, feat_hbm, snd_hbm, rcv_hbm, msk_hbm,
    go_ref, gg_ref, gi_ref, at_hbm, ge_hbm,
    at_ref, ge_ref,
    eo_ref, ei_ref, gw_ref, ns_ref, og_ref, nm_ref, feat_ref, snd_ref, rcv_ref, msk_ref,
    wall, xsb, xo, wis, stage, stage1, stage2, wtmp, stmp, itmp, nmrow, featw, keyw,
    featp, featt, gbt, kron, emat, hid, hidt, slope, bmat, cmat, dsb, dpre, gacc, sacc, gfull, eights,
    grads, rc, sb, rp, ta, tb, r2a, r2b, zs, rz, fin, osb, oso, geo, gis, giz, giz_s,
    lsem, fsem, zsem, zfsem, psem, csem, rsem, xs_s, xs_r, wi_s, wi_r,
    cs, cr, ps, pr, p2s, p2r, z2, zr, os_s, os_r, ge_s, ge_r, gi_s, gi_r, gz_s, gz_r,
):
    ndp, nmp, half, nm = z.ndp, z.nmp, z.half, z.nm
    hl, il, wr, rb, rw = z.hl, z.il, z.wr, z.rb, z.rw
    d = lax.axis_index("dp")
    m = lax.axis_index("mp")
    u = d // 2
    c = d % 2
    relay = half == 4
    low = jnp.where(2 * m < nmp, 1, 0)
    side = low * m + (1 - low) * (nmp - 1 - m)
    near = [jnp.where(i <= side, i - 1, i) for i in range(1, nmp)]
    zcols = [low * i + (1 - low) * (nmp - 1 - i) for i in near]
    zp = [(d, col) for col in zcols]
    if relay:
        ux = u + 1 - 2 * (u % 2)
        uy = (u + 2) % half
        ud = (ux + 2) % half
        chips = [ud, ux, uy, u]
        px, py = (2 * ux + c, m), (2 * uy + c, m)
        pp = [px, py]
    else:
        chips = [(u + t) % half for t in range(1, half)] + [u]
        pp = [(2 * v + c, m) for v in chips[:-1]]
    ra = rb // 2
    cp = (2 * u + (1 - c), m)
    dpp = [((d + i) % ndp, m) for i in range(1, ndp)]
    pairs = (
        (eo_hbm, eo_ref), (gw_hbm, gw_ref), (ei_hbm, ei_ref), (ns_hbm, ns_ref), (og_hbm, og_ref), (nm_hbm, nm_ref),
        (feat_hbm, feat_ref), (snd_hbm, snd_ref), (rcv_hbm, rcv_ref), (msk_hbm, msk_ref),
    )
    loads = [pltpu.make_async_copy(a, b, lsem.at[i]) for i, (a, b) in enumerate(pairs)]
    for x in loads:
        x.start()
    bar = pltpu.get_barrier_semaphore()
    near_by = [cp] + pp if relay else dpp
    for p in near_by:
        pl.semaphore_signal(bar, inc=1, device_id=p, device_id_type=MESH)
    for col in (m - 1, m + 1):

        @pl.when((col >= 0) & (col < nmp))
        def _():
            pl.semaphore_signal(bar, inc=1, device_id=(d, col), device_id_type=MESH)

    lane = lax.broadcasted_iota(jnp.int32, (1, HID), 1)

    def two_up(v):
        return jnp.where(lane < 64, v[: z.rows // 2], pltpu.roll(v[z.rows // 2 :], 64, 1))

    def one_up(v):
        return jnp.concatenate([v, pltpu.roll(v, 64, 1)], axis=0)

    for x in loads[:3]:
        x.wait()
    for r in range(rw):
        wtmp[:, r, :] = eo_ref[:, r * HID : (r + 1) * HID]
    wall[d, m, 0:wr, :] = wtmp[...].reshape(wr, HID).astype(bf)
    stmp[...] = jnp.zeros(stmp.shape, f32)
    for s in range(2):
        for g in range(3):
            stmp[16 * s : 16 * s + il, g * z.uw : (g + 1) * z.uw] = gw_ref[s, g]
    wall[d, m, wr:rb, :] = stmp[...].astype(bf)
    itmp[...] = jnp.zeros(itmp.shape, f32)
    itmp[:, 0 : z.ew] = ei_ref[...]
    wis[d] = pltpu.roll(itmp[...], d * z.ew, 1).astype(bf)
    for x in loads[3:6]:
        x.wait()
    stage[...] = jnp.zeros(stage.shape, f32)
    stage[0 : z.uw, 0 : z.atoms] = ns_ref[...].astype(f32)
    nmrow[0, :] = nm_ref[...].astype(f32)
    stage[z.uw : 2 * z.uw, 0 : z.atoms] = og_ref[...] * nmrow[...]
    stage1[...] = stage[...].T
    stage2[...] = jnp.zeros(stage2.shape, f32)
    for i in range(z.mols):
        stage2[i * PADA : i * PADA + MA, :] = stage1[i * MA : (i + 1) * MA, :]
    for j in range(nmp):
        xsb[j] = two_up(stage2[j * z.rows : (j + 1) * z.rows, :]).astype(bf)
    pl.semaphore_wait(bar, len(near_by) + jnp.where(m > 0, 1, 0) + jnp.where(m < nmp - 1, 1, 0))

    sends = []
    maybe = []

    def go(*copies):
        for x in copies:
            x.start()
        sends.extend(copies)

    def go_if(ok, x):
        pl.when(ok)(x.start)
        maybe.append((ok, x))

    def inside(col):
        return (col >= 0) & (col < nmp)

    def w_in_to(n, row, *devs):
        for i, p in enumerate(devs):
            go(rcopy(wis.at[row], wis.at[row], wi_s.at[n + i], wi_r.at[row], p))

    def w_in_from(row):
        rcopy(wis.at[row], wis.at[row], fsem, wi_r.at[row], cp).wait_recv()

    w_in_to(0, d, *(near_by if relay else dpp))

    rows_x = [2 * ux + c, 2 * uy + c] if relay else [2 * v + c for v in chips[:-1]]
    here_cols = [m] + zcols
    turns = [0]

    def piece(row, col, k):
        return wall.at[row, col, pl.ds(k * ra, ra), :]

    def arrived(row, col, k):
        src = piece(row, col, k)
        rcopy(src, src, fsem, rsem.at[row, col, k], cp).wait_recv()

    def give(row, col, k, sem, dev):
        src = piece(row, col, k)
        go(rcopy(src, src, sem, rsem.at[row, col, k], dev))

    def to_core(row, col, k):
        give(row, col, k, csem.at[turns[0]], cp)
        turns[0] += 1

    def push(n, k):
        col = here_cols[n]
        for t in range(len(pp)):
            t = t if k == 0 else len(pp) - 1 - t
            give(d, col, k, psem.at[n, k, t], pp[len(pp) - 1 - t])
        to_core(d, col, k)

    def along_z(n):
        col = here_cols[n]
        for k in (0, 1):
            arrived(d, col, k)
            beyond = m + 1 - 2 * jnp.where(col > m, 1, 0)
            src = piece(d, col, k)
            go_if(inside(beyond), rcopy(src, src, zfsem.at[n - 1, k], rsem.at[d, col, k], (d, beyond)))
            push(n, k)

    def in_plane(n):
        col = here_cols[n]
        if not relay:
            for row in rows_x:
                for k in (0, 1):
                    arrived(row, col, k)
                    to_core(row, col, k)
            return
        for k in (0, 1):
            for t in (k, 1 - k):
                row = rows_x[1 - t]
                arrived(row, col, k)
                if t == k:
                    give(row, col, k, psem.at[n, k, 3], (px, py)[k])
                to_core(row, col, k)

    def from_diagonal(n):
        if relay:
            for k in (0, 1):
                arrived(2 * ud + c, here_cols[n], k)
                to_core(2 * ud + c, here_cols[n], k)

    for k in (0, 1):
        for i, col in enumerate((m - 1, m + 1)):
            src = piece(d, m, k)
            go_if(inside(col), rcopy(src, src, zsem.at[i, k], rsem.at[d, m, k], (d, col)))
        push(0, k)
    xo[m] = xsb[m]

    start = pl.multiple_of(z.per * m // 128 * 128, 128)
    main = z.win - 128
    for x in loads[6:]:
        x.wait()
    featw[:, 0:main] = feat_ref[:, pl.ds(start, main)]
    keys = (snd_ref, rcv_ref, msk_ref)
    for n, ref in enumerate(keys):
        keyw[n, 0:main] = ref[pl.ds(start, main)]

    @pl.when(m < nmp - 1)
    def _():
        after = pl.multiple_of(start + main, 128)
        featw[:, main:] = feat_ref[:, pl.ds(after, 128)]
        for n, ref in enumerate(keys):
            keyw[n, main:] = ref[pl.ds(after, 128)]

    @pl.when(m == nmp - 1)
    def _():
        featw[:, main:] = jnp.zeros((EFEAT, 128), bf)
        keyw[:, main:] = jnp.zeros((3, 128), jnp.int32)
        tail = z.edges - z.full
        if tail:
            featw[:, main : main + tail] = feat_ref[:, z.full :]
            for n, ref in enumerate(keys):
                keyw[n, main : main + tail] = ref[z.full :]

    place = lax.broadcasted_iota(jnp.int32, (1, z.win), 1) + (start - z.per * m)
    valid = (place >= 0) & (place < z.per)
    mol = jnp.zeros((1, z.win), jnp.int32)
    for i in range(1, nm):
        mol = mol + jnp.where(place >= ME * i, PADA, 0)
    keyw[0:1, :] = jnp.where(valid & (keyw[2:3, :] == 1), keyw[0:1, :], -1)
    keyw[1:2, :] = jnp.where(valid, keyw[1:2, :] + mol, -1)

    wio = lax.broadcasted_iota(jnp.int32, (PADA, 1024), 0)

    def permute(i):
        b = z.bases[i]
        st = wio == keyw[0:1, b : b + 1024]
        rt = jnp.where(wio + PADA * i == keyw[1:2, b : b + 1024], 1.0, 0.0).astype(bf)
        ff = featw[:, b : b + 1024].astype(f32)
        for q in range(4):
            zz = jnp.concatenate(
                [jnp.where(st, ff[f : f + 1, :], 0.0).astype(bf) for f in range(4 * q, 4 * q + 4)], axis=0
            )
            featp[i * PADA : (i + 1) * PADA, q * 128 : (q + 1) * 128] = dot(rt, zz, NT).astype(bf)

    for i in range(nm):
        permute(i)

    if relay:
        for n, (v, devs) in enumerate(((ux, (py, cp)), (uy, (cp,)))):
            w_in_from(2 * v + c)
            w_in_to(3 + 2 * n, 2 * v + c, *devs)
    along_z(1)
    in_plane(0)
    fp = featp[...]
    featt[...] = fp.T
    if relay:
        w_in_from(2 * ud + c)
        w_in_to(7, 2 * ud + c, cp)
        for v in (u, ux, uy, ud):
            w_in_from(2 * v + 1 - c)
    else:
        for i in range(1, ndp):
            w_in_from((d - i + ndp) % ndp)
    w_in = wis[...].astype(f32).sum(axis=0).astype(bf)
    delta = (
        lax.broadcasted_iota(jnp.int32, (PADA, 256), 0)
        == lax.broadcasted_iota(jnp.int32, (PADA, 256), 1) % PADA
    )

    @pl.loop(0, 16, unroll=4)
    def _(k):
        e = jnp.where(
            lax.broadcasted_iota(jnp.int32, (HID, 256), 0)
            == k * 8 + lax.broadcasted_iota(jnp.int32, (HID, 256), 1) // PADA,
            1.0,
            0.0,
        ).astype(bf)
        emat[k] = e
        wexp = dot(w_in, e, NN)
        for f in range(EFEAT):
            kron[k, f * PADA : (f + 1) * PADA, :] = jnp.where(delta, wexp[f : f + 1, :], 0.0).astype(bf)


    def hidden(lo):
        @pl.loop(lo, lo + 8, unroll=4)
        def _(k):
            p = dot(fp, kron[k], NN)
            s = sig(p)
            h = p * s
            hid[k] = h.astype(bf)
            hidt[k] = h.T.astype(bf)
            slope[k] = (s + h - h * s).astype(bf)

    along_z(2)
    hidden(0)
    in_plane(1)
    for i, p in enumerate(zp):
        go(rcopy(xsb.at[p[1]], xo.at[m], xs_s.at[i], xs_r.at[m], p))

    along_z(3)
    hidden(8)
    from_diagonal(0)
    in_plane(2)
    from_diagonal(1)

    for col in zcols:
        rcopy(xo.at[col], xo.at[col], xs_s.at[0], xs_r.at[col], cp).wait_recv()
    xf = jnp.zeros((z.rows, HID), f32)
    cf = jnp.zeros((z.rows, HID), f32)
    for j in range(nmp):
        sl = one_up(xo[j].astype(f32))
        here = (lane >= z.uw * j) & (lane < z.uw * (j + 1))
        xf = jnp.where(here, roll(sl, 0, z.uw * j), xf)
        cf = jnp.where(here, roll(sl, z.uw, z.uw * j), cf)
    x = xf.astype(bf)

    def rows_of(row, qs):
        return jnp.concatenate(
            [wall[row, j, q * rw : (q + 1) * rw, :] for q in qs for j in range(nmp)], axis=0
        )

    def make_b(row):
        for q in range(hl // 2):
            o = dot(x, rows_of(row, (2 * q, 2 * q + 1)), NT).astype(bf)
            bmat[row * hl + 2 * q] = o[:, :HID]
            bmat[row * hl + 2 * q + 1] = o[:, HID:]

    sacc[...] = jnp.zeros(sacc.shape, f32)

    def use_row(row):
        make_b(row)
        if hl % 8 == 0:
            parts = [row * (hl // 8) + k for k in range(hl // 8)]
            for i in range(nm):
                at = pl.ds(i * PADA, PADA)
                hm = jnp.concatenate([hid[k, at, :] for k in parts], axis=1)
                sacc[at, :] += dot(hm, bmat[pl.ds(row * hl, hl), at, :].reshape(PADA * hl, HID), NN)

    def from_core(row):
        for col in here_cols:
            for k in (0, 1):
                arrived(row, col, k)
        use_row(row)

    use_row(d)
    in_plane(3)
    for row in rows_x:
        use_row(row)
    from_core(cp[0])
    from_diagonal(2)
    from_diagonal(3)
    if relay:
        use_row(2 * ud + c)
    for row in rows_x + ([2 * ud + c] if relay else []):
        from_core(row + 1 - 2 * c)
    if hl % 8:
        for i in range(nm):
            hm = jnp.concatenate([hid[k, i * PADA : (i + 1) * PADA, :] for k in range(16)], axis=1)
            sacc[i * PADA : (i + 1) * PADA, :] = dot(
                hm, bmat[:, i * PADA : (i + 1) * PADA, :].reshape(PADA * HID, HID), NN
            )
    summed = sacc[...].astype(bf)

    def gru_rows(s, j):
        if il == 16:
            return jnp.concatenate([wall[k, j, wr + 16 * s : wr + 16 * s + 16, :] for k in range(ndp)], axis=0)
        for k in range(ndp):
            gfull[k * il : (k + 1) * il, 0:HID] = wall[k, j, wr + 16 * s : wr + 16 * s + 16, :].astype(f32)[:il]
        return gfull[0:HID, 0:HID].astype(bf)

    wg = [[gru_rows(s, j) for j in range(nmp)] for s in range(2)]

    def gates(a, s):
        outs = [dot(a, wg[s][j], NN) for j in range(nmp)]
        res = []
        for g in range(3):
            t = None
            for j in range(nmp):
                y = roll(outs[j], z.uw * g, z.uw * j)
                here = (lane >= z.uw * j) & (lane < z.uw * (j + 1))
                t = y if t is None else jnp.where(here, y, t)
            res.append(t)
        return res

    gi = gates(summed, 0)
    gs = gates(x, 1)
    reset = sig(gi[0] + gs[0])
    update = sig(gi[1] + gs[1])
    cand = jnp.tanh(gi[2] + reset * gs[2])
    ostate = (1.0 - update) * cand + update * xf
    dc = cf * (1.0 - update) * (1.0 - cand * cand)
    du = cf * (xf - cand) * update * (1.0 - update)
    dr = dc * gs[2] * reset * (1.0 - reset)

    def pack(gl, j):
        t = jnp.zeros((z.rows, HID), f32)
        for g in range(3):
            here = (lane >= z.uw * g) & (lane < z.uw * (g + 1))
            t = jnp.where(here, roll(gl[g], z.uw * j, z.uw * g), t)
        return t.astype(bf)

    al = [pack([dr, du, dc], j) for j in range(nmp)]
    bl = [pack([dr, du, dc * reset], j) for j in range(nmp)]
    ds = dot(jnp.concatenate(al, axis=1), jnp.concatenate(wg[0], axis=1), NT).astype(bf)
    gfull[:, HID : 2 * HID] = cf * update
    gfull[:, 0:HID] = dot(jnp.concatenate(bl, axis=1), jnp.concatenate(wg[1], axis=1), NT)
    for j in range(nmp):
        for s, (l, r) in enumerate(((summed, al[j]), (x, bl[j]))):
            gg = dot(l, r, TN)
            for k in range(ndp):
                part = gg[k * il : (k + 1) * il]
                if il < 16:
                    part = jnp.concatenate([part, jnp.zeros((16 - il, HID), f32)], axis=0)
                grads[k, j, wr + 16 * s : wr + 16 * s + 16, :] = part.astype(bf)

    dsb[...] = jnp.zeros(dsb.shape, bf)
    for i in range(nm):
        dsb[i * PADA : (i + 1) * PADA, i * HID : (i + 1) * HID] = ds[i * PADA : (i + 1) * PADA]

    def c_block(k):
        for p in range(nm // 2):
            o = dot(hidt[k], dsb[:, p * 256 : (p + 1) * 256], NN).astype(bf)
            for i in range(2):
                at = (2 * p + i) * PADA
                cmat[pl.ds(k * 8, 8), at : at + PADA, :] = o[:, i * HID : (i + 1) * HID].reshape(8, PADA, HID)

    if hl % 8:
        pl.loop(0, 16, unroll=8)(c_block)

    def grad_w(row):
        for k in range(hl // 8):
            c_block(row * (hl // 8) + k)
        for q in range(hl):
            o = dot(cmat[row * hl + q], x, TN).astype(bf)
            for j in range(nmp):
                grads[row, j, q * rw : (q + 1) * rw, :] = o[rw * j : rw * (j + 1)]

    cols = zcols[::-1] + [m]

    def core_arrived(t, col):
        rcopy(rc.at[t, col], rc.at[t, col], fsem, cr.at[t, col], cp).wait_recv()

    def plane_out(t, *which):
        row = 2 * chips[t] + c
        for i in which:
            col = cols[i]
            core_arrived(t, col)
            sb[t, i] = (grads[row, col].astype(f32) + rc[t, col].astype(f32)).astype(bf)
            if not relay:
                go(rcopy(sb.at[t, i], rp.at[t, col], ps.at[t, i], pr.at[t, col], pp[t]))
                continue
            if t < 2:
                go(rcopy(sb.at[t, i, pl.ds(0, ra), :], rp.at[t, col, pl.ds(0, ra), :], ps.at[t, i], pr.at[t, col], px))
            if t != 1:
                k = t // 2 + 2
                go(rcopy(sb.at[t, i, pl.ds(ra, ra), :], rp.at[k % 3, col, pl.ds(ra, ra), :], ps.at[k, i], pr.at[k, col], py))

    def row_out(t):
        row = 2 * chips[t] + (1 - c)
        grad_w(row)
        for i, col in enumerate(cols):
            go(rcopy(grads.at[row, col], rc.at[t, col], cs.at[t, i], cr.at[t, col], cp))

    def row_own(t):
        grad_w(2 * chips[t] + c)

    def part_arrived(slot, lo, col, k):
        here = rp.at[slot, col, pl.ds(lo, ra), :]
        rcopy(here, here, fsem, pr.at[k, col], cp).wait_recv()
        return rp[slot, col, lo : lo + ra, :].astype(f32)

    def turn(i):
        if not relay:
            return
        col = cols[i]
        ta[i] = (sb[2, i, 0:ra, :].astype(f32) + part_arrived(0, 0, col, 0)).astype(bf)
        go(rcopy(ta.at[i], r2a.at[col], p2s.at[0, i], p2r.at[0, col], py))
        tb[i] = (sb[1, i, ra:, :].astype(f32) + part_arrived(2, ra, col, 2)).astype(bf)
        go(rcopy(tb.at[i], r2b.at[col], p2s.at[1, i], p2r.at[1, col], px))

    def column(i):
        col = cols[i]
        core_arrived(half - 1, col)
        q = grads[d, col].astype(f32) + rc[half - 1, col].astype(f32)
        if not relay:
            for t in range(half - 1):
                here = rp.at[t, col]
                rcopy(here, here, fsem, pr.at[t, col], cp).wait_recv()
                q = q + rp[t, col].astype(f32)
            return q
        rcopy(r2a.at[col], r2a.at[col], fsem, p2r.at[0, col], cp).wait_recv()
        rcopy(r2b.at[col], r2b.at[col], fsem, p2r.at[1, col], cp).wait_recv()
        qa = q[:ra] + part_arrived(1, 0, col, 1) + r2a[col].astype(f32)
        qb = q[ra:] + part_arrived(0, ra, col, 3) + r2b[col].astype(f32)
        return jnp.concatenate([qa, qb], axis=0)

    at_end = (m == 0) | (m == nmp - 1)
    between = (m > 0) & (m < nmp - 1)

    def z_piece(ref, k):
        return ref.at[pl.ds(k * ra, ra), :]

    def z_arrived(way, col):
        for k in (0, 1):
            here = z_piece(rz.at[way, col], k)
            rcopy(here, here, fsem, zr.at[way, col, k], cp).wait_recv()
        return rz[way, col].astype(f32)

    def z_copies(i):
        col = cols[i]
        up = jnp.where(col > m, 1, 0)
        way = 1 - up
        return way, [
            rcopy(z_piece(zs.at[i], k), z_piece(rz.at[way, col], k), z2.at[i, k], zr.at[way, col, k], (d, m + 2 * up - 1))
            for k in (0, 1)
        ]

    def to_z(i, when, chained):
        @pl.when(when)
        def _():
            q = column(i)
            way, copies = z_copies(i)
            if chained:
                q = q + z_arrived(way, cols[i])
            zs[i] = q.astype(bf)
            for x in copies:
                x.start()

    def by_eight(v, mask):
        v = jnp.where(mask[None], v.reshape(EFEAT, PADA, -1), 0.0)
        return (v[:, 0:8] + v[:, 8:16] + v[:, 16:24] + v[:, 24:32]).reshape(EFEAT * 8, -1).astype(bf)

    eight = jnp.where(
        lax.broadcasted_iota(jnp.int32, (EFEAT, EFEAT * 8), 0)
        == lax.broadcasted_iota(jnp.int32, (EFEAT, EFEAT * 8), 1) // 8,
        1.0,
        0.0,
    ).astype(bf)
    tiles = -(-z.win // 256)
    cuts = (0, tiles // 2, tiles)

    def edges_back(part):
        for n in range(cuts[part], cuts[part + 1]):
            count = min(256, z.win - n * 256)
            at = pl.ds(n * 256, count)
            all_rows = lax.broadcasted_iota(jnp.int32, (z.rows, count), 0)
            rt = jnp.where(all_rows == keyw[1:2, at], 1.0, 0.0).astype(bf)
            eights[n, :, 0:count] = by_eight(dot(gbt[...], rt, NN), wio[:, :count] == keyw[0:1, at])
        for n in range(cuts[part], cuts[part + 1]):
            count = min(256, z.win - n * 256)
            geo[m, :, n * 256 : n * 256 + count] = dot(eight, eights[n, :, 0:count], NN).astype(bf)

    def edges_on(s):
        for part in (0, 1):
            edges_on_part(s, part)

    def edges_on_part(s, part):
        lo, hi = 256 * cuts[part], min(256 * cuts[part + 1], z.win)
        for way in (0, 1):
            col = m - s if way == 0 else m + s
            nxt = m + 1 if way == 0 else m - 1
            src = geo.at[col, :, pl.ds(lo, hi - lo)]
            if s:
                pl.when(inside(col))(rcopy(src, src, fsem, ge_r.at[part, col], cp).wait_recv)
            if s < nmp - 1:
                go_if(
                    inside(col) & inside(nxt),
                    rcopy(src, src, ge_s.at[part, s, way], ge_r.at[part, col], (d, nxt)),
                )

    step = min(DXC, hl)

    def state_grad(lo, hi):
        @pl.loop(lo, hi, unroll=2)
        def _(row):
            for q in range(0, hl, step):
                qs = range(q, q + step)
                cc = jnp.concatenate([cmat[row * hl + k] for k in qs], axis=1)
                gacc[...] += dot(cc, rows_of(row, qs), NN)

    def hidden_grad(lo, hi):
        for i in range(nm):
            dm = ds[i * PADA : (i + 1) * PADA]
            for k in range(lo, hi):
                o = dot(dm, bmat[k * 8 : (k + 1) * 8, i * PADA : (i + 1) * PADA, :].reshape(256, HID), NT)
                dpre[k, i * PADA : (i + 1) * PADA, :] = (
                    o * slope[k, i * PADA : (i + 1) * PADA, :].astype(f32)
                ).astype(bf)

    others = range(half - 1)
    row_out(0)
    row_own(0)
    row_out(1)
    plane_out(0, 0)
    row_own(1)
    plane_out(0, 1)
    for t in others[2:]:
        row_out(t)
        plane_out(t - 1, 0)
        row_own(t)
    hidden_grad(0, 8)
    plane_out(half - 2, 0)
    hidden_grad(8, 16)
    gb = dot(
        jnp.concatenate([dpre[k] for k in range(16)], axis=1),
        jnp.concatenate([kron[k] for k in range(16)], axis=1),
        NT,
    ).astype(bf)
    gbt[...] = gb.T
    turn(0)
    for t in others[1:]:
        plane_out(t, 1)
    plane_out(0, 2)
    edges_back(0)
    edges_on_part(0, 0)
    edges_back(1)
    edges_on_part(0, 1)
    turn(1)
    for t in others[1:]:
        plane_out(t, 2)
    plane_out(0, 3)
    row_out(half - 1)
    row_own(half - 1)

    @pl.loop(0, 16, unroll=16)
    def _(k):
        eights[k] = by_eight(dot(featt[...], dpre[k], NN), delta)

    gin = dot(
        jnp.concatenate([eights[k] for k in range(16)], axis=1),
        jnp.concatenate([emat[k] for k in range(16)], axis=1),
        NT,
    )
    gis[d] = gin.reshape(EFEAT, 8, HID).sum(axis=1).astype(bf)
    for i, p in enumerate(dpp):
        go(rcopy(gis.at[d], gis.at[d], gi_s.at[i], gi_r.at[d], p))
    to_z(0, at_end, False)

    gacc[...] = jnp.zeros(gacc.shape, f32)
    state_grad(0, ndp // 2)
    turn(2)
    for t in others[1:]:
        plane_out(t, 3)
    edges_on(1)
    state_grad(ndp // 2, ndp)
    gfin = gacc[...] + gfull[:, 0:HID] + gfull[:, HID : 2 * HID]
    for j in range(nmp):
        a = roll(ostate, z.uw * j, 0)
        b = roll(gfin, z.uw * j, z.uw)
        osb[j] = two_up(jnp.where(lane < z.uw, a, b)).astype(bf)
    for i, p in enumerate(zp):
        go(rcopy(osb.at[p[1]], oso.at[m], os_s.at[i], os_r.at[m], p))
    oso[m] = osb[m]

    to_z(1, at_end, False)
    to_z(0, between, True)
    gi_sum = gis[d].astype(f32)
    for i in range(1, ndp):
        row = (d - i + ndp) % ndp
        rcopy(gis.at[row], gis.at[row], gi_s.at[0], gi_r.at[row], cp).wait_recv()
        gi_sum = gi_sum + gis[row].astype(f32)
    giz_s[...] = gi_sum.astype(bf)
    for i, p in enumerate(zp):
        go(rcopy(giz_s, giz.at[m], gz_s.at[i], gz_r.at[m], p))
    turn(3)
    edges_on(2)
    to_z(2, at_end, False)
    to_z(1, between, True)
    to_z(2, between, True)

    for col in zcols:
        rcopy(oso.at[col], oso.at[col], os_s.at[0], os_r.at[col], cp).wait_recv()
    for j in range(nmp):
        stage2[j * z.rows : (j + 1) * z.rows, :] = one_up(oso[j].astype(f32))
    for i in range(z.mols):
        stage1[i * MA : (i + 1) * MA, :] = stage2[i * PADA : i * PADA + MA, :]
    stage[...] = stage1[...].T
    at_ref[0 : z.uw, :] = stage[0 : z.uw, 0 : z.atoms] * nmrow[...]
    at_ref[z.uw : 2 * z.uw, :] = stage[z.uw : 2 * z.uw, 0 : z.atoms]
    at_out = pltpu.make_async_copy(at_ref, at_hbm, lsem.at[0])
    at_out.start()

    fin[...] = column(nmp - 1)
    edges_on(3)
    for j, lo in enumerate(z.starts):
        first = geo[j, :, 0:128]
        if j:
            first = (first.astype(f32) + geo[j - 1, :, main:].astype(f32)).astype(bf)
        ge_ref[:, lo : lo + 128] = first
        ge_ref[:, lo + 128 : lo + main] = geo[j, :, 128:main]
    if z.edges > z.full:
        ge_ref[:, z.full :] = geo[nmp - 1, :, main : main + z.edges - z.full]
    ge_out = pltpu.make_async_copy(ge_ref, ge_hbm, lsem.at[1])
    ge_out.start()

    for col in zcols:
        rcopy(giz.at[col], giz.at[col], gz_s.at[0], gz_r.at[col], cp).wait_recv()
        gi_sum = gi_sum + giz[col].astype(f32)
    gi_ref[...] = pltpu.roll(gi_sum, HID - d * z.ew, 1)[:, 0 : z.ew]

    @pl.when(m > 0)
    def _():
        fin[...] += z_arrived(0, m)

    @pl.when(m < nmp - 1)
    def _():
        fin[...] += z_arrived(1, m)

    for s in range(2):
        for g in range(3):
            gg_ref[s, g] = fin[wr + 16 * s : wr + 16 * s + il, g * z.uw : (g + 1) * z.uw]
    wtmp[...] = fin[0:wr, :].reshape(hl, rw, HID)
    for r in range(rw):
        go_ref[:, r * HID : (r + 1) * HID] = wtmp[:, r, :]

    at_out.wait()
    ge_out.wait()
    for i in range(nmp - 1):
        sends.extend(z_copies(i)[1])
    for y in sends:
        y.wait_send()
    for ok, y in maybe:
        pl.when(ok)(y.wait_send)


def whole_step(z, eo, ei, gw, ns, og, live, feat, snd, rcv, msk):
    dma = pltpu.SemaphoreType.DMA
    ndp, nmp, half = z.ndp, z.nmp, z.half
    rows, rb, win = z.rows, z.rb, z.win
    vm = pltpu.VMEM
    ra = rb // 2
    relay = half == 4
    return pl.pallas_call(
        functools.partial(kernel, z),
        out_shape=(
            jax.ShapeDtypeStruct(eo.shape, f32),
            jax.ShapeDtypeStruct(gw.shape, f32),
            jax.ShapeDtypeStruct(ei.shape, f32),
            jax.ShapeDtypeStruct((2 * z.uw, z.atoms), f32),
            jax.ShapeDtypeStruct(feat.shape, bf),
        ),
        in_specs=[pl.BlockSpec(memory_space=pl.ANY)] * 10,
        out_specs=(pl.BlockSpec(memory_space=vm),) * 3 + (pl.BlockSpec(memory_space=pl.ANY),) * 2,
        scratch_shapes=[
            vm((2 * z.uw, z.atoms), f32),
            vm(feat.shape, bf),
            *(vm(a.shape, a.dtype) for a in (eo, ei, gw, ns, og, live, feat, snd, rcv, msk)),
            vm((ndp, nmp, rb, HID), bf),
            vm((nmp, rows // 2, HID), bf),
            vm((nmp, rows // 2, HID), bf),
            vm((ndp, EFEAT, HID), bf),
            vm((HID, -(-z.atoms // 128) * 128), f32),
            vm((-(-z.atoms // 128) * 128, HID), f32),
            vm((nmp * rows, HID), f32),
            vm((z.hl, z.rw, HID), f32),
            vm((32, HID), f32),
            vm((EFEAT, HID), f32),
            vm((1, z.atoms), f32),
            vm((EFEAT, win), bf),
            vm((3, win), jnp.int32),
            vm((rows, 512), bf),
            vm((512, rows), bf),
            vm((512, rows), bf),
            vm((16, 512, 256), bf),
            vm((16, HID, 256), bf),
            vm((16, rows, 256), bf),
            vm((16, 256, rows), bf),
            vm((16, rows, 256), bf),
            vm((HID, rows, HID), bf),
            vm((HID, rows, HID), bf),
            vm((rows, z.nm * HID), bf),
            vm((16, rows, 256), bf),
            vm((rows, HID), f32),
            vm((rows, HID), f32),
            vm((rows, 512), f32),
            vm((max(16, -(-win // 256)), EFEAT * 8, 256), bf),
            vm((ndp, nmp, rb, HID), bf),
            vm((half, nmp, rb, HID), bf),
            vm((half - 1, nmp, rb, HID), bf),
            vm((half - 1, nmp, rb, HID), bf),
            vm((nmp, ra, HID), bf),
            vm((nmp, ra, HID), bf),
            vm((nmp, ra, HID), bf),
            vm((nmp, ra, HID), bf),
            vm((nmp - 1, rb, HID), bf),
            vm((2, nmp, rb, HID), bf),
            vm((rb, HID), f32),
            vm((nmp, rows // 2, HID), bf),
            vm((nmp, rows // 2, HID), bf),
            vm((nmp, EFEAT, win), bf),
            vm((ndp, EFEAT, HID), bf),
            vm((nmp, EFEAT, HID), bf),
            vm((EFEAT, HID), bf),
            dma((10,)),
            dma(()),
            dma((nmp - 1, 2)),
            dma((nmp - 1, 2)),
            dma((nmp, 2, max(half - 1, 4))),
            dma((2 * nmp * half,)),
            dma((ndp, nmp, 2)),
            dma((nmp - 1,)), dma((nmp,)),
            dma((max(ndp - 1, 8),)), dma((ndp,)),
            dma((half, nmp)), dma((half, nmp)),
            dma((max(half - 1, 4), nmp)), dma((max(half - 1, 4), nmp)),
            dma((2, nmp)), dma((2, nmp)),
            dma((nmp - 1, 2)), dma((2, nmp, 2)),
            dma((nmp - 1,)), dma((nmp,)),
            dma((2, nmp - 1, 2)), dma((2, nmp)),
            dma((ndp - 1,)), dma((ndp,)),
            dma((nmp - 1,)), dma((nmp,)),
        ],
        compiler_params=pltpu.CompilerParams(
            collective_id=0, has_side_effects=True, vmem_limit_bytes=VMEM_LIMIT
        ),
    )(eo, ei, gw, ns, og, live, feat, snd, rcv, msk)


beta_one = 0.5
beta_two = 0.5
learn_rate = 0.05
decay_rate = 0.01
epsilon = 1e-08


def adam_update(weight, gradient, first_moment, second_moment):
    first_new = beta_one * first_moment + (1.0 - beta_one) * gradient
    second_new = beta_two * second_moment + (1.0 - beta_two) * gradient * gradient
    mean_hat = first_new / (1.0 - beta_one**STEP)
    square_hat = second_new / (1.0 - beta_two**STEP)
    weight_new = weight - learn_rate * (
        mean_hat / (jnp.sqrt(square_hat) + epsilon) + decay_rate * weight
    )
    return (first_new, second_new, weight_new, weight_new.astype(bf))


def finish_kernel(*refs):
    ins, outs = refs[:14], refs[14:29]
    vin, vout = refs[29:43], refs[43:58]
    isem, osem = refs[58:]
    loads = [pltpu.make_async_copy(a, b, isem.at[i]) for i, (a, b) in enumerate(zip(ins, vin))]
    stores = [pltpu.make_async_copy(a, b, osem.at[i]) for i, (a, b) in enumerate(zip(vout, outs))]
    order = [1, 6, 7, 8, 9, 0, 2, 3, 4, 5, 10, 11, 12, 13]
    for i in order:
        loads[i].start()
    loads[1].wait()
    vout[2][...] = vin[1][...].astype(f32)
    stores[2].start()

    def layer(n):
        for i in range(2 + 4 * n, 6 + 4 * n):
            loads[i].wait()
        new = adam_update(*[vin[i][...] for i in range(2 + 4 * n, 6 + 4 * n)])
        for i, v in enumerate(new):
            vout[3 + 4 * n + i][...] = v
            stores[3 + 4 * n + i].start()

    layer(1)
    loads[0].wait()
    uw = vin[0].shape[0] // 2
    vout[0][...] = vin[0][0:uw, :]
    vout[1][...] = vin[0][uw:, :]
    stores[0].start()
    stores[1].start()
    layer(0)
    layer(2)
    for x in stores:
        x.wait()


def finish(at, ge, *layers):
    half = jax.ShapeDtypeStruct((at.shape[0] // 2, at.shape[1]), f32)
    results = [half, half, jax.ShapeDtypeStruct(ge.shape, f32)]
    for n in range(3):
        results += [jax.ShapeDtypeStruct(layers[4 * n].shape, t) for t in (f32, f32, f32, bf)]
    args = (at, ge, *layers)
    return pl.pallas_call(
        finish_kernel,
        out_shape=tuple(results),
        in_specs=[pl.BlockSpec(memory_space=pl.ANY)] * 14,
        out_specs=(pl.BlockSpec(memory_space=pl.ANY),) * 15,
        scratch_shapes=[pltpu.VMEM(v.shape, v.dtype) for v in (*args, *results)]
        + [pltpu.SemaphoreType.DMA((14,)), pltpu.SemaphoreType.DMA((15,))],
        compiler_params=pltpu.CompilerParams(vmem_limit_bytes=VMEM_LIMIT),
    )(*args)


def body(
    ndp, nmp,
    node_state, edge_feat, sender, receiver, edge_mask, node_mask, out_grad,
    edge_in, edge_out, gru_weight,
    edge_in_m1, edge_in_m2, edge_out_m1, edge_out_m2, gru_m1, gru_m2,
):
    z = Shape(ndp, nmp, node_state, edge_feat, edge_in, edge_out, gru_weight)
    g_out, g_gru, g_in, at, ge = whole_step(
        z, edge_out, edge_in, gru_weight, node_state.T, out_grad.T, node_mask,
        edge_feat, sender, receiver, edge_mask,
    )
    out_state, grad_state, *rest = finish(
        at, ge,
        edge_in, g_in, edge_in_m1, edge_in_m2,
        edge_out, g_out, edge_out_m1, edge_out_m2,
        gru_weight, g_gru, gru_m1, gru_m2,
    )
    return (out_state.T, grad_state.T, *rest)


def solution(mesh):
    ndp, nmp = mesh.shape["dp"], mesh.shape["mp"]
    rows, lanes, gru = P("dp", "mp"), P(None, "dp"), P(None, None, "dp", "mp")
    edge = P("dp")
    return jax.shard_map(
        functools.partial(body, ndp, nmp),
        mesh=mesh,
        in_specs=(
            rows, lanes, edge, edge, edge, edge, rows,
            lanes, rows, gru, lanes, lanes, rows, rows, gru, gru,
        ),
        out_specs=(rows, rows, lanes) + (lanes,) * 4 + (rows,) * 4 + (gru,) * 4,
        check_vma=False,
    )
```

```python
import functools

import jax
import jax.numpy as jnp
from jax import lax
from jax.experimental import pallas as pl
from jax.experimental.pallas import tpu as pltpu
from jax.sharding import PartitionSpec as P

HID = 128
EFEAT = 16
MA = 29
ME = 812
PADA = 32
STEP = 5
DXC = 4
MESH = pl.DeviceIdType.MESH
VMEM_LIMIT = 60 << 20
bf = jnp.bfloat16
f32 = jnp.float32
NT = (((1,), (1,)), ((), ()))
TN = (((0,), (0,)), ((), ()))
NN = (((1,), (0,)), ((), ()))


def dot(a, b, dims):
    return lax.dot_general(a, b, dims, preferred_element_type=f32)


def roll(x, src, dst):
    shift = (dst - src) % HID
    return pltpu.roll(x, shift, 1) if shift else x


def sig(v):
    return 0.5 + 0.5 * jnp.tanh(0.5 * v)


def rcopy(src, dst, ssem, rsem, dev):
    return pltpu.make_async_remote_copy(
        src_ref=src, dst_ref=dst, send_sem=ssem, recv_sem=rsem, device_id=dev, device_id_type=MESH
    )


class Shape:
    def __init__(self, ndp, nmp, node_state, edge_feat, edge_in, edge_out, gru):
        self.ndp, self.nmp, self.half = ndp, nmp, ndp // 2
        self.atoms, self.uw = node_state.shape
        self.edges = edge_feat.shape[1]
        self.mols = self.atoms // MA
        self.nm = self.mols // nmp
        self.rows = self.nm * PADA
        self.hl, self.il, self.ew = edge_out.shape[0], gru.shape[2], edge_in.shape[1]
        self.rw = edge_out.shape[1] // HID
        self.wr = self.hl * self.rw
        self.rb = self.wr + 32
        self.per = self.nm * ME
        self.starts = [self.per * j // 128 * 128 for j in range(nmp)]
        self.bases = [ME * i // 128 * 128 for i in range(self.nm)]
        self.win = self.bases[-1] + 1024
        self.full = self.edges // 128 * 128
        shift = max(self.per * j - s for j, s in enumerate(self.starts))
        assert all(ME * i + shift + ME <= b + 1024 for i, b in enumerate(self.bases))
        assert self.starts[-1] + self.win - 128 == self.full
        assert all(b - a == self.win - 128 for a, b in zip(self.starts, self.starts[1:]))


def kernel(
    z,
    eo_hbm, ei_hbm, gw_hbm, ns_hbm, og_hbm, nm_hbm, feat_hbm, snd_hbm, rcv_hbm, msk_hbm,
    go_ref, gg_ref, gi_ref, at_hbm, ge_hbm,
    at_ref, ge_ref,
    eo_ref, ei_ref, gw_ref, ns_ref, og_ref, nm_ref, feat_ref, snd_ref, rcv_ref, msk_ref,
    wall, xsb, xo, wis, stage, stage1, stage2, wtmp, stmp, itmp, nmrow, featw, keyw,
    featp, featt, gbt, kron, emat, hid, hidt, slope, bmat, cmat, dsb, dpre, gacc, sacc, gfull, eights,
    grads, rc, sb, rp, ta, tb, r2a, r2b, zs, rz, fin, osb, oso, geo, gis, giz, giz_s,
    lsem, fsem, zsem, zfsem, psem, csem, rsem, xs_s, xs_r, wi_s, wi_r,
    cs, cr, ps, pr, p2s, p2r, z2, zr, os_s, os_r, ge_s, ge_r, gi_s, gi_r, gz_s, gz_r,
):
    ndp, nmp, half, nm = z.ndp, z.nmp, z.half, z.nm
    hl, il, wr, rb, rw = z.hl, z.il, z.wr, z.rb, z.rw
    d = lax.axis_index("dp")
    m = lax.axis_index("mp")
    u = d // 2
    c = d % 2
    relay = half == 4
    low = jnp.where(2 * m < nmp, 1, 0)
    side = low * m + (1 - low) * (nmp - 1 - m)
    near = [jnp.where(i <= side, i - 1, i) for i in range(1, nmp)]
    zcols = [low * i + (1 - low) * (nmp - 1 - i) for i in near]
    zp = [(d, col) for col in zcols]
    if relay:
        ux = u + 1 - 2 * (u % 2)
        uy = (u + 2) % half
        ud = (ux + 2) % half
        chips = [ud, ux, uy, u]
        px, py = (2 * ux + c, m), (2 * uy + c, m)
        pp = [px, py]
    else:
        chips = [(u + t) % half for t in range(1, half)] + [u]
        pp = [(2 * v + c, m) for v in chips[:-1]]
    ra = rb // 2
    cp = (2 * u + (1 - c), m)
    dpp = [((d + i) % ndp, m) for i in range(1, ndp)]
    pairs = (
        (eo_hbm, eo_ref), (gw_hbm, gw_ref), (ei_hbm, ei_ref), (ns_hbm, ns_ref), (og_hbm, og_ref), (nm_hbm, nm_ref),
        (feat_hbm, feat_ref), (snd_hbm, snd_ref), (rcv_hbm, rcv_ref), (msk_hbm, msk_ref),
    )
    loads = [pltpu.make_async_copy(a, b, lsem.at[i]) for i, (a, b) in enumerate(pairs)]
    for x in loads:
        x.start()
    bar = pltpu.get_barrier_semaphore()
    near_by = [cp] + pp if relay else dpp
    for p in near_by:
        pl.semaphore_signal(bar, inc=1, device_id=p, device_id_type=MESH)
    for col in (m - 1, m + 1):

        @pl.when((col >= 0) & (col < nmp))
        def _():
            pl.semaphore_signal(bar, inc=1, device_id=(d, col), device_id_type=MESH)

    lane = lax.broadcasted_iota(jnp.int32, (1, HID), 1)

    def two_up(v):
        return jnp.where(lane < 64, v[: z.rows // 2], pltpu.roll(v[z.rows // 2 :], 64, 1))

    def one_up(v):
        return jnp.concatenate([v, pltpu.roll(v, 64, 1)], axis=0)

    for x in loads[:3]:
        x.wait()
    for r in range(rw):
        wtmp[:, r, :] = eo_ref[:, r * HID : (r + 1) * HID]
    wall[d, m, 0:wr, :] = wtmp[...].reshape(wr, HID).astype(bf)
    stmp[...] = jnp.zeros(stmp.shape, f32)
    for s in range(2):
        for g in range(3):
            stmp[16 * s : 16 * s + il, g * z.uw : (g + 1) * z.uw] = gw_ref[s, g]
    wall[d, m, wr:rb, :] = stmp[...].astype(bf)
    itmp[...] = jnp.zeros(itmp.shape, f32)
    itmp[:, 0 : z.ew] = ei_ref[...]
    wis[d] = pltpu.roll(itmp[...], d * z.ew, 1).astype(bf)
    for x in loads[3:6]:
        x.wait()
    stage[...] = jnp.zeros(stage.shape, f32)
    stage[0 : z.uw, 0 : z.atoms] = ns_ref[...].astype(f32)
    nmrow[0, :] = nm_ref[...].astype(f32)
    stage[z.uw : 2 * z.uw, 0 : z.atoms] = og_ref[...] * nmrow[...]
    stage1[...] = stage[...].T
    stage2[...] = jnp.zeros(stage2.shape, f32)
    for i in range(z.mols):
        stage2[i * PADA : i * PADA + MA, :] = stage1[i * MA : (i + 1) * MA, :]
    for j in range(nmp):
        xsb[j] = two_up(stage2[j * z.rows : (j + 1) * z.rows, :]).astype(bf)
    pl.semaphore_wait(bar, len(near_by) + jnp.where(m > 0, 1, 0) + jnp.where(m < nmp - 1, 1, 0))

    sends = []
    maybe = []

    def go(*copies):
        for x in copies:
            x.start()
        sends.extend(copies)

    def go_if(ok, x):
        pl.when(ok)(x.start)
        maybe.append((ok, x))

    def inside(col):
        return (col >= 0) & (col < nmp)

    def w_in_to(n, row, *devs):
        for i, p in enumerate(devs):
            go(rcopy(wis.at[row], wis.at[row], wi_s.at[n + i], wi_r.at[row], p))

    def w_in_from(row):
        rcopy(wis.at[row], wis.at[row], fsem, wi_r.at[row], cp).wait_recv()

    w_in_to(0, d, *(near_by if relay else dpp))

    rows_x = [2 * ux + c, 2 * uy + c] if relay else [2 * v + c for v in chips[:-1]]
    here_cols = [m] + zcols
    turns = [0]

    def piece(row, col, k):
        return wall.at[row, col, pl.ds(k * ra, ra), :]

    def arrived(row, col, k):
        src = piece(row, col, k)
        rcopy(src, src, fsem, rsem.at[row, col, k], cp).wait_recv()

    def give(row, col, k, sem, dev):
        src = piece(row, col, k)
        go(rcopy(src, src, sem, rsem.at[row, col, k], dev))

    def to_core(row, col, k):
        give(row, col, k, csem.at[turns[0]], cp)
        turns[0] += 1

    def push(n, k):
        col = here_cols[n]
        for t in range(len(pp)):
            t = t if k == 0 else len(pp) - 1 - t
            give(d, col, k, psem.at[n, k, t], pp[len(pp) - 1 - t])
        to_core(d, col, k)

    def along_z(n):
        col = here_cols[n]
        for k in (0, 1):
            arrived(d, col, k)
            beyond = m + 1 - 2 * jnp.where(col > m, 1, 0)
            src = piece(d, col, k)
            go_if(inside(beyond), rcopy(src, src, zfsem.at[n - 1, k], rsem.at[d, col, k], (d, beyond)))
            push(n, k)

    def in_plane(n):
        col = here_cols[n]
        if not relay:
            for row in rows_x:
                for k in (0, 1):
                    arrived(row, col, k)
                    to_core(row, col, k)
            return
        for k in (0, 1):
            for t in (k, 1 - k):
                row = rows_x[1 - t]
                arrived(row, col, k)
                if t == k:
                    give(row, col, k, psem.at[n, k, 3], (px, py)[k])
                to_core(row, col, k)

    def from_diagonal(n):
        if relay:
            for k in (0, 1):
                arrived(2 * ud + c, here_cols[n], k)
                to_core(2 * ud + c, here_cols[n], k)

    for k in (0, 1):
        for i, col in enumerate((m - 1, m + 1)):
            src = piece(d, m, k)
            go_if(inside(col), rcopy(src, src, zsem.at[i, k], rsem.at[d, m, k], (d, col)))
        push(0, k)
    xo[m] = xsb[m]

    start = pl.multiple_of(z.per * m // 128 * 128, 128)
    main = z.win - 128
    for x in loads[6:]:
        x.wait()
    featw[:, 0:main] = feat_ref[:, pl.ds(start, main)]
    keys = (snd_ref, rcv_ref, msk_ref)
    for n, ref in enumerate(keys):
        keyw[n, 0:main] = ref[pl.ds(start, main)]

    @pl.when(m < nmp - 1)
    def _():
        after = pl.multiple_of(start + main, 128)
        featw[:, main:] = feat_ref[:, pl.ds(after, 128)]
        for n, ref in enumerate(keys):
            keyw[n, main:] = ref[pl.ds(after, 128)]

    @pl.when(m == nmp - 1)
    def _():
        featw[:, main:] = jnp.zeros((EFEAT, 128), bf)
        keyw[:, main:] = jnp.zeros((3, 128), jnp.int32)
        tail = z.edges - z.full
        if tail:
            featw[:, main : main + tail] = feat_ref[:, z.full :]
            for n, ref in enumerate(keys):
                keyw[n, main : main + tail] = ref[z.full :]

    place = lax.broadcasted_iota(jnp.int32, (1, z.win), 1) + (start - z.per * m)
    valid = (place >= 0) & (place < z.per)
    mol = jnp.zeros((1, z.win), jnp.int32)
    for i in range(1, nm):
        mol = mol + jnp.where(place >= ME * i, PADA, 0)
    keyw[0:1, :] = jnp.where(valid & (keyw[2:3, :] == 1), keyw[0:1, :], -1)
    keyw[1:2, :] = jnp.where(valid, keyw[1:2, :] + mol, -1)

    wio = lax.broadcasted_iota(jnp.int32, (PADA, 1024), 0)

    def permute(i):
        b = z.bases[i]
        st = wio == keyw[0:1, b : b + 1024]
        rt = jnp.where(wio + PADA * i == keyw[1:2, b : b + 1024], 1.0, 0.0).astype(bf)
        ff = featw[:, b : b + 1024].astype(f32)
        for q in range(4):
            zz = jnp.concatenate(
                [jnp.where(st, ff[f : f + 1, :], 0.0).astype(bf) for f in range(4 * q, 4 * q + 4)], axis=0
            )
            featp[i * PADA : (i + 1) * PADA, q * 128 : (q + 1) * 128] = dot(rt, zz, NT).astype(bf)

    for i in range(nm):
        permute(i)

    if relay:
        for n, (v, devs) in enumerate(((ux, (py, cp)), (uy, (cp,)))):
            w_in_from(2 * v + c)
            w_in_to(3 + 2 * n, 2 * v + c, *devs)
    along_z(1)
    in_plane(0)
    fp = featp[...]
    featt[...] = fp.T
    if relay:
        w_in_from(2 * ud + c)
        w_in_to(7, 2 * ud + c, cp)
        for v in (u, ux, uy, ud):
            w_in_from(2 * v + 1 - c)
    else:
        for i in range(1, ndp):
            w_in_from((d - i + ndp) % ndp)
    w_in = wis[...].astype(f32).sum(axis=0).astype(bf)
    delta = (
        lax.broadcasted_iota(jnp.int32, (PADA, 256), 0)
        == lax.broadcasted_iota(jnp.int32, (PADA, 256), 1) % PADA
    )

    @pl.loop(0, 16, unroll=4)
    def _(k):
        e = jnp.where(
            lax.broadcasted_iota(jnp.int32, (HID, 256), 0)
            == k * 8 + lax.broadcasted_iota(jnp.int32, (HID, 256), 1) // PADA,
            1.0,
            0.0,
        ).astype(bf)
        emat[k] = e
        wexp = dot(w_in, e, NN)
        for f in range(EFEAT):
            kron[k, f * PADA : (f + 1) * PADA, :] = jnp.where(delta, wexp[f : f + 1, :], 0.0).astype(bf)


    def hidden(lo):
        @pl.loop(lo, lo + 8, unroll=4)
        def _(k):
            p = dot(fp, kron[k], NN)
            s = sig(p)
            h = p * s
            hid[k] = h.astype(bf)
            hidt[k] = h.T.astype(bf)
            slope[k] = (s + h - h * s).astype(bf)

    along_z(2)
    hidden(0)
    in_plane(1)
    for i, p in enumerate(zp):
        go(rcopy(xsb.at[p[1]], xo.at[m], xs_s.at[i], xs_r.at[m], p))

    along_z(3)
    hidden(8)
    from_diagonal(0)
    in_plane(2)
    from_diagonal(1)

    for col in zcols:
        rcopy(xo.at[col], xo.at[col], xs_s.at[0], xs_r.at[col], cp).wait_recv()
    xf = jnp.zeros((z.rows, HID), f32)
    cf = jnp.zeros((z.rows, HID), f32)
    for j in range(nmp):
        sl = one_up(xo[j].astype(f32))
        here = (lane >= z.uw * j) & (lane < z.uw * (j + 1))
        xf = jnp.where(here, roll(sl, 0, z.uw * j), xf)
        cf = jnp.where(here, roll(sl, z.uw, z.uw * j), cf)
    x = xf.astype(bf)

    def rows_of(row, qs):
        return jnp.concatenate(
            [wall[row, j, q * rw : (q + 1) * rw, :] for q in qs for j in range(nmp)], axis=0
        )

    def make_b(row):
        for q in range(hl // 2):
            o = dot(x, rows_of(row, (2 * q, 2 * q + 1)), NT).astype(bf)
            bmat[row * hl + 2 * q] = o[:, :HID]
            bmat[row * hl + 2 * q + 1] = o[:, HID:]

    sacc[...] = jnp.zeros(sacc.shape, f32)

    def use_row(row):
        make_b(row)
        if hl % 8 == 0:
            parts = [row * (hl // 8) + k for k in range(hl // 8)]
            for i in range(nm):
                at = pl.ds(i * PADA, PADA)
                hm = jnp.concatenate([hid[k, at, :] for k in parts], axis=1)
                sacc[at, :] += dot(hm, bmat[pl.ds(row * hl, hl), at, :].reshape(PADA * hl, HID), NN)

    def from_core(row):
        for col in here_cols:
            for k in (0, 1):
                arrived(row, col, k)
        use_row(row)

    use_row(d)
    in_plane(3)
    for row in rows_x:
        use_row(row)
    from_core(cp[0])
    from_diagonal(2)
    from_diagonal(3)
    if relay:
        use_row(2 * ud + c)
    for row in rows_x + ([2 * ud + c] if relay else []):
        from_core(row + 1 - 2 * c)
    if hl % 8:
        for i in range(nm):
            hm = jnp.concatenate([hid[k, i * PADA : (i + 1) * PADA, :] for k in range(16)], axis=1)
            sacc[i * PADA : (i + 1) * PADA, :] = dot(
                hm, bmat[:, i * PADA : (i + 1) * PADA, :].reshape(PADA * HID, HID), NN
            )
    summed = sacc[...].astype(bf)

    def gru_rows(s, j):
        if il == 16:
            return jnp.concatenate([wall[k, j, wr + 16 * s : wr + 16 * s + 16, :] for k in range(ndp)], axis=0)
        for k in range(ndp):
            gfull[k * il : (k + 1) * il, 0:HID] = wall[k, j, wr + 16 * s : wr + 16 * s + 16, :].astype(f32)[:il]
        return gfull[0:HID, 0:HID].astype(bf)

    wg = [[gru_rows(s, j) for j in range(nmp)] for s in range(2)]

    def gates(a, s):
        outs = [dot(a, wg[s][j], NN) for j in range(nmp)]
        res = []
        for g in range(3):
            t = None
            for j in range(nmp):
                y = roll(outs[j], z.uw * g, z.uw * j)
                here = (lane >= z.uw * j) & (lane < z.uw * (j + 1))
                t = y if t is None else jnp.where(here, y, t)
            res.append(t)
        return res

    gi = gates(summed, 0)
    gs = gates(x, 1)
    reset = sig(gi[0] + gs[0])
    update = sig(gi[1] + gs[1])
    cand = jnp.tanh(gi[2] + reset * gs[2])
    ostate = (1.0 - update) * cand + update * xf
    dc = cf * (1.0 - update) * (1.0 - cand * cand)
    du = cf * (xf - cand) * update * (1.0 - update)
    dr = dc * gs[2] * reset * (1.0 - reset)

    def pack(gl, j):
        t = jnp.zeros((z.rows, HID), f32)
        for g in range(3):
            here = (lane >= z.uw * g) & (lane < z.uw * (g + 1))
            t = jnp.where(here, roll(gl[g], z.uw * j, z.uw * g), t)
        return t.astype(bf)

    al = [pack([dr, du, dc], j) for j in range(nmp)]
    bl = [pack([dr, du, dc * reset], j) for j in range(nmp)]
    ds = dot(jnp.concatenate(al, axis=1), jnp.concatenate(wg[0], axis=1), NT).astype(bf)
    gfull[:, HID : 2 * HID] = cf * update
    gfull[:, 0:HID] = dot(jnp.concatenate(bl, axis=1), jnp.concatenate(wg[1], axis=1), NT)
    for j in range(nmp):
        for s, (l, r) in enumerate(((summed, al[j]), (x, bl[j]))):
            gg = dot(l, r, TN)
            for k in range(ndp):
                part = gg[k * il : (k + 1) * il]
                if il < 16:
                    part = jnp.concatenate([part, jnp.zeros((16 - il, HID), f32)], axis=0)
                grads[k, j, wr + 16 * s : wr + 16 * s + 16, :] = part.astype(bf)

    dsb[...] = jnp.zeros(dsb.shape, bf)
    for i in range(nm):
        dsb[i * PADA : (i + 1) * PADA, i * HID : (i + 1) * HID] = ds[i * PADA : (i + 1) * PADA]

    def c_block(k):
        for p in range(nm // 2):
            o = dot(hidt[k], dsb[:, p * 256 : (p + 1) * 256], NN).astype(bf)
            for i in range(2):
                at = (2 * p + i) * PADA
                cmat[pl.ds(k * 8, 8), at : at + PADA, :] = o[:, i * HID : (i + 1) * HID].reshape(8, PADA, HID)

    if hl % 8:
        pl.loop(0, 16, unroll=8)(c_block)

    def grad_w(row):
        for k in range(hl // 8):
            c_block(row * (hl // 8) + k)
        for q in range(hl):
            o = dot(cmat[row * hl + q], x, TN).astype(bf)
            for j in range(nmp):
                grads[row, j, q * rw : (q + 1) * rw, :] = o[rw * j : rw * (j + 1)]

    cols = zcols[::-1] + [m]

    def core_arrived(t, col):
        rcopy(rc.at[t, col], rc.at[t, col], fsem, cr.at[t, col], cp).wait_recv()

    def plane_out(t, *which):
        row = 2 * chips[t] + c
        for i in which:
            col = cols[i]
            core_arrived(t, col)
            sb[t, i] = (grads[row, col].astype(f32) + rc[t, col].astype(f32)).astype(bf)
            if not relay:
                go(rcopy(sb.at[t, i], rp.at[t, col], ps.at[t, i], pr.at[t, col], pp[t]))
                continue
            if t < 2:
                go(rcopy(sb.at[t, i, pl.ds(0, ra), :], rp.at[t, col, pl.ds(0, ra), :], ps.at[t, i], pr.at[t, col], px))
            if t != 1:
                k = t // 2 + 2
                go(rcopy(sb.at[t, i, pl.ds(ra, ra), :], rp.at[k % 3, col, pl.ds(ra, ra), :], ps.at[k, i], pr.at[k, col], py))

    def row_out(t):
        row = 2 * chips[t] + (1 - c)
        grad_w(row)
        for i, col in enumerate(cols):
            go(rcopy(grads.at[row, col], rc.at[t, col], cs.at[t, i], cr.at[t, col], cp))

    def row_own(t):
        grad_w(2 * chips[t] + c)

    def part_arrived(slot, lo, col, k):
        here = rp.at[slot, col, pl.ds(lo, ra), :]
        rcopy(here, here, fsem, pr.at[k, col], cp).wait_recv()
        return rp[slot, col, lo : lo + ra, :].astype(f32)

    def turn(i):
        if not relay:
            return
        col = cols[i]
        ta[i] = (sb[2, i, 0:ra, :].astype(f32) + part_arrived(0, 0, col, 0)).astype(bf)
        go(rcopy(ta.at[i], r2a.at[col], p2s.at[0, i], p2r.at[0, col], py))
        tb[i] = (sb[1, i, ra:, :].astype(f32) + part_arrived(2, ra, col, 2)).astype(bf)
        go(rcopy(tb.at[i], r2b.at[col], p2s.at[1, i], p2r.at[1, col], px))

    def column(i, k):
        col = cols[i]
        at = pl.ds(k * ra, ra)
        if k == 0:
            core_arrived(half - 1, col)
        q = grads[d, col, at, :].astype(f32) + rc[half - 1, col, at, :].astype(f32)
        if not relay:
            for t in range(half - 1):
                here = rp.at[t, col]
                if k == 0:
                    rcopy(here, here, fsem, pr.at[t, col], cp).wait_recv()
                q = q + rp[t, col, at, :].astype(f32)
            return q
        turned = (r2a, r2b)[k]
        rcopy(turned.at[col], turned.at[col], fsem, p2r.at[k, col], cp).wait_recv()
        return q + part_arrived(1 - k, k * ra, col, 1 + 2 * k) + turned[col].astype(f32)

    at_end = (m == 0) | (m == nmp - 1)
    between = (m > 0) & (m < nmp - 1)

    def z_piece(ref, k):
        return ref.at[pl.ds(k * ra, ra), :]

    def z_arrived(way, col, k):
        here = z_piece(rz.at[way, col], k)
        rcopy(here, here, fsem, zr.at[way, col, k], cp).wait_recv()
        return rz[way, col, k * ra : (k + 1) * ra, :].astype(f32)

    def z_copies(i):
        col = cols[i]
        up = jnp.where(col > m, 1, 0)
        way = 1 - up
        return way, [
            rcopy(z_piece(zs.at[i], k), z_piece(rz.at[way, col], k), z2.at[i, k], zr.at[way, col, k], (d, m + 2 * up - 1))
            for k in (0, 1)
        ]

    def to_z(i, when, chained):
        @pl.when(when)
        def _():
            way, copies = z_copies(i)
            for k, x in enumerate(copies):
                q = column(i, k)
                if chained:
                    q = q + z_arrived(way, cols[i], k)
                zs[i, k * ra : (k + 1) * ra, :] = q.astype(bf)
                x.start()

    def by_eight(v, mask):
        v = jnp.where(mask[None], v.reshape(EFEAT, PADA, -1), 0.0)
        return (v[:, 0:8] + v[:, 8:16] + v[:, 16:24] + v[:, 24:32]).reshape(EFEAT * 8, -1).astype(bf)

    eight = jnp.where(
        lax.broadcasted_iota(jnp.int32, (EFEAT, EFEAT * 8), 0)
        == lax.broadcasted_iota(jnp.int32, (EFEAT, EFEAT * 8), 1) // 8,
        1.0,
        0.0,
    ).astype(bf)
    tiles = -(-z.win // 256)
    cuts = (0, tiles // 2, tiles)

    def edges_back(part):
        for n in range(cuts[part], cuts[part + 1]):
            count = min(256, z.win - n * 256)
            at = pl.ds(n * 256, count)
            all_rows = lax.broadcasted_iota(jnp.int32, (z.rows, count), 0)
            rt = jnp.where(all_rows == keyw[1:2, at], 1.0, 0.0).astype(bf)
            eights[n, :, 0:count] = by_eight(dot(gbt[...], rt, NN), wio[:, :count] == keyw[0:1, at])
        for n in range(cuts[part], cuts[part + 1]):
            count = min(256, z.win - n * 256)
            geo[m, :, n * 256 : n * 256 + count] = dot(eight, eights[n, :, 0:count], NN).astype(bf)

    def edges_on(s):
        for part in (0, 1):
            edges_on_part(s, part)

    def edges_on_part(s, part):
        lo, hi = 256 * cuts[part], min(256 * cuts[part + 1], z.win)
        for way in (0, 1):
            col = m - s if way == 0 else m + s
            nxt = m + 1 if way == 0 else m - 1
            src = geo.at[col, :, pl.ds(lo, hi - lo)]
            if s:
                pl.when(inside(col))(rcopy(src, src, fsem, ge_r.at[part, col], cp).wait_recv)
            if s < nmp - 1:
                go_if(
                    inside(col) & inside(nxt),
                    rcopy(src, src, ge_s.at[part, s, way], ge_r.at[part, col], (d, nxt)),
                )

    step = min(DXC, hl)

    def state_grad(lo, hi):
        @pl.loop(lo, hi, unroll=2)
        def _(row):
            for q in range(0, hl, step):
                qs = range(q, q + step)
                cc = jnp.concatenate([cmat[row * hl + k] for k in qs], axis=1)
                gacc[...] += dot(cc, rows_of(row, qs), NN)

    def hidden_grad(lo, hi):
        for i in range(nm):
            dm = ds[i * PADA : (i + 1) * PADA]
            for k in range(lo, hi):
                o = dot(dm, bmat[k * 8 : (k + 1) * 8, i * PADA : (i + 1) * PADA, :].reshape(256, HID), NT)
                dpre[k, i * PADA : (i + 1) * PADA, :] = (
                    o * slope[k, i * PADA : (i + 1) * PADA, :].astype(f32)
                ).astype(bf)

    others = range(half - 1)
    row_out(0)
    row_own(0)
    row_out(1)
    plane_out(0, 0)
    row_own(1)
    plane_out(0, 1)
    for t in others[2:]:
        row_out(t)
        plane_out(t - 1, 0)
        row_own(t)
    hidden_grad(0, 8)
    plane_out(half - 2, 0)
    hidden_grad(8, 16)
    gb = dot(
        jnp.concatenate([dpre[k] for k in range(16)], axis=1),
        jnp.concatenate([kron[k] for k in range(16)], axis=1),
        NT,
    ).astype(bf)
    gbt[...] = gb.T
    turn(0)
    for t in others[1:]:
        plane_out(t, 1)
    plane_out(0, 2)
    edges_back(0)
    edges_on_part(0, 0)
    edges_back(1)
    edges_on_part(0, 1)
    turn(1)
    for t in others[1:]:
        plane_out(t, 2)
    plane_out(0, 3)
    row_out(half - 1)
    row_own(half - 1)

    @pl.loop(0, 16, unroll=16)
    def _(k):
        eights[k] = by_eight(dot(featt[...], dpre[k], NN), delta)

    gin = dot(
        jnp.concatenate([eights[k] for k in range(16)], axis=1),
        jnp.concatenate([emat[k] for k in range(16)], axis=1),
        NT,
    )
    gis[d] = gin.reshape(EFEAT, 8, HID).sum(axis=1).astype(bf)
    for i, p in enumerate(dpp):
        go(rcopy(gis.at[d], gis.at[d], gi_s.at[i], gi_r.at[d], p))
    to_z(0, at_end, False)

    gacc[...] = jnp.zeros(gacc.shape, f32)
    state_grad(0, ndp // 2)
    turn(2)
    for t in others[1:]:
        plane_out(t, 3)
    edges_on(1)
    state_grad(ndp // 2, ndp)
    gfin = gacc[...] + gfull[:, 0:HID] + gfull[:, HID : 2 * HID]
    for j in range(nmp):
        a = roll(ostate, z.uw * j, 0)
        b = roll(gfin, z.uw * j, z.uw)
        osb[j] = two_up(jnp.where(lane < z.uw, a, b)).astype(bf)
    for i, p in enumerate(zp):
        go(rcopy(osb.at[p[1]], oso.at[m], os_s.at[i], os_r.at[m], p))
    oso[m] = osb[m]

    to_z(1, at_end, False)
    to_z(0, between, True)
    gi_sum = gis[d].astype(f32)
    for i in range(1, ndp):
        row = (d - i + ndp) % ndp
        rcopy(gis.at[row], gis.at[row], gi_s.at[0], gi_r.at[row], cp).wait_recv()
        gi_sum = gi_sum + gis[row].astype(f32)
    giz_s[...] = gi_sum.astype(bf)
    for i, p in enumerate(zp):
        go(rcopy(giz_s, giz.at[m], gz_s.at[i], gz_r.at[m], p))
    turn(3)
    edges_on(2)
    to_z(2, at_end, False)
    to_z(1, between, True)
    to_z(2, between, True)

    for col in zcols:
        rcopy(oso.at[col], oso.at[col], os_s.at[0], os_r.at[col], cp).wait_recv()
    for j in range(nmp):
        stage2[j * z.rows : (j + 1) * z.rows, :] = one_up(oso[j].astype(f32))
    for i in range(z.mols):
        stage1[i * MA : (i + 1) * MA, :] = stage2[i * PADA : i * PADA + MA, :]
    stage[...] = stage1[...].T
    at_ref[0 : z.uw, :] = stage[0 : z.uw, 0 : z.atoms] * nmrow[...]
    at_ref[z.uw : 2 * z.uw, :] = stage[z.uw : 2 * z.uw, 0 : z.atoms]
    at_out = pltpu.make_async_copy(at_ref, at_hbm, lsem.at[0])
    at_out.start()

    for k in (0, 1):
        fin[k * ra : (k + 1) * ra, :] = column(nmp - 1, k)
    edges_on(3)
    for j, lo in enumerate(z.starts):
        first = geo[j, :, 0:128]
        if j:
            first = (first.astype(f32) + geo[j - 1, :, main:].astype(f32)).astype(bf)
        ge_ref[:, lo : lo + 128] = first
        ge_ref[:, lo + 128 : lo + main] = geo[j, :, 128:main]
    if z.edges > z.full:
        ge_ref[:, z.full :] = geo[nmp - 1, :, main : main + z.edges - z.full]
    ge_out = pltpu.make_async_copy(ge_ref, ge_hbm, lsem.at[1])
    ge_out.start()

    for col in zcols:
        rcopy(giz.at[col], giz.at[col], gz_s.at[0], gz_r.at[col], cp).wait_recv()
        gi_sum = gi_sum + giz[col].astype(f32)
    gi_ref[...] = pltpu.roll(gi_sum, HID - d * z.ew, 1)[:, 0 : z.ew]

    @pl.when(m > 0)
    def _():
        for k in (0, 1):
            fin[k * ra : (k + 1) * ra, :] += z_arrived(0, m, k)

    @pl.when(m < nmp - 1)
    def _():
        for k in (0, 1):
            fin[k * ra : (k + 1) * ra, :] += z_arrived(1, m, k)

    for s in range(2):
        for g in range(3):
            gg_ref[s, g] = fin[wr + 16 * s : wr + 16 * s + il, g * z.uw : (g + 1) * z.uw]
    wtmp[...] = fin[0:wr, :].reshape(hl, rw, HID)
    for r in range(rw):
        go_ref[:, r * HID : (r + 1) * HID] = wtmp[:, r, :]

    at_out.wait()
    ge_out.wait()
    for i in range(nmp - 1):
        sends.extend(z_copies(i)[1])
    for y in sends:
        y.wait_send()
    for ok, y in maybe:
        pl.when(ok)(y.wait_send)


def whole_step(z, eo, ei, gw, ns, og, live, feat, snd, rcv, msk):
    dma = pltpu.SemaphoreType.DMA
    ndp, nmp, half = z.ndp, z.nmp, z.half
    rows, rb, win = z.rows, z.rb, z.win
    vm = pltpu.VMEM
    ra = rb // 2
    relay = half == 4
    return pl.pallas_call(
        functools.partial(kernel, z),
        out_shape=(
            jax.ShapeDtypeStruct(eo.shape, f32),
            jax.ShapeDtypeStruct(gw.shape, f32),
            jax.ShapeDtypeStruct(ei.shape, f32),
            jax.ShapeDtypeStruct((2 * z.uw, z.atoms), f32),
            jax.ShapeDtypeStruct(feat.shape, bf),
        ),
        in_specs=[pl.BlockSpec(memory_space=pl.ANY)] * 10,
        out_specs=(pl.BlockSpec(memory_space=vm),) * 3 + (pl.BlockSpec(memory_space=pl.ANY),) * 2,
        scratch_shapes=[
            vm((2 * z.uw, z.atoms), f32),
            vm(feat.shape, bf),
            *(vm(a.shape, a.dtype) for a in (eo, ei, gw, ns, og, live, feat, snd, rcv, msk)),
            vm((ndp, nmp, rb, HID), bf),
            vm((nmp, rows // 2, HID), bf),
            vm((nmp, rows // 2, HID), bf),
            vm((ndp, EFEAT, HID), bf),
            vm((HID, -(-z.atoms // 128) * 128), f32),
            vm((-(-z.atoms // 128) * 128, HID), f32),
            vm((nmp * rows, HID), f32),
            vm((z.hl, z.rw, HID), f32),
            vm((32, HID), f32),
            vm((EFEAT, HID), f32),
            vm((1, z.atoms), f32),
            vm((EFEAT, win), bf),
            vm((3, win), jnp.int32),
            vm((rows, 512), bf),
            vm((512, rows), bf),
            vm((512, rows), bf),
            vm((16, 512, 256), bf),
            vm((16, HID, 256), bf),
            vm((16, rows, 256), bf),
            vm((16, 256, rows), bf),
            vm((16, rows, 256), bf),
            vm((HID, rows, HID), bf),
            vm((HID, rows, HID), bf),
            vm((rows, z.nm * HID), bf),
            vm((16, rows, 256), bf),
            vm((rows, HID), f32),
            vm((rows, HID), f32),
            vm((rows, 512), f32),
            vm((max(16, -(-win // 256)), EFEAT * 8, 256), bf),
            vm((ndp, nmp, rb, HID), bf),
            vm((half, nmp, rb, HID), bf),
            vm((half - 1, nmp, rb, HID), bf),
            vm((half - 1, nmp, rb, HID), bf),
            vm((nmp, ra, HID), bf),
            vm((nmp, ra, HID), bf),
            vm((nmp, ra, HID), bf),
            vm((nmp, ra, HID), bf),
            vm((nmp - 1, rb, HID), bf),
            vm((2, nmp, rb, HID), bf),
            vm((rb, HID), f32),
            vm((nmp, rows // 2, HID), bf),
            vm((nmp, rows // 2, HID), bf),
            vm((nmp, EFEAT, win), bf),
            vm((ndp, EFEAT, HID), bf),
            vm((nmp, EFEAT, HID), bf),
            vm((EFEAT, HID), bf),
            dma((10,)),
            dma(()),
            dma((nmp - 1, 2)),
            dma((nmp - 1, 2)),
            dma((nmp, 2, max(half - 1, 4))),
            dma((2 * nmp * half,)),
            dma((ndp, nmp, 2)),
            dma((nmp - 1,)), dma((nmp,)),
            dma((max(ndp - 1, 8),)), dma((ndp,)),
            dma((half, nmp)), dma((half, nmp)),
            dma((max(half - 1, 4), nmp)), dma((max(half - 1, 4), nmp)),
            dma((2, nmp)), dma((2, nmp)),
            dma((nmp - 1, 2)), dma((2, nmp, 2)),
            dma((nmp - 1,)), dma((nmp,)),
            dma((2, nmp - 1, 2)), dma((2, nmp)),
            dma((ndp - 1,)), dma((ndp,)),
            dma((nmp - 1,)), dma((nmp,)),
        ],
        compiler_params=pltpu.CompilerParams(
            collective_id=0, has_side_effects=True, vmem_limit_bytes=VMEM_LIMIT
        ),
    )(eo, ei, gw, ns, og, live, feat, snd, rcv, msk)


beta_one = 0.5
beta_two = 0.5
learn_rate = 0.05
decay_rate = 0.01
epsilon = 1e-08


def adam_update(weight, gradient, first_moment, second_moment):
    first_new = beta_one * first_moment + (1.0 - beta_one) * gradient
    second_new = beta_two * second_moment + (1.0 - beta_two) * gradient * gradient
    mean_hat = first_new / (1.0 - beta_one**STEP)
    square_hat = second_new / (1.0 - beta_two**STEP)
    weight_new = weight - learn_rate * (
        mean_hat / (jnp.sqrt(square_hat) + epsilon) + decay_rate * weight
    )
    return (first_new, second_new, weight_new, weight_new.astype(bf))


def finish_kernel(*refs):
    ins, outs = refs[:14], refs[14:29]
    vin, vout = refs[29:43], refs[43:58]
    isem, osem = refs[58:]
    loads = [pltpu.make_async_copy(a, b, isem.at[i]) for i, (a, b) in enumerate(zip(ins, vin))]
    stores = [pltpu.make_async_copy(a, b, osem.at[i]) for i, (a, b) in enumerate(zip(vout, outs))]
    order = [1, 6, 7, 8, 9, 0, 2, 3, 4, 5, 10, 11, 12, 13]
    for i in order:
        loads[i].start()
    loads[1].wait()
    vout[2][...] = vin[1][...].astype(f32)
    stores[2].start()

    def layer(n):
        for i in range(2 + 4 * n, 6 + 4 * n):
            loads[i].wait()
        new = adam_update(*[vin[i][...] for i in range(2 + 4 * n, 6 + 4 * n)])
        for i, v in enumerate(new):
            vout[3 + 4 * n + i][...] = v
            stores[3 + 4 * n + i].start()

    layer(1)
    loads[0].wait()
    uw = vin[0].shape[0] // 2
    vout[0][...] = vin[0][0:uw, :]
    vout[1][...] = vin[0][uw:, :]
    stores[0].start()
    stores[1].start()
    layer(0)
    layer(2)
    for x in stores:
        x.wait()


def finish(at, ge, *layers):
    half = jax.ShapeDtypeStruct((at.shape[0] // 2, at.shape[1]), f32)
    results = [half, half, jax.ShapeDtypeStruct(ge.shape, f32)]
    for n in range(3):
        results += [jax.ShapeDtypeStruct(layers[4 * n].shape, t) for t in (f32, f32, f32, bf)]
    args = (at, ge, *layers)
    return pl.pallas_call(
        finish_kernel,
        out_shape=tuple(results),
        in_specs=[pl.BlockSpec(memory_space=pl.ANY)] * 14,
        out_specs=(pl.BlockSpec(memory_space=pl.ANY),) * 15,
        scratch_shapes=[pltpu.VMEM(v.shape, v.dtype) for v in (*args, *results)]
        + [pltpu.SemaphoreType.DMA((14,)), pltpu.SemaphoreType.DMA((15,))],
        compiler_params=pltpu.CompilerParams(vmem_limit_bytes=VMEM_LIMIT),
    )(*args)


def body(
    ndp, nmp,
    node_state, edge_feat, sender, receiver, edge_mask, node_mask, out_grad,
    edge_in, edge_out, gru_weight,
    edge_in_m1, edge_in_m2, edge_out_m1, edge_out_m2, gru_m1, gru_m2,
):
    z = Shape(ndp, nmp, node_state, edge_feat, edge_in, edge_out, gru_weight)
    g_out, g_gru, g_in, at, ge = whole_step(
        z, edge_out, edge_in, gru_weight, node_state.T, out_grad.T, node_mask,
        edge_feat, sender, receiver, edge_mask,
    )
    out_state, grad_state, *rest = finish(
        at, ge,
        edge_in, g_in, edge_in_m1, edge_in_m2,
        edge_out, g_out, edge_out_m1, edge_out_m2,
        gru_weight, g_gru, gru_m1, gru_m2,
    )
    return (out_state.T, grad_state.T, *rest)


def solution(mesh):
    ndp, nmp = mesh.shape["dp"], mesh.shape["mp"]
    rows, lanes, gru = P("dp", "mp"), P(None, "dp"), P(None, None, "dp", "mp")
    edge = P("dp")
    return jax.shard_map(
        functools.partial(body, ndp, nmp),
        mesh=mesh,
        in_specs=(
            rows, lanes, edge, edge, edge, edge, rows,
            lanes, rows, gru, lanes, lanes, rows, rows, gru, gru,
        ),
        out_specs=(rows, rows, lanes) + (lanes,) * 4 + (rows,) * 4 + (gru,) * 4,
        check_vma=False,
    )
```
